32 devices in a mesh: rows: 8 (over z, y), cols: 4 (over x, core).
Axes of the slice: x: 2, y: 2, z: 4, core: 2. Of those that a mesh axis runs over, the one named last changes fastest.
Arguments:
- features: bfloat16 [192, 96, 2048], P('rows', 'cols'), may hold values from -216 to 216
- image_ids: int32 [192, 96], replicated, may hold values from 0 to 35, as said below
- w_point: bfloat16 [2048, 256], replicated, may hold values from -0.125 to 0.125
- w_atrous: bfloat16 [3, 9, 2048, 256], replicated, may hold values from -0.046875 to 0.046875
- w_pool: bfloat16 [2048, 256], replicated, may hold values from -0.125 to 0.125
- w_proj: bfloat16 [1280, 256], replicated, may hold values from -0.15625 to 0.15625
- norm_gain: float32 [6, 256], replicated, may hold values from 0.5 to 1.5
- norm_shift: float32 [6, 256], replicated, may hold values from -3 to 3
- cotangent: bfloat16 [192, 96, 256], P('rows', 'cols'), may hold values from -6 to 6
Outputs:
- output: bfloat16 [192, 96, 256], P('rows', 'cols')
- grad_features: bfloat16 [192, 96, 2048], P('rows', 'cols')
- grad_point: float32 [2048, 256], P('rows')
- grad_atrous: float32 [3, 9, 2048, 256], P(None, None, 'rows')
- grad_pool: float32 [2048, 256], P('rows')
- grad_proj: float32 [1280, 256], P('rows')
- grad_gain: float32 [6, 256], replicated
- grad_shift: float32 [6, 256], replicated
The draws below stay inside these ranges and needn't reach their ends.
Inputs may be any that keep to these rules, and one draw needn't show every extreme that they name: `image_ids`: the images are rectangles that tile the grid: vertical bands, each cut across into 12 rectangles, numbered band by band from the left and top to bottom inside a band; every number occurs.
All inputs are finite; a program needn't handle non-finite values.
Results may differ from the reference program's by a relative error of at most 0.017.
Values may be sent and summed in bfloat16 or wider, within the bound.
A program may use at most 384 MiB of HBM per device.

```python
import math
import jax
import jax.numpy as jnp
from jax import lax

C_IN = 2048
C_BR = 256
RATE_LOW = 6
RATE_MID = 12
RATE_TOP = 18
GRID_ROWS = 192
GRID_COLS = 96
NIMG = 36


def draw_features(key, part):
    key = jax.random.fold_in(key, 11)
    key_base, key_pixel, key_chan = jax.random.split(key, 3)
    shape = (GRID_ROWS, GRID_COLS, C_IN)
    row_pos = jnp.arange(GRID_ROWS, dtype=jnp.float32) / max(GRID_ROWS - 1, 1)
    trend = jnp.exp(math.log(3.0) * row_pos)[:, None, None]
    chan_scale = jnp.exp(jax.random.uniform(key_chan, (C_IN,), jnp.float32, math.log(0.3), math.log(3.0)))
    pixel_scale = jnp.exp(math.log(4.0) * jax.random.uniform(key_pixel, (GRID_ROWS, GRID_COLS, 1), jnp.float32))
    base = jnp.clip(jax.random.normal(key_base, shape, jnp.float32), -6.0, 6.0)
    return (base * trend * pixel_scale * chan_scale).astype(jnp.bfloat16)


def draw_image_ids(key, part):
    key = jax.random.fold_in(key, 23)
    key_cols, key_rows = jax.random.split(key)
    band_count = GRID_COLS // 32
    cut_count = GRID_ROWS // 16
    col_cuts = jnp.sort(jax.random.permutation(key_cols, jnp.arange(1, GRID_COLS, dtype=jnp.int32))[:band_count - 1])
    band = jnp.sum((jnp.arange(GRID_COLS, dtype=jnp.int32)[:, None] >= col_cuts[None, :]).astype(jnp.int32), axis=1)
    row_keys = jax.random.split(key_rows, band_count)

    def band_cuts(row_key):
        return jnp.sort(jax.random.permutation(row_key, jnp.arange(1, GRID_ROWS, dtype=jnp.int32))[:cut_count - 1])
    row_cuts = jax.vmap(band_cuts)(row_keys)
    cuts_here = jnp.take(row_cuts, band, axis=0)
    segment = jnp.sum((jnp.arange(GRID_ROWS, dtype=jnp.int32)[:, None, None] >= cuts_here[None, :, :]).astype(jnp.int32), axis=2)
    return (band[None, :] * cut_count + segment).astype(jnp.int32)


def steps_of(stream_key, extent, pieces, smallest, largest):
    loudness = 1.0
    for dim, blocks in pieces:
        draws = jax.random.uniform(jax.random.fold_in(jax.random.fold_in(stream_key, 6), dim), (blocks,), jnp.float32, smallest / len(pieces), largest / len(pieces))
        loudness = loudness * jnp.repeat(jnp.exp(draws), extent[dim] // blocks).reshape((-1,) + (1,) * (len(extent) - 1 - dim))
    return loudness


def centred(key, shape, width, bound, shards=(), kind=jnp.bfloat16):
    level = steps_of(key, shape, shards, -0.22, 0.18) if shards else 1.0
    values = jax.random.normal(key, shape, jnp.float32) * width * level
    return jnp.minimum(jnp.maximum(values, -bound), bound).astype(kind)


def setup_inputs(seed: int = 0) -> dict:
    key_of = jax.random.split(jax.random.key(seed), 10)
    features = draw_features(jax.random.fold_in(key_of[9], 71), 0)
    image_ids = draw_image_ids(jax.random.fold_in(key_of[9], 71), 0)
    w_point = centred(key_of[2], (C_IN, C_BR), C_IN ** -0.5, 0.125)
    w_atrous = centred(key_of[3], (3, 9, C_IN, C_BR), (9 * C_IN) ** -0.5, 0.046875)
    w_pool = centred(key_of[4], (C_IN, C_BR), C_IN ** -0.5, 0.125)
    w_proj = centred(key_of[5], (5 * C_BR, C_BR), (5 * C_BR) ** -0.5, 0.15625)
    norm_gain = jnp.clip(1.0 + 0.1 * jax.random.normal(key_of[6], (6, C_BR), jnp.float32), 0.5, 1.5)
    norm_shift = centred(key_of[7], (6, C_BR), 0.5, 3.0, (), jnp.float32)
    cotangent = centred(key_of[8], (GRID_ROWS, GRID_COLS, C_BR), 1.0, 6.0, ((0, 8), (1, 4)))
    return {"features": features, "image_ids": image_ids, "w_point": w_point, "w_atrous": w_atrous, "w_pool": w_pool, "w_proj": w_proj, "norm_gain": norm_gain, "norm_shift": norm_shift, "cotangent": cotangent}


epsilon = 1e-05

@jax.custom_vjp
def low(v):
    return lax.optimization_barrier(v.astype(jnp.bfloat16)).astype(jnp.float32)

@jax.custom_vjp
def low_back(v):
    return v

def low_keep(v):
    return (low(v), None)

def low_pass(kept, grad):
    return (grad,)

def back_keep(v):
    return (v, None)

def back_low(kept, grad):
    return (low(grad),)
low.defvjp(low_keep, low_pass)
low_back.defvjp(back_keep, back_low)

def matmul(left, right):
    return jnp.dot(left, right, precision=lax.Precision.HIGHEST, preferred_element_type=jnp.float32)

def norm_act(values, gain, shift):
    average = lax.optimization_barrier(jnp.mean(values, axis=0))
    square = lax.optimization_barrier(jnp.mean(values * values, axis=0))
    inverse_std = lax.rsqrt(square - average * average + epsilon)
    return jax.nn.silu(gain * ((values - average) * inverse_std) + shift)

def atrous_sum(padded, id_padded, image_ids, kernel, dilation):
    height, breadth = image_ids.shape

    def one_tap(running, stencil_item):
        stencil, weight = stencil_item
        row_start = (RATE_TOP + (stencil // 3 - 1) * dilation).astype(jnp.int32)
        col_start = (RATE_TOP + (stencil % 3 - 1) * dilation).astype(jnp.int32)
        zero_start = jnp.zeros((), jnp.int32)
        source = lax.dynamic_slice(padded, (row_start, col_start, zero_start), (height, breadth, padded.shape[2]))
        source_ids = lax.dynamic_slice(id_padded, (row_start, col_start), (height, breadth))
        same_image = (source_ids == image_ids).astype(jnp.float32)
        product = matmul(source.reshape(height * breadth, padded.shape[2]), weight)
        return (running + same_image.reshape(height * breadth, 1) * product, None)
    start = jnp.zeros((height * breadth, kernel.shape[2]), jnp.float32)
    running, _ = lax.scan(jax.checkpoint(one_tap), start, (jnp.arange(9, dtype=jnp.int32), kernel))
    return running

def reference(features, image_ids, w_point, w_atrous, w_pool, w_proj, norm_gain, norm_shift, cotangent):
    pixels = GRID_ROWS * GRID_COLS
    dilations = (RATE_LOW, RATE_MID, RATE_TOP)
    id_padded = jnp.pad(image_ids, RATE_TOP, constant_values=-1)
    ids_flat = image_ids.reshape(pixels)
    counts = jax.ops.segment_sum(jnp.ones((pixels,), jnp.float32), ids_flat, NIMG)

    def forward(feat_in, point_in, atrous_in, pool_in, proj_in, gain_in, shift_in):
        flattened = feat_in.reshape(pixels, C_IN)
        padded = jnp.pad(feat_in, ((RATE_TOP, RATE_TOP), (RATE_TOP, RATE_TOP), (0, 0)))
        branches = []
        point_z = low_back(matmul(flattened, point_in))
        branches.append(low(norm_act(point_z, gain_in[0], shift_in[0])))
        for branch, dilation in enumerate(dilations):
            atrous_z = low_back(atrous_sum(padded, id_padded, image_ids, atrous_in[branch], dilation))
            branches.append(low(norm_act(atrous_z, gain_in[branch + 1], shift_in[branch + 1])))
        pooled = low(jax.ops.segment_sum(flattened, ids_flat, NIMG) / counts[:, None])
        pool_z = low_back(matmul(pooled, pool_in))
        pool_active = low(norm_act(pool_z, gain_in[4], shift_in[4]))
        branches.append(jnp.take(pool_active, ids_flat, axis=0))
        joined = jnp.concatenate(branches, axis=1)
        final_z = low_back(matmul(joined, proj_in))
        return norm_act(final_z, gain_in[5], shift_in[5])
    inputs = (features.astype(jnp.float32), w_point.astype(jnp.float32), w_atrous.astype(jnp.float32), w_pool.astype(jnp.float32), w_proj.astype(jnp.float32), norm_gain, norm_shift)
    result, pullback = jax.vjp(forward, *inputs)
    grads = pullback(cotangent.reshape(pixels, C_BR).astype(jnp.float32))
    return (result.reshape(GRID_ROWS, GRID_COLS, C_BR).astype(jnp.bfloat16), grads[0].astype(jnp.bfloat16), grads[1], grads[2], grads[3], grads[4], grads[5], grads[6])
```

```python
import functools
import jax
import jax.numpy as jnp
from jax import lax
from jax.experimental import pallas as pl
from jax.experimental.pallas import tpu as pltpu
from jax.sharding import PartitionSpec as P

MESH = pl.DeviceIdType.MESH
RATE_LOW = 6
RATE_MID = 12
RATE_TOP = 18
STEP = RATE_LOW
REACH = RATE_TOP // STEP
HALO = {1: 48, 2: 80, 3: 112}
SLOTS = 4
epsilon = 1e-05
F32 = jnp.float32
BF16 = jnp.bfloat16


def wide(column, width):
    return jnp.concatenate([column] * (width // column.shape[-1]), axis=-1)


def silu_parts(preact):
    sigma = jax.nn.sigmoid(preact)
    return preact * sigma, sigma * (1.0 + preact * (1.0 - sigma))


def contract_rows(left, right):
    return lax.dot_general(left, right, (((0,), (0,)), ((), ())), preferred_element_type=F32)


def contract_lanes(left, right):
    return lax.dot_general(left, right, (((1,), (1,)), ((), ())), preferred_element_type=F32)


def greet_all(rows, cols, r, c):
    barrier = pltpu.get_barrier_semaphore()
    for dr in range(rows):
        for dc in range(cols):
            if dr or dc:
                other = (lax.rem(r + dr, rows), lax.rem(c + dc, cols))
                pl.semaphore_signal(barrier, inc=1, device_id=other, device_id_type=MESH)
    pl.semaphore_wait(barrier, rows * cols - 1)


class Exchange:
    def __init__(self, axis_size, place, to_device, slots, send_sems, recv_sems):
        self.size, self.place, self.to_device = axis_size, place, to_device
        self.slots, self.send_sems, self.recv_sems = slots, send_sems, recv_sems

    def copy(self, step, source=None):
        other = lax.rem(self.place + step, self.size)
        mine = self.slots.at[self.place]
        return pltpu.make_async_remote_copy(
            src_ref=mine if source is None else source(other),
            dst_ref=mine,
            send_sem=self.send_sems.at[step],
            recv_sem=self.recv_sems.at[self.place],
            device_id=self.to_device(other),
            device_id_type=MESH,
        )

    def start(self, source=None):
        for step in range(1, self.size):
            self.copy(step, source).start()

    def finish(self, source=None):
        for step in range(1, self.size):
            other = lax.rem(self.place + step, self.size)
            there = self.slots.at[other]
            pltpu.make_async_remote_copy(
                src_ref=there,
                dst_ref=there,
                send_sem=self.send_sems.at[step],
                recv_sem=self.recv_sems.at[other],
                device_id=self.to_device(other),
                device_id_type=MESH,
            ).wait_recv()
        for step in range(1, self.size):
            self.copy(step, source).wait_send()

    def total(self):
        value = self.slots[0]
        for other in range(1, self.size):
            value = value + self.slots[other]
        return value


def forward_kernel(
    rows, cols, image_count, total_pixels,
    x_ref, ids_ref, wat_ref, wpt_ref, wpl_ref, wpj_ref, gain_ref, shift_ref, cot_ref, counts_ref,
    out_ref, dz_ref, pj_ref, stat_ref, pooled_ref, pooln_ref, pools_ref, dap_ref, xsub_ref,
    idrep, wbuf, wplbuf, ubuf, zx1, zx2, zx3, zs1, zs2, zs3,
    halo_bufs, zn, slope, joined, zf, dzf, isum, cbuf, rbuf, pr_buf, pc_buf, pz_buf,
    wsem, wplsem, hsend, hrecv, csend, crecv, rsend, rrecv, psend, precv, pcsend, pcrecv, pzsend, pzrecv,
    xsend, xrecv,
):
    r, c = lax.axis_index("rows"), lax.axis_index("cols")
    blocks, rb, width = zn.shape[1], zn.shape[2], zn.shape[3]
    pixels = blocks * rb
    own = REACH * 36
    images = isum.shape[0]
    zx, zs = {1: zx1, 2: zx2, 3: zx3}, {1: zs1, 2: zs2, 3: zs3}
    order = (3, 2, 1)
    taps = 27

    def weight_copy(n):
        branch, tap = 2 - n // 9, lax.rem(n, 9)
        slot = lax.rem(n, SLOTS)
        return pltpu.make_async_copy(wat_ref.at[branch, tap], wbuf.at[slot], wsem.at[slot])

    for n in range(SLOTS - 1):
        weight_copy(jnp.int32(n)).start()
    share = x_ref.shape[1] // rows
    pool_weight = pltpu.make_async_copy(
        wpl_ref.at[pl.ds(pl.multiple_of(r * share, share), share)], wplbuf, wplsem
    )
    pool_weight.start()
    for block in range(idrep.shape[0]):
        idrep[block] = jnp.broadcast_to(ids_ref[:, block : block + 1], idrep.shape[1:])
    greet_all(rows, cols, r, c)

    own_ids = jnp.concatenate([idrep[REACH + a, own : own + rb, :] for a in range(blocks)], axis=0)
    lanes = lax.broadcasted_iota(jnp.int32, (pixels, 128), 1).astype(F32)
    one_hot = jnp.concatenate(
        [(own_ids == lanes + 128.0 * part).astype(F32).astype(BF16) for part in range(pl.cdiv(images, 128))],
        axis=1,
    )
    for part in range(rows):
        piece = slice(part * share, (part + 1) * share)
        isum[:, piece] = contract_rows(one_hot, x_ref[:, piece])[:images]
    pool_rows = Exchange(rows, r, lambda other: (other, c), pr_buf, psend, precv)

    def share_of(other):
        return isum.at[:, pl.ds(pl.multiple_of(other * share, share), share)]

    pr_buf[r] = isum[:, pl.ds(pl.multiple_of(r * share, share), share)]
    pool_rows.start(share_of)

    def halo_copies(m):
        height = HALO[m]
        a_range = {-1: (0, m), 0: (m, blocks), 1: (m + blocks, m)}
        r_range = {-1: (0, height), 0: (height, rb), 1: (height + rb, height)}
        copies = []
        for place, (dr, dc) in enumerate(DIRECTIONS):
            a0, na = a_range[dc]
            r0, nr = r_range[dr]
            copies.append(
                (
                    dr,
                    dc,
                    pltpu.make_async_remote_copy(
                        src_ref=zs[m].at[pl.ds(a0, na), pl.ds(r0, nr)],
                        dst_ref=halo_bufs[(m - 1) * 8 + place],
                        send_sem=hsend.at[m - 1, place],
                        recv_sem=hrecv.at[m - 1, place],
                        device_id=(lax.rem(r + dr + rows, rows), lax.rem(c + dc + cols, cols)),
                        device_id_type=MESH,
                    ),
                )
            )
        return copies

    def inside(dr, dc):
        return (r + dr >= 0) & (r + dr < rows) & (c + dc >= 0) & (c + dc < cols)

    for position, m in enumerate(order):
        height = HALO[m]

        @pl.loop(0, blocks + 2 * m)
        def _(block):
            zx[m][block] = jnp.zeros(zx[m].shape[1:], F32)

        for i in range(3):
            @pl.loop(0, blocks + 2 * m)
            def _(block):
                ubuf[block] = jnp.zeros(ubuf.shape[1:], F32)

            @pl.loop(0, 3)
            def _(j):
                n = position * 9 + 3 * i + j
                slot = lax.rem(n, SLOTS)
                ahead = n + SLOTS - 1

                @pl.when(ahead < taps)
                def _():
                    weight_copy(ahead).start()

                weight_copy(n).wait()
                product = jnp.dot(x_ref[...], wbuf[slot], preferred_element_type=F32)
                for a in range(blocks):
                    same = idrep[REACH + a, own : own + rb] == idrep[REACH + a - (j - 1) * m, own : own + rb]
                    part = product[a * rb : (a + 1) * rb]
                    ubuf[a + (2 - j) * m] += jnp.where(wide(same.astype(F32), width) > 0.0, part, 0.0)

            up = (i - 1) * 36 * m

            @pl.loop(0, blocks + 2 * m)
            def _(block):
                value = ubuf[block]
                if i != 1:
                    here = REACH - m + block
                    same = idrep[here, own : own + rb] == idrep[here, own - up : own - up + rb]
                    value = jnp.where(wide(same.astype(F32), width) > 0.0, value, 0.0)
                zx[m][block, height - up : height - up + rb] += value

        @pl.loop(0, blocks + 2 * m)
        def _(block):
            zs[m][block] = zx[m][block].astype(BF16)

        for dr, dc, copy in halo_copies(m):
            pl.when(inside(dr, dc))(copy.start)

        @pl.loop(0, blocks)
        def _(a):
            zn[m, a] = zx[m][m + a, height : height + rb]

    product = jnp.dot(x_ref[...], wpt_ref[...], preferred_element_type=F32)
    for a in range(blocks):
        zn[0, a] = product[a * rb : (a + 1) * rb]

    members = [(dy, dx, dk) for dy in range(2) for dx in range(2) for dk in range(2)]
    half = share // 2

    def channel_slices(y, x, k):
        return [pl.multiple_of((2 * (2 * k + l) + y) * share + x * half, 128) for l in range(2)]

    def member_copies():
        mine = lax.rem(r, 2) * cols + c
        copies = []
        for step, (dy, dx, dk) in enumerate(members):
            y, x, k = lax.rem(r + dy, 2), lax.rem(c // 2 + dx, 2), lax.rem(c + dk, 2)
            for l, start in enumerate(channel_slices(y, x, k)):
                source = x_ref.at[:, pl.ds(start, half)]
                target = xsub_ref.at[l, mine]
                if step == 0:
                    copies.append(pltpu.make_async_copy(source, target, xrecv.at[l, mine]))
                else:
                    copies.append(
                        pltpu.make_async_remote_copy(
                            src_ref=source,
                            dst_ref=target,
                            send_sem=xsend.at[l, step],
                            recv_sem=xrecv.at[l, mine],
                            device_id=(2 * (r // 2) + y, 2 * x + k),
                            device_id_type=MESH,
                        )
                    )
        return copies

    for copy in member_copies():
        copy.start()

    pool_rows.finish(share_of)
    pool_cols = Exchange(cols, c, lambda other: (r, other), pc_buf, pcsend, pcrecv)
    pc_buf[c] = pool_rows.total()
    pool_cols.start()
    pool_cols.finish()
    counts = counts_ref[...]
    pooled = (pool_cols.total() / wide(counts, share)).astype(BF16)
    pooled_ref[...] = pooled
    pool_weight.wait()
    pool_z = Exchange(rows, r, lambda other: (other, c), pz_buf, pzsend, pzrecv)
    pz_buf[r] = jnp.dot(pooled, wplbuf[...], preferred_element_type=F32)
    pool_z.start()
    pool_z.finish()
    zp = pool_z.total()
    pool_avg = jnp.sum(zp, axis=0, keepdims=True) / image_count
    pool_square = jnp.sum(zp * zp, axis=0, keepdims=True) / image_count
    pool_inverse = lax.rsqrt(pool_square - pool_avg * pool_avg + epsilon)
    pool_normed = (zp - pool_avg) * pool_inverse
    pool_active, pool_slope = silu_parts(gain_ref[4:5] * pool_normed + shift_ref[4:5])
    pooln_ref[...] = pool_normed
    pools_ref[...] = pool_slope
    spare = one_hot.shape[1] - images
    pool_active = jnp.concatenate([pool_active, jnp.zeros((spare, width), F32)], axis=0).astype(BF16)
    joined[:, 4 * width : 5 * width] = jnp.dot(one_hot, pool_active, preferred_element_type=F32).astype(BF16)

    for m in order:
        height = HALO[m]
        a_range = {-1: (blocks - m, m), 0: (0, blocks), 1: (0, m)}
        r_range = {-1: (rb - height, height), 0: (0, rb), 1: (0, height)}
        for place, (dr, dc, copy) in enumerate(halo_copies(m)):
            a0, na = a_range[dc]
            r0, nr = r_range[dr]

            @pl.when(inside(-dr, -dc))
            def _():
                copy.wait_recv()
                for a in range(na):
                    zn[m, a0 + a, r0 : r0 + nr] += halo_bufs[(m - 1) * 8 + place][a].astype(F32)

    def all_sum(step, value):
        across = Exchange(cols, c, lambda other: (r, other), cbuf.at[step], csend.at[step], crecv.at[step])
        cbuf[step, c] = value
        across.start()
        across.finish()
        down = Exchange(rows, r, lambda other: (other, c), rbuf.at[step], rsend.at[step], rrecv.at[step])
        rbuf[step, r] = across.total()
        down.start()
        down.finish()
        return down.total()

    zero = jnp.zeros((1, width), F32)

    def row_sum(value):
        return jnp.sum(value, axis=0, keepdims=True)

    firsts, seconds = [], []
    for k in range(4):
        first, second = zero, zero
        for a in range(blocks):
            value = zn[k, a]
            first, second = first + row_sum(value), second + row_sum(value * value)
        firsts.append(first)
        seconds.append(second)
    moments = all_sum(0, jnp.concatenate(firsts + seconds, axis=0))
    average = moments[0:4] / total_pixels
    inverse = lax.rsqrt(moments[4:8] / total_pixels - average * average + epsilon)
    for k in range(4):
        @pl.loop(0, blocks)
        def _(a):
            normed = (zn[k, a] - average[k : k + 1]) * inverse[k : k + 1]
            active, slant = silu_parts(gain_ref[k : k + 1] * normed + shift_ref[k : k + 1])
            zn[k, a] = normed
            slope[k, a] = slant
            joined[pl.ds(pl.multiple_of(a * rb, rb), rb), k * width : (k + 1) * width] = active.astype(BF16)

    zf[...] = jnp.dot(joined[...], wpj_ref[...], preferred_element_type=F32)
    first, second = zero, zero
    for a in range(blocks):
        value = zf[a * rb : (a + 1) * rb]
        first, second = first + row_sum(value), second + row_sum(value * value)
    moments = all_sum(1, jnp.concatenate([first, second] + [zero] * 6, axis=0))
    final_avg = moments[0:1] / total_pixels
    final_inverse = lax.rsqrt(moments[1:2] / total_pixels - final_avg * final_avg + epsilon)
    shift_last, gain_last = zero, zero
    for a in range(blocks):
        piece = slice(a * rb, (a + 1) * rb)
        normed = (zf[piece] - final_avg) * final_inverse
        result, slant = silu_parts(gain_ref[5:6] * normed + shift_ref[5:6])
        out_ref[piece] = result.astype(BF16)
        grad = cot_ref[piece].astype(F32) * slant
        zf[piece] = normed
        slope_last = grad
        dzf[piece] = slope_last
        shift_last, gain_last = shift_last + row_sum(grad), gain_last + row_sum(grad * normed)
    sums = all_sum(2, jnp.concatenate([shift_last, gain_last] + [zero] * 6, axis=0))
    shift_last, gain_last = sums[0:1], sums[1:2]
    gain = gain_ref[5:6]
    for a in range(blocks):
        piece = slice(a * rb, (a + 1) * rb)
        dzf[piece] = final_inverse * (
            dzf[piece] * gain
            - gain * shift_last / total_pixels
            - zf[piece] * (gain * gain_last / total_pixels)
        )
    grad_final = dzf[...].astype(BF16)

    shifts, gains = [], []
    for k in range(4):
        grad = contract_lanes(grad_final, wpj_ref[k * width : (k + 1) * width])
        shift_sum, gain_sum = zero, zero
        for a in range(blocks):
            part = grad[a * rb : (a + 1) * rb] * slope[k, a]
            slope[k, a] = part
            shift_sum, gain_sum = shift_sum + row_sum(part), gain_sum + row_sum(part * zn[k, a])
        shifts.append(shift_sum)
        gains.append(gain_sum)
    grad_pixel = contract_lanes(grad_final, wpj_ref[4 * width : 5 * width])
    upper = grad_pixel.astype(BF16)
    lower = (grad_pixel - upper.astype(F32)).astype(BF16)
    dap_ref[...] = (contract_rows(one_hot, upper) + contract_rows(one_hot, lower))[:images]
    sums = all_sum(3, jnp.concatenate(shifts + gains, axis=0))
    for k in range(4):
        gain = gain_ref[k : k + 1]
        from_shift = gain * sums[k : k + 1] / total_pixels
        from_gain = gain * sums[4 + k : 5 + k] / total_pixels

        @pl.loop(0, blocks)
        def _(a):
            dz_ref[k, a] = (
                inverse[k : k + 1] * (slope[k, a] * gain - from_shift - zn[k, a] * from_gain)
            ).astype(BF16)

    for k in range(5):
        piece = slice(k * width, (k + 1) * width)
        pj_ref[piece] = contract_rows(joined[:, piece], grad_final).astype(BF16)
    stat_ref[...] = jnp.concatenate([sums, shift_last, gain_last, pool_inverse] + [zero] * 5, axis=0)

    for m in order:
        for dr, dc, copy in halo_copies(m):
            pl.when(inside(dr, dc))(copy.wait_send)
    for step, copy in enumerate(member_copies()):
        if step < 2:
            copy.wait()
        else:
            copy.wait_send()
    for l in range(2):
        for step, (dy, dx, dk) in enumerate(members):
            if step:
                y, x, k = lax.rem(r + dy, 2), lax.rem(c // 2 + dx, 2), lax.rem(c + dk, 2)
                there = xsub_ref.at[l, y * cols + 2 * x + k]
                pltpu.make_async_remote_copy(
                    src_ref=there,
                    dst_ref=there,
                    send_sem=xsend.at[l, step],
                    recv_sem=xrecv.at[l, y * cols + 2 * x + k],
                    device_id=(2 * (r // 2) + y, 2 * x + k),
                    device_id_type=MESH,
                ).wait_recv()


DIRECTIONS = ((-1, 0), (1, 0), (-1, -1), (-1, 1), (1, -1), (1, 1), (0, -1), (0, 1))


def forward_call(rows, cols, image_count, x, ids, wat, wpt, wpl, wpj, gain, shift, cot, counts):
    pixels, channels = x.shape
    width = wpt.shape[1]
    blocks, rb = 4, pixels // 4
    images = counts.shape[0]
    share = channels // rows
    total_pixels = float(pixels * rows * cols)
    vmem = pl.BlockSpec(memory_space=pltpu.VMEM)
    hbm = pl.BlockSpec(memory_space=pl.ANY)

    def ext(m, kind):
        return pltpu.VMEM((blocks + 2 * m, 2 * HALO[m] + rb, width), kind)

    halo_bufs = []
    for m in (1, 2, 3):
        for dr, dc in DIRECTIONS:
            halo_bufs.append(pltpu.VMEM((m if dc else blocks, HALO[m] if dr else rb, width), BF16))
    dma = pltpu.SemaphoreType.DMA
    return pl.pallas_call(
        functools.partial(forward_kernel, rows, cols, float(image_count), total_pixels),
        out_shape=(
            jax.ShapeDtypeStruct((pixels, width), BF16),
            jax.ShapeDtypeStruct((4, blocks, rb, width), BF16),
            jax.ShapeDtypeStruct((5 * width, width), BF16),
            jax.ShapeDtypeStruct((16, width), F32),
            jax.ShapeDtypeStruct((images, share), BF16),
            jax.ShapeDtypeStruct((images, width), F32),
            jax.ShapeDtypeStruct((images, width), F32),
            jax.ShapeDtypeStruct((images, width), F32),
            jax.ShapeDtypeStruct((2, 8, pixels, share // 2), BF16),
        ),
        in_specs=[vmem, vmem, hbm, vmem, hbm, vmem, vmem, vmem, vmem, vmem],
        out_specs=(vmem,) * 8 + (hbm,),
        scratch_shapes=[
            pltpu.VMEM((blocks + 2 * REACH, ids.shape[0], 128), F32),
            pltpu.VMEM((SLOTS, channels, width), BF16),
            pltpu.VMEM((share, width), BF16),
            pltpu.VMEM((blocks + 2 * REACH, rb, width), F32),
            ext(1, F32), ext(2, F32), ext(3, F32),
            ext(1, BF16), ext(2, BF16), ext(3, BF16),
            halo_bufs,
            pltpu.VMEM((4, blocks, rb, width), F32),
            pltpu.VMEM((4, blocks, rb, width), F32),
            pltpu.VMEM((pixels, 5 * width), BF16),
            pltpu.VMEM((pixels, width), F32),
            pltpu.VMEM((pixels, width), F32),
            pltpu.VMEM((images, channels), F32),
            pltpu.VMEM((4, cols, 8, width), F32),
            pltpu.VMEM((4, rows, 8, width), F32),
            pltpu.VMEM((rows, images, share), F32),
            pltpu.VMEM((cols, images, share), F32),
            pltpu.VMEM((rows, images, width), F32),
            dma((SLOTS,)), dma,
            dma((3, 8)), dma((3, 8)),
            dma((4, cols)), dma((4, cols)),
            dma((4, rows)), dma((4, rows)),
            dma((rows,)), dma((rows,)),
            dma((cols,)), dma((cols,)),
            dma((rows,)), dma((rows,)),
            dma((2, 8)), dma((2, 8)),
        ],
        compiler_params=pltpu.CompilerParams(
            collective_id=0, has_side_effects=True, vmem_limit_bytes=60 * 2**20
        ),
        cost_estimate=pl.CostEstimate(flops=2 * pixels * channels * width * 28, bytes_accessed=40_000_000, transcendentals=0),
    )(x, ids, wat, wpt, wpl, wpj, gain, shift, cot, counts)


def extended(cells, sides, width):
    for axis, dim in sides:
        count = lax.axis_size(axis)
        ends = count - 1
        head = lax.slice_in_dim(cells, 0, width, axis=dim)
        tail = lax.slice_in_dim(cells, cells.shape[dim] - width, cells.shape[dim], axis=dim)
        cells = jnp.concatenate(
            [
                lax.ppermute(tail, axis, [(i, (i + 1) % count) for i in range(ends)]),
                cells,
                lax.ppermute(head, axis, [((i + 1) % count, i) for i in range(ends)]),
            ],
            axis=dim,
        )
    return cells


def image_match(window, own_ids, row_start, col_start):
    rows_here, cols_here = own_ids.shape
    section = window[row_start : row_start + rows_here, col_start : col_start + cols_here]
    return (section == own_ids).astype(jnp.float32).reshape(rows_here * cols_here, 1)


def silu_slope(preact_in):
    sigma = jax.nn.sigmoid(preact_in)
    return sigma * (1.0 + preact_in * (1.0 - sigma))


def transposed(left, right):
    return lax.dot_general(
        left, right, (((1,), (1,)), ((), ())), preferred_element_type=jnp.float32
    )


def shards(
    features, image_ids, w_point, w_atrous, w_pool, w_proj, norm_gain, norm_shift, cotangent
):
    rows_here, cols_here, channels = features.shape
    branch_width = w_point.shape[1]
    pixels = rows_here * cols_here
    grid_rows, grid_cols = image_ids.shape
    total_pixels = float(grid_rows * grid_cols)
    image_count = grid_rows // 16 * (grid_cols // 32)
    dilations = (RATE_LOW, RATE_MID, RATE_TOP)
    margin = RATE_TOP
    row_index = lax.axis_index("rows")
    col_index = lax.axis_index("cols")
    id_padded = jnp.pad(image_ids, margin, constant_values=-1)
    window = lax.dynamic_slice(
        id_padded,
        (row_index * rows_here, col_index * cols_here),
        (rows_here + 2 * margin, cols_here + 2 * margin),
    )
    own_ids = window[margin : margin + rows_here, margin : margin + cols_here]
    own_flat = own_ids.reshape(pixels)
    flattened = features.reshape(pixels, channels)
    padded = extended(features, (("rows", 0), ("cols", 1)), margin)
    one_hot = (own_flat[:, None] == jnp.arange(image_count, dtype=jnp.int32)[None, :]).astype(
        jnp.bfloat16
    )
    local_sums = jnp.einsum("pn,pc->nc", one_hot, flattened, preferred_element_type=jnp.float32)
    counts = jax.ops.segment_sum(
        jnp.ones((grid_rows * grid_cols,), jnp.float32), image_ids.reshape(-1), image_count
    )
    image_totals = lax.psum(local_sums, ("rows", "cols"))
    branch_outs = [jnp.dot(flattened, w_point, preferred_element_type=jnp.float32)]
    for branch, dilation in enumerate(dilations):
        running = jnp.zeros((pixels, branch_width), jnp.float32)
        for stencil in range(9):
            row_shift = (stencil // 3 - 1) * dilation
            col_shift = (stencil % 3 - 1) * dilation
            source = padded[
                margin + row_shift : margin + row_shift + rows_here,
                margin + col_shift : margin + col_shift + cols_here,
            ].reshape(pixels, channels)
            same_image = image_match(window, own_ids, margin + row_shift, margin + col_shift)
            running = running + same_image * jnp.dot(
                source, w_atrous[branch, stencil], preferred_element_type=jnp.float32
            )
        branch_outs.append(running)
    spatial = jnp.stack(branch_outs, axis=1)
    first_sum = jnp.sum(spatial, axis=0)
    second_sum = jnp.sum(spatial * spatial, axis=0)
    first_sum, second_sum = lax.psum((first_sum, second_sum), ("rows", "cols"))
    average = first_sum / total_pixels
    inverse_std = lax.rsqrt(second_sum / total_pixels - average * average + epsilon)
    normed = (spatial - average) * inverse_std
    preact = norm_gain[:4] * normed + norm_shift[:4]
    active = jax.nn.silu(preact).astype(jnp.bfloat16)
    pooled = (image_totals / counts[:, None]).astype(jnp.bfloat16)
    pool_z = jnp.dot(pooled, w_pool, preferred_element_type=jnp.float32)
    pool_avg = jnp.mean(pool_z, axis=0)
    pool_square = jnp.mean(pool_z * pool_z, axis=0)
    pool_inverse = lax.rsqrt(pool_square - pool_avg * pool_avg + epsilon)
    pool_normed = (pool_z - pool_avg) * pool_inverse
    pool_pre = norm_gain[4] * pool_normed + norm_shift[4]
    pool_active = jax.nn.silu(pool_pre).astype(jnp.bfloat16)
    joined = jnp.concatenate(
        [active.reshape(pixels, 4 * branch_width), jnp.take(pool_active, own_flat, axis=0)], axis=1
    )
    final_z = jnp.dot(joined, w_proj, preferred_element_type=jnp.float32)
    final_first, final_second = lax.psum(
        (jnp.sum(final_z, axis=0), jnp.sum(final_z * final_z, axis=0)), ("rows", "cols")
    )
    final_avg = final_first / total_pixels
    final_inverse = lax.rsqrt(final_second / total_pixels - final_avg * final_avg + epsilon)
    final_normed = (final_z - final_avg) * final_inverse
    final_pre = norm_gain[5] * final_normed + norm_shift[5]
    output = jax.nn.silu(final_pre).astype(jnp.bfloat16).reshape(rows_here, cols_here, branch_width)
    upstream = cotangent.reshape(pixels, branch_width).astype(jnp.float32)
    grad_final = upstream * silu_slope(final_pre)
    shift_last, gain_last = lax.psum(
        (jnp.sum(grad_final, axis=0), jnp.sum(grad_final * final_normed, axis=0)), ("rows", "cols")
    )
    grad_final_z = (
        final_inverse
        * (
            grad_final * norm_gain[5]
            - norm_gain[5] * shift_last / total_pixels
            - final_normed * (norm_gain[5] * gain_last / total_pixels)
        )
    ).astype(jnp.bfloat16)
    proj_term = jnp.einsum("pk,pc->kc", joined, grad_final_z, preferred_element_type=jnp.float32)
    grad_joined = transposed(grad_final_z, w_proj)
    grad_pre = grad_joined[:, : 4 * branch_width].reshape(pixels, 4, branch_width) * silu_slope(
        preact
    )
    grad_pixel = grad_joined[:, 4 * branch_width :]
    shift_sums = jnp.sum(grad_pre, axis=0)
    gain_sums = jnp.sum(grad_pre * normed, axis=0)
    image_grads = jax.ops.segment_sum(grad_pixel, own_flat, image_count)
    shift_sums, gain_sums, image_grads = lax.psum(
        (shift_sums, gain_sums, image_grads), ("rows", "cols")
    )
    grad_branch = (
        inverse_std
        * (
            grad_pre * norm_gain[:4]
            - norm_gain[:4] * shift_sums / total_pixels
            - normed * (norm_gain[:4] * gain_sums / total_pixels)
        )
    ).astype(jnp.bfloat16)
    grad_pool_pre = image_grads * silu_slope(pool_pre)
    pool_shift = jnp.sum(grad_pool_pre, axis=0)
    pool_gain = jnp.sum(grad_pool_pre * pool_normed, axis=0)
    grad_pool_z = (
        pool_inverse
        * (
            grad_pool_pre * norm_gain[4]
            - norm_gain[4] * pool_shift / image_count
            - pool_normed * (norm_gain[4] * pool_gain / image_count)
        )
    ).astype(jnp.bfloat16)
    row_share = channels // lax.axis_size("rows")
    pool_columns = lax.dynamic_slice_in_dim(pooled, row_index * row_share, row_share, 1)
    grad_pool = jnp.einsum(
        "nk,nc->kc", pool_columns, grad_pool_z, preferred_element_type=jnp.float32
    )
    grad_pooled = transposed(grad_pool_z, w_pool) / counts[:, None]
    grad_input = jnp.take(grad_pooled, own_flat, axis=0) + transposed(grad_branch[:, 0], w_point)
    point_term = jnp.einsum(
        "pk,pc->kc", flattened, grad_branch[:, 0], preferred_element_type=jnp.float32
    )
    stacked = grad_branch[:, 1:].reshape(rows_here, cols_here, 3 * branch_width)
    grad_padded = extended(stacked, (("rows", 0), ("cols", 1)), margin)
    rim_list = [
        grad_padded[:, :, branch * branch_width : (branch + 1) * branch_width]
        for branch in range(3)
    ]
    rim_bases = [margin, margin, margin]
    atrous_terms = []
    for branch, dilation in enumerate(dilations):
        tap_terms = []
        rim_base = rim_bases[branch]
        for stencil in range(9):
            row_shift = (stencil // 3 - 1) * dilation
            col_shift = (stencil % 3 - 1) * dilation
            source = padded[
                margin + row_shift : margin + row_shift + rows_here,
                margin + col_shift : margin + col_shift + cols_here,
            ].reshape(pixels, channels)
            same_image = image_match(window, own_ids, margin + row_shift, margin + col_shift)
            masked = same_image.astype(jnp.bfloat16) * grad_branch[:, branch + 1]
            tap_terms.append(
                jnp.einsum("pk,pc->kc", source, masked, preferred_element_type=jnp.float32)
            )
            incoming = rim_list[branch][
                rim_base - row_shift : rim_base - row_shift + rows_here,
                rim_base - col_shift : rim_base - col_shift + cols_here,
            ].reshape(pixels, branch_width)
            back_image = image_match(window, own_ids, margin - row_shift, margin - col_shift)
            grad_input = grad_input + back_image * transposed(incoming, w_atrous[branch, stencil])
        atrous_terms.append(jnp.stack(tap_terms))
    atrous_term = jnp.stack(atrous_terms)
    shared = (
        lax.psum_scatter(
            point_term.astype(jnp.bfloat16), "rows", scatter_dimension=0, tiled=True
        ).astype(jnp.float32),
        lax.psum_scatter(
            atrous_term.astype(jnp.bfloat16), "rows", scatter_dimension=2, tiled=True
        ).astype(jnp.float32),
        lax.psum_scatter(
            proj_term.astype(jnp.bfloat16), "rows", scatter_dimension=0, tiled=True
        ).astype(jnp.float32),
    )
    shared = (
        lax.psum(shared[0].astype(jnp.bfloat16), "cols").astype(jnp.float32),
        lax.psum(shared[1].astype(jnp.bfloat16), "cols").astype(jnp.float32),
        lax.psum(shared[2].astype(jnp.bfloat16), "cols").astype(jnp.float32),
    )
    grad_gain = jnp.concatenate([gain_sums, pool_gain[None], gain_last[None]], axis=0)
    grad_shift = jnp.concatenate([shift_sums, pool_shift[None], shift_last[None]], axis=0)
    grad_features = grad_input.astype(jnp.bfloat16).reshape(rows_here, cols_here, channels)
    return (
        output,
        grad_features,
        shared[0],
        shared[1],
        grad_pool,
        shared[2],
        grad_gain,
        grad_shift,
    )


def to_blocks(cells):
    height, breadth, depth = cells.shape
    cells = cells.reshape(height, breadth // STEP, STEP, depth)
    return cells.transpose(1, 0, 2, 3).reshape(height * breadth, depth)


def from_blocks(cells, height, breadth):
    depth = cells.shape[-1]
    cells = cells.reshape(breadth // STEP, height, STEP, depth)
    return cells.transpose(1, 0, 2, 3).reshape(height, breadth, depth)


def id_columns(ids):
    height, breadth = ids.shape
    table = ids.reshape(height, breadth // STEP, STEP).transpose(0, 2, 1).reshape(height * STEP, breadth // STEP)
    return jnp.pad(table.astype(F32), ((0, 0), (0, 128 - breadth // STEP)))


def quick_shards(
    features, image_ids, w_point, w_atrous, w_pool, w_proj, norm_gain, norm_shift, cotangent
):
    rows_here, cols_here, channels = features.shape
    branch_width = w_point.shape[1]
    pixels = rows_here * cols_here
    grid_rows, grid_cols = image_ids.shape
    image_count = grid_rows // 16 * (grid_cols // 32)
    images = -(-image_count // 16) * 16
    margin = RATE_TOP
    rows, cols = lax.axis_size("rows"), lax.axis_size("cols")
    row_index = lax.axis_index("rows")
    col_index = lax.axis_index("cols")
    id_padded = jnp.pad(image_ids, margin, constant_values=-1)
    window = lax.dynamic_slice(
        id_padded,
        (row_index * rows_here, col_index * cols_here),
        (rows_here + 2 * margin, cols_here + 2 * margin),
    )
    own_ids = window[margin : margin + rows_here, margin : margin + cols_here]
    own_flat = own_ids.reshape(pixels)
    counts = jnp.sum(
        (image_ids.reshape(-1, 1) == jnp.arange(images, dtype=jnp.int32)[None, :]).astype(F32), axis=0
    )
    counts = jnp.maximum(counts, 1.0)
    x = to_blocks(features)
    cot = to_blocks(cotangent)
    output, dz, proj_term, stats, pooled, pool_normed, pool_slope, dap, xsub = forward_call(
        rows, cols, image_count, x, id_columns(window), w_atrous, w_point, w_pool, w_proj,
        norm_gain, norm_shift, cot, jnp.broadcast_to(counts[:, None], (images, 128)),
    )
    output = from_blocks(output, rows_here, cols_here)
    flattened = features.reshape(pixels, channels)
    grad_branch = dz.reshape(4, cols_here // STEP, rows_here, STEP, branch_width).transpose(2, 1, 3, 0, 4).reshape(pixels, 4, branch_width)
    image_grads = lax.psum(dap, ("rows", "cols"))
    grad_pool_pre = image_grads * pool_slope
    pool_shift = jnp.sum(grad_pool_pre, axis=0)
    pool_gain = jnp.sum(grad_pool_pre * pool_normed, axis=0)
    grad_pool_z = (
        stats[10]
        * (
            grad_pool_pre * norm_gain[4]
            - norm_gain[4] * pool_shift / image_count
            - pool_normed * (norm_gain[4] * pool_gain / image_count)
        )
    ).astype(BF16)
    grad_pool = contract_rows(pooled, grad_pool_z)
    grad_pooled = contract_lanes(grad_pool_z, w_pool) / counts[:, None]
    one_hot = (own_flat[:, None] == jnp.arange(images, dtype=jnp.int32)[None, :]).astype(BF16)
    grad_input = jnp.dot(one_hot, grad_pooled.astype(BF16), preferred_element_type=F32)
    grad_input = grad_input + contract_lanes(grad_branch[:, 0], w_point)
    point_term = contract_rows(flattened, grad_branch[:, 0])
    stacked = grad_branch[:, 1:].reshape(rows_here, cols_here, 3 * branch_width)
    grad_padded = extended(stacked, (("rows", 0), ("cols", 1)), margin)
    terms = []
    for branch, dilation in enumerate((RATE_LOW, RATE_MID, RATE_TOP)):
        for stencil in range(9):
            row_shift = (stencil // 3 - 1) * dilation
            col_shift = (stencil % 3 - 1) * dilation
            incoming = grad_padded[
                margin - row_shift : margin - row_shift + rows_here,
                margin - col_shift : margin - col_shift + cols_here,
                branch * branch_width : (branch + 1) * branch_width,
            ].reshape(pixels, branch_width)
            same = image_match(window, own_ids, margin - row_shift, margin - col_shift)
            masked = jnp.where(same > 0, incoming, jnp.zeros((), BF16))
            grad_input = grad_input + contract_lanes(masked, w_atrous[branch, stencil])
            terms.append(contract_rows(flattened, masked))
    atrous_term = jnp.stack(terms).reshape(3, 9, channels, branch_width)

    def shared(term, dim):
        part = lax.psum_scatter(term.astype(BF16), "rows", scatter_dimension=dim, tiled=True)
        return lax.psum(part, "cols").astype(F32)

    grad_gain = jnp.concatenate([stats[4:8], pool_gain[None], stats[9:10]], axis=0)
    grad_shift = jnp.concatenate([stats[0:4], pool_shift[None], stats[8:9]], axis=0)
    grad_features = grad_input.astype(BF16).reshape(rows_here, cols_here, channels)
    return (
        output, grad_features, shared(point_term, 0), shared(atrous_term, 2), grad_pool,
        shared(proj_term, 0), grad_gain, grad_shift,
    )


def solution(mesh):
    placed = (P("rows", "cols", None), P(), P(), P(), P(), P(), P(), P(), P("rows", "cols", None))
    quick = mesh.shape["rows"] == 8 and mesh.shape["cols"] == 4
    return jax.shard_map(
        quick_shards if quick else shards,
        mesh=mesh,
        in_specs=placed,
        out_specs=(
            P("rows", "cols", None),
            P("rows", "cols", None),
            P("rows", None),
            P(None, None, "rows", None),
            P("rows", None),
            P("rows", None),
            P(),
            P(),
        ),
        check_vma=False,
    )
```

```python
import functools
import jax
import jax.numpy as jnp
from jax import lax
from jax.experimental import pallas as pl
from jax.experimental.pallas import tpu as pltpu
from jax.sharding import PartitionSpec as P

MESH = pl.DeviceIdType.MESH
RATE_LOW = 6
RATE_MID = 12
RATE_TOP = 18
STEP = RATE_LOW
REACH = RATE_TOP // STEP
HALO = {1: 48, 2: 80, 3: 112}
SLOTS = 4
epsilon = 1e-05
F32 = jnp.float32
BF16 = jnp.bfloat16


def wide(column, width):
    return jnp.concatenate([column] * (width // column.shape[-1]), axis=-1)


def silu_parts(preact):
    sigma = jax.nn.sigmoid(preact)
    return preact * sigma, sigma * (1.0 + preact * (1.0 - sigma))


def contract_rows(left, right):
    return lax.dot_general(left, right, (((0,), (0,)), ((), ())), preferred_element_type=F32)


def contract_lanes(left, right):
    return lax.dot_general(left, right, (((1,), (1,)), ((), ())), preferred_element_type=F32)


def greet_all(rows, cols, r, c):
    barrier = pltpu.get_barrier_semaphore()
    for dr in range(rows):
        for dc in range(cols):
            if dr or dc:
                other = (lax.rem(r + dr, rows), lax.rem(c + dc, cols))
                pl.semaphore_signal(barrier, inc=1, device_id=other, device_id_type=MESH)
    pl.semaphore_wait(barrier, rows * cols - 1)


class Exchange:
    def __init__(self, axis_size, place, to_device, slots, send_sems, recv_sems):
        self.size, self.place, self.to_device = axis_size, place, to_device
        self.slots, self.send_sems, self.recv_sems = slots, send_sems, recv_sems

    def copy(self, step, source=None):
        other = lax.rem(self.place + step, self.size)
        mine = self.slots.at[self.place]
        return pltpu.make_async_remote_copy(
            src_ref=mine if source is None else source(other),
            dst_ref=mine,
            send_sem=self.send_sems.at[step],
            recv_sem=self.recv_sems.at[self.place],
            device_id=self.to_device(other),
            device_id_type=MESH,
        )

    def start(self, source=None):
        for step in range(1, self.size):
            self.copy(step, source).start()

    def finish(self, source=None):
        for step in range(1, self.size):
            other = lax.rem(self.place + step, self.size)
            there = self.slots.at[other]
            pltpu.make_async_remote_copy(
                src_ref=there,
                dst_ref=there,
                send_sem=self.send_sems.at[step],
                recv_sem=self.recv_sems.at[other],
                device_id=self.to_device(other),
                device_id_type=MESH,
            ).wait_recv()
        for step in range(1, self.size):
            self.copy(step, source).wait_send()

    def total(self):
        value = self.slots[0]
        for other in range(1, self.size):
            value = value + self.slots[other]
        return value


def forward_kernel(
    rows, cols, image_count, total_pixels,
    x_ref, ids_ref, wat_ref, wpt_ref, wpl_ref, wpj_ref, gain_ref, shift_ref, cot_ref, counts_ref,
    out_ref, dz_ref, pj_ref, stat_ref, pooled_ref, pooln_ref, pools_ref, dap_ref, xsub_ref,
    idrep, wbuf, wplbuf, ubuf, zx1, zx2, zx3, zs1, zs2, zs3,
    halo_bufs, zn, slope, joined, zf, dzf, isum, cbuf, rbuf, pr_buf, pc_buf, pz_buf,
    wsem, wplsem, hsend, hrecv, csend, crecv, rsend, rrecv, psend, precv, pcsend, pcrecv, pzsend, pzrecv,
    xsend, xrecv,
):
    r, c = lax.axis_index("rows"), lax.axis_index("cols")
    blocks, rb, width = zn.shape[1], zn.shape[2], zn.shape[3]
    pixels = blocks * rb
    own = REACH * 36
    images = isum.shape[0]
    zx, zs = {1: zx1, 2: zx2, 3: zx3}, {1: zs1, 2: zs2, 3: zs3}
    order = (3, 2, 1)
    taps = 27

    def weight_copy(n):
        branch, tap = 2 - n // 9, lax.rem(n, 9)
        slot = lax.rem(n, SLOTS)
        return pltpu.make_async_copy(wat_ref.at[branch, tap], wbuf.at[slot], wsem.at[slot])

    for n in range(SLOTS - 1):
        weight_copy(jnp.int32(n)).start()
    share = x_ref.shape[1] // rows
    pool_weight = pltpu.make_async_copy(
        wpl_ref.at[pl.ds(pl.multiple_of(r * share, share), share)], wplbuf, wplsem
    )
    pool_weight.start()
    for block in range(idrep.shape[0]):
        idrep[block] = jnp.broadcast_to(ids_ref[:, block : block + 1], idrep.shape[1:])
    greet_all(rows, cols, r, c)

    own_ids = jnp.concatenate([idrep[REACH + a, own : own + rb, :] for a in range(blocks)], axis=0)
    lanes = lax.broadcasted_iota(jnp.int32, (pixels, 128), 1).astype(F32)
    one_hot = jnp.concatenate(
        [(own_ids == lanes + 128.0 * part).astype(F32).astype(BF16) for part in range(pl.cdiv(images, 128))],
        axis=1,
    )
    for part in range(rows):
        piece = slice(part * share, (part + 1) * share)
        isum[:, piece] = contract_rows(one_hot, x_ref[:, piece])[:images]
    pool_rows = Exchange(rows, r, lambda other: (other, c), pr_buf, psend, precv)

    def share_of(other):
        return isum.at[:, pl.ds(pl.multiple_of(other * share, share), share)]

    pr_buf[r] = isum[:, pl.ds(pl.multiple_of(r * share, share), share)]
    pool_rows.start(share_of)

    def halo_copies(m):
        height = HALO[m]
        a_range = {-1: (0, m), 0: (m, blocks), 1: (m + blocks, m)}
        r_range = {-1: (0, height), 0: (height, rb), 1: (height + rb, height)}
        copies = []
        for place, (dr, dc) in enumerate(DIRECTIONS):
            a0, na = a_range[dc]
            r0, nr = r_range[dr]
            copies.append(
                (
                    dr,
                    dc,
                    pltpu.make_async_remote_copy(
                        src_ref=zs[m].at[pl.ds(a0, na), pl.ds(r0, nr)],
                        dst_ref=halo_bufs[(m - 1) * 8 + place],
                        send_sem=hsend.at[m - 1, place],
                        recv_sem=hrecv.at[m - 1, place],
                        device_id=(lax.rem(r + dr + rows, rows), lax.rem(c + dc + cols, cols)),
                        device_id_type=MESH,
                    ),
                )
            )
        return copies

    def inside(dr, dc):
        return (r + dr >= 0) & (r + dr < rows) & (c + dc >= 0) & (c + dc < cols)

    for position, m in enumerate(order):
        height = HALO[m]

        @pl.loop(0, blocks + 2 * m)
        def _(block):
            zx[m][block] = jnp.zeros(zx[m].shape[1:], F32)

        for i in range(3):
            @pl.loop(0, blocks + 2 * m)
            def _(block):
                ubuf[block] = jnp.zeros(ubuf.shape[1:], F32)

            @pl.loop(0, 3)
            def _(j):
                n = position * 9 + 3 * i + j
                slot = lax.rem(n, SLOTS)
                ahead = n + SLOTS - 1

                @pl.when(ahead < taps)
                def _():
                    weight_copy(ahead).start()

                weight_copy(n).wait()
                product = jnp.dot(x_ref[...], wbuf[slot], preferred_element_type=F32)
                for a in range(blocks):
                    same = idrep[REACH + a, own : own + rb] == idrep[REACH + a - (j - 1) * m, own : own + rb]
                    part = product[a * rb : (a + 1) * rb]
                    ubuf[a + (2 - j) * m] += jnp.where(wide(same.astype(F32), width) > 0.0, part, 0.0)

            up = (i - 1) * 36 * m

            @pl.loop(0, blocks + 2 * m)
            def _(block):
                value = ubuf[block]
                if i != 1:
                    here = REACH - m + block
                    same = idrep[here, own : own + rb] == idrep[here, own - up : own - up + rb]
                    value = jnp.where(wide(same.astype(F32), width) > 0.0, value, 0.0)
                zx[m][block, height - up : height - up + rb] += value

        @pl.loop(0, blocks + 2 * m)
        def _(block):
            zs[m][block] = zx[m][block].astype(BF16)

        for dr, dc, copy in halo_copies(m):
            pl.when(inside(dr, dc))(copy.start)

        @pl.loop(0, blocks)
        def _(a):
            zn[m, a] = zx[m][m + a, height : height + rb]

    product = jnp.dot(x_ref[...], wpt_ref[...], preferred_element_type=F32)
    for a in range(blocks):
        zn[0, a] = product[a * rb : (a + 1) * rb]

    members = [(dy, dx, dk) for dy in range(2) for dx in range(2) for dk in range(2)]
    half = share // 2

    def channel_slices(y, x, k):
        return [pl.multiple_of((2 * (2 * k + l) + y) * share + x * half, 128) for l in range(2)]

    def member_copies():
        mine = lax.rem(r, 2) * cols + c
        copies = []
        for step, (dy, dx, dk) in enumerate(members):
            y, x, k = lax.rem(r + dy, 2), lax.rem(c // 2 + dx, 2), lax.rem(c + dk, 2)
            for l, start in enumerate(channel_slices(y, x, k)):
                source = x_ref.at[:, pl.ds(start, half)]
                target = xsub_ref.at[l, mine]
                if step == 0:
                    copies.append(pltpu.make_async_copy(source, target, xrecv.at[l, mine]))
                else:
                    copies.append(
                        pltpu.make_async_remote_copy(
                            src_ref=source,
                            dst_ref=target,
                            send_sem=xsend.at[l, step],
                            recv_sem=xrecv.at[l, mine],
                            device_id=(2 * (r // 2) + y, 2 * x + k),
                            device_id_type=MESH,
                        )
                    )
        return copies

    for copy in member_copies():
        copy.start()

    pool_rows.finish(share_of)
    pool_cols = Exchange(cols, c, lambda other: (r, other), pc_buf, pcsend, pcrecv)
    pc_buf[c] = pool_rows.total()
    pool_cols.start()
    pool_cols.finish()
    counts = counts_ref[...]
    pooled = (pool_cols.total() / wide(counts, share)).astype(BF16)
    pooled_ref[...] = pooled
    pool_weight.wait()
    pool_z = Exchange(rows, r, lambda other: (other, c), pz_buf, pzsend, pzrecv)
    pz_buf[r] = jnp.dot(pooled, wplbuf[...], preferred_element_type=F32)
    pool_z.start()
    pool_z.finish()
    zp = pool_z.total()
    pool_avg = jnp.sum(zp, axis=0, keepdims=True) / image_count
    pool_square = jnp.sum(zp * zp, axis=0, keepdims=True) / image_count
    pool_inverse = lax.rsqrt(pool_square - pool_avg * pool_avg + epsilon)
    pool_normed = (zp - pool_avg) * pool_inverse
    pool_active, pool_slope = silu_parts(gain_ref[4:5] * pool_normed + shift_ref[4:5])
    pooln_ref[...] = pool_normed
    pools_ref[...] = pool_slope
    spare = one_hot.shape[1] - images
    pool_active = jnp.concatenate([pool_active, jnp.zeros((spare, width), F32)], axis=0).astype(BF16)
    joined[:, 4 * width : 5 * width] = jnp.dot(one_hot, pool_active, preferred_element_type=F32).astype(BF16)

    for m in order:
        height = HALO[m]
        a_range = {-1: (blocks - m, m), 0: (0, blocks), 1: (0, m)}
        r_range = {-1: (rb - height, height), 0: (0, rb), 1: (0, height)}
        for place, (dr, dc, copy) in enumerate(halo_copies(m)):
            a0, na = a_range[dc]
            r0, nr = r_range[dr]

            @pl.when(inside(-dr, -dc))
            def _():
                copy.wait_recv()
                for a in range(na):
                    zn[m, a0 + a, r0 : r0 + nr] += halo_bufs[(m - 1) * 8 + place][a].astype(F32)

    def all_sum(step, value):
        across = Exchange(cols, c, lambda other: (r, other), cbuf.at[step], csend.at[step], crecv.at[step])
        cbuf[step, c] = value
        across.start()
        across.finish()
        down = Exchange(rows, r, lambda other: (other, c), rbuf.at[step], rsend.at[step], rrecv.at[step])
        rbuf[step, r] = across.total()
        down.start()
        down.finish()
        return down.total()

    zero = jnp.zeros((1, width), F32)

    def row_sum(value):
        return jnp.sum(value, axis=0, keepdims=True)

    firsts, seconds = [], []
    for k in range(4):
        first, second = zero, zero
        for a in range(blocks):
            value = zn[k, a]
            first, second = first + row_sum(value), second + row_sum(value * value)
        firsts.append(first)
        seconds.append(second)
    moments = all_sum(0, jnp.concatenate(firsts + seconds, axis=0))
    average = moments[0:4] / total_pixels
    inverse = lax.rsqrt(moments[4:8] / total_pixels - average * average + epsilon)
    for k in range(4):
        @pl.loop(0, blocks)
        def _(a):
            normed = (zn[k, a] - average[k : k + 1]) * inverse[k : k + 1]
            active, slant = silu_parts(gain_ref[k : k + 1] * normed + shift_ref[k : k + 1])
            zn[k, a] = normed
            slope[k, a] = slant
            joined[pl.ds(pl.multiple_of(a * rb, rb), rb), k * width : (k + 1) * width] = active.astype(BF16)

    zf[...] = jnp.dot(joined[...], wpj_ref[...], preferred_element_type=F32)
    first, second = zero, zero
    for a in range(blocks):
        value = zf[a * rb : (a + 1) * rb]
        first, second = first + row_sum(value), second + row_sum(value * value)
    moments = all_sum(1, jnp.concatenate([first, second] + [zero] * 6, axis=0))
    final_avg = moments[0:1] / total_pixels
    final_inverse = lax.rsqrt(moments[1:2] / total_pixels - final_avg * final_avg + epsilon)
    shift_last, gain_last = zero, zero
    for a in range(blocks):
        piece = slice(a * rb, (a + 1) * rb)
        normed = (zf[piece] - final_avg) * final_inverse
        result, slant = silu_parts(gain_ref[5:6] * normed + shift_ref[5:6])
        out_ref[piece] = result.astype(BF16)
        grad = cot_ref[piece].astype(F32) * slant
        zf[piece] = normed
        slope_last = grad
        dzf[piece] = slope_last
        shift_last, gain_last = shift_last + row_sum(grad), gain_last + row_sum(grad * normed)
    sums = all_sum(2, jnp.concatenate([shift_last, gain_last] + [zero] * 6, axis=0))
    shift_last, gain_last = sums[0:1], sums[1:2]
    gain = gain_ref[5:6]
    for a in range(blocks):
        piece = slice(a * rb, (a + 1) * rb)
        dzf[piece] = final_inverse * (
            dzf[piece] * gain
            - gain * shift_last / total_pixels
            - zf[piece] * (gain * gain_last / total_pixels)
        )
    grad_final = dzf[...].astype(BF16)

    shifts, gains = [], []
    for k in range(4):
        grad = contract_lanes(grad_final, wpj_ref[k * width : (k + 1) * width])
        shift_sum, gain_sum = zero, zero
        for a in range(blocks):
            part = grad[a * rb : (a + 1) * rb] * slope[k, a]
            slope[k, a] = part
            shift_sum, gain_sum = shift_sum + row_sum(part), gain_sum + row_sum(part * zn[k, a])
        shifts.append(shift_sum)
        gains.append(gain_sum)
    grad_pixel = contract_lanes(grad_final, wpj_ref[4 * width : 5 * width])
    upper = grad_pixel.astype(BF16)
    lower = (grad_pixel - upper.astype(F32)).astype(BF16)
    dap_ref[...] = (contract_rows(one_hot, upper) + contract_rows(one_hot, lower))[:images]
    sums = all_sum(3, jnp.concatenate(shifts + gains, axis=0))
    for k in range(4):
        gain = gain_ref[k : k + 1]
        from_shift = gain * sums[k : k + 1] / total_pixels
        from_gain = gain * sums[4 + k : 5 + k] / total_pixels

        @pl.loop(0, blocks)
        def _(a):
            dz_ref[k, a] = (
                inverse[k : k + 1] * (slope[k, a] * gain - from_shift - zn[k, a] * from_gain)
            ).astype(BF16)

    for k in range(5):
        piece = slice(k * width, (k + 1) * width)
        pj_ref[piece] = contract_rows(joined[:, piece], grad_final).astype(BF16)
    stat_ref[...] = jnp.concatenate([sums, shift_last, gain_last, pool_inverse] + [zero] * 5, axis=0)

    for m in order:
        for dr, dc, copy in halo_copies(m):
            pl.when(inside(dr, dc))(copy.wait_send)
    for step, copy in enumerate(member_copies()):
        if step < 2:
            copy.wait()
        else:
            copy.wait_send()
    for l in range(2):
        for step, (dy, dx, dk) in enumerate(members):
            if step:
                y, x, k = lax.rem(r + dy, 2), lax.rem(c // 2 + dx, 2), lax.rem(c + dk, 2)
                there = xsub_ref.at[l, y * cols + 2 * x + k]
                pltpu.make_async_remote_copy(
                    src_ref=there,
                    dst_ref=there,
                    send_sem=xsend.at[l, step],
                    recv_sem=xrecv.at[l, y * cols + 2 * x + k],
                    device_id=(2 * (r // 2) + y, 2 * x + k),
                    device_id_type=MESH,
                ).wait_recv()


DIRECTIONS = ((-1, 0), (1, 0), (-1, -1), (-1, 1), (1, -1), (1, 1), (0, -1), (0, 1))


def forward_call(rows, cols, image_count, x, ids, wat, wpt, wpl, wpj, gain, shift, cot, counts):
    pixels, channels = x.shape
    width = wpt.shape[1]
    blocks, rb = 4, pixels // 4
    images = counts.shape[0]
    share = channels // rows
    total_pixels = float(pixels * rows * cols)
    vmem = pl.BlockSpec(memory_space=pltpu.VMEM)
    hbm = pl.BlockSpec(memory_space=pl.ANY)

    def ext(m, kind):
        return pltpu.VMEM((blocks + 2 * m, 2 * HALO[m] + rb, width), kind)

    halo_bufs = []
    for m in (1, 2, 3):
        for dr, dc in DIRECTIONS:
            halo_bufs.append(pltpu.VMEM((m if dc else blocks, HALO[m] if dr else rb, width), BF16))
    dma = pltpu.SemaphoreType.DMA
    return pl.pallas_call(
        functools.partial(forward_kernel, rows, cols, float(image_count), total_pixels),
        out_shape=(
            jax.ShapeDtypeStruct((pixels, width), BF16),
            jax.ShapeDtypeStruct((4, blocks, rb, width), BF16),
            jax.ShapeDtypeStruct((5 * width, width), BF16),
            jax.ShapeDtypeStruct((16, width), F32),
            jax.ShapeDtypeStruct((images, share), BF16),
            jax.ShapeDtypeStruct((images, width), F32),
            jax.ShapeDtypeStruct((images, width), F32),
            jax.ShapeDtypeStruct((images, width), F32),
            jax.ShapeDtypeStruct((2, 8, pixels, share // 2), BF16),
        ),
        in_specs=[vmem, vmem, hbm, vmem, hbm, vmem, vmem, vmem, vmem, vmem],
        out_specs=(vmem,) * 8 + (hbm,),
        scratch_shapes=[
            pltpu.VMEM((blocks + 2 * REACH, ids.shape[0], 128), F32),
            pltpu.VMEM((SLOTS, channels, width), BF16),
            pltpu.VMEM((share, width), BF16),
            pltpu.VMEM((blocks + 2 * REACH, rb, width), F32),
            ext(1, F32), ext(2, F32), ext(3, F32),
            ext(1, BF16), ext(2, BF16), ext(3, BF16),
            halo_bufs,
            pltpu.VMEM((4, blocks, rb, width), F32),
            pltpu.VMEM((4, blocks, rb, width), F32),
            pltpu.VMEM((pixels, 5 * width), BF16),
            pltpu.VMEM((pixels, width), F32),
            pltpu.VMEM((pixels, width), F32),
            pltpu.VMEM((images, channels), F32),
            pltpu.VMEM((4, cols, 8, width), F32),
            pltpu.VMEM((4, rows, 8, width), F32),
            pltpu.VMEM((rows, images, share), F32),
            pltpu.VMEM((cols, images, share), F32),
            pltpu.VMEM((rows, images, width), F32),
            dma((SLOTS,)), dma,
            dma((3, 8)), dma((3, 8)),
            dma((4, cols)), dma((4, cols)),
            dma((4, rows)), dma((4, rows)),
            dma((rows,)), dma((rows,)),
            dma((cols,)), dma((cols,)),
            dma((rows,)), dma((rows,)),
            dma((2, 8)), dma((2, 8)),
        ],
        compiler_params=pltpu.CompilerParams(
            collective_id=0, has_side_effects=True, vmem_limit_bytes=60 * 2**20
        ),
        cost_estimate=pl.CostEstimate(flops=2 * pixels * channels * width * 28, bytes_accessed=40_000_000, transcendentals=0),
    )(x, ids, wat, wpt, wpl, wpj, gain, shift, cot, counts)


def backward_kernel(
    rows, cols, image_count, height,
    dz_ref, xsub_ref, ids_ref, wat_ref, wpt_ref, wpl_ref, gain_ref, counts_ref,
    pooled_ref, pooln_ref, pools_ref, dap_ref, stat_ref,
    gx_ref, dw_ref, gpool_ref, gstat_ref,
    ext0, ext1, ext2, ext3, shifted, colmask, idrep, gmat, gown, xall, xt, acc, wbuf, wpt,
    send1, recv1, keep, relay, dw, pcbuf, prbuf,
    xsem, wsem, wptsem, zsend, zrecv, agsend, agrecv, s1send, s1recv, s2send, s2recv, s3send, s3recv,
    pcsend, pcrecv, prsend, prrecv, outsem,
):
    r, c = lax.axis_index("rows"), lax.axis_index("cols")
    z, y = r // 2, lax.rem(r, 2)
    x, k = c // 2, lax.rem(c, 2)
    levels = rows // 2
    z_lo, z_hi = lax.rem(z, 2), z // 2
    blocks, rb, width = dz_ref.shape[1:]
    pair = 2 * rb
    across = cols * blocks
    pixels = blocks * rb
    own = REACH * 36
    half = xt.shape[0] // 2
    images = dap_ref.shape[0]
    ext = {0: ext0, 1: ext1, 2: ext2, 3: ext3}
    tall = {0: 0, **HALO}
    directs = ((0, 1), (1, 0), (1, 1))

    def x_copy(l, dev, a):
        dev_y, dev_c = dev // cols, lax.rem(dev, cols)
        start = pl.multiple_of((dev_c * blocks + a) * pair + dev_y * rb, 16)
        return pltpu.make_async_copy(
            xsub_ref.at[l, dev, a], xall.at[l, pl.ds(start, rb)], xsem.at[l, dev, a]
        )

    for l in range(2):
        for a in range(blocks):
            @pl.loop(0, 2 * cols)
            def _(dev):
                x_copy(l, dev, a).start()

    def weight_copy(n, j):
        branch, i = n // 3, lax.rem(n, 3)
        slot = lax.rem(n, 2)
        return pltpu.make_async_copy(
            wat_ref.at[branch, 3 * i + j],
            wbuf.at[slot, :, pl.ds(j * width, width)],
            wsem.at[slot, j],
        )

    point_copy = pltpu.make_async_copy(wpt_ref, wpt, wptsem)
    point_copy.start()
    for n in range(2):
        for j in range(3):
            weight_copy(jnp.int32(n), j).start()

    greet_all(rows, cols, r, c)

    def has_rim(dev_y):
        return (dev_y == 1) & (z >= 1) | (dev_y == 0) & (z <= levels - 2)

    def rim_copy(m, sending):
        high = tall[m]
        start = pl.multiple_of(y * (rb - high), 16)
        target = pl.multiple_of((1 - y) * (high + pair), 16)
        return pltpu.make_async_remote_copy(
            src_ref=dz_ref.at[m, :, pl.ds(start, high)],
            dst_ref=ext[m].at[pl.ds(c * blocks, blocks), pl.ds(target, high)],
            send_sem=zsend.at[m],
            recv_sem=zrecv.at[m],
            device_id=(lax.rem(r + 4 * y - 2 + rows, rows), c),
            device_id_type=MESH,
        )

    sends_rim = (y == 1) & (z <= levels - 2) | (y == 0) & (z >= 1)

    def item(m, kind, dev_y, dev_c):
        high = tall[m]
        if kind == 0:
            return ext[m].at[pl.ds(dev_c * blocks, blocks), pl.ds(pl.multiple_of(high + rb * dev_y, 16), rb)]
        return ext[m].at[
            pl.ds(dev_c * blocks, blocks), pl.ds(pl.multiple_of((1 - dev_y) * (high + pair), 16), high)
        ]

    def gather_copy(m, kind, dev_y, dev_c, slot, target):
        piece = item(m, kind, dev_y, dev_c)
        return pltpu.make_async_remote_copy(
            src_ref=piece,
            dst_ref=piece,
            send_sem=agsend.at[m, kind, slot],
            recv_sem=agrecv.at[m, kind, dev_y * cols + dev_c],
            device_id=target,
            device_id_type=MESH,
        )

    sibling = (r, 2 * x + 1 - k)

    def place(dy, dx):
        return lax.rem(y + dy, 2), 2 * lax.rem(x + dx, 2) + k

    def if_there(kind, dev_y, action):
        if kind == 0:
            action()
        else:
            pl.when(has_rim(dev_y))(action)

    def kinds(m):
        return (0,) if m == 0 else (0, 1)

    def first_copies(m, kind):
        copies = []
        for slot, (dy, dx) in enumerate(directs):
            dev_y, dev_c = place(dy, dx)
            copies.append(gather_copy(m, kind, y, c, slot, (2 * z + dev_y, dev_c)))
        copies.append(gather_copy(m, kind, y, c, 3, sibling))
        return copies

    def start_first(m, kind):
        def action():
            for copy in first_copies(m, kind):
                copy.start()

        if_there(kind, y, action)

    def forward(m):
        for kind in kinds(m):
            for slot, (dy, dx) in enumerate(directs):
                dev_y, dev_c = place(dy, dx)

                def action():
                    copy = gather_copy(m, kind, dev_y, dev_c, 4 + slot, sibling)
                    copy.wait_recv()
                    copy.start()

                if_there(kind, dev_y, action)

    def finish_gather(m):
        for kind in kinds(m):
            for dy, dx in ((0, 0),) + directs:
                dev_y, dev_c = place(dy, dx)
                dev_c = dev_c + 1 - 2 * k
                if_there(kind, dev_y, lambda: gather_copy(m, kind, dev_y, dev_c, 0, sibling).wait_recv())

    def finish_sends(m):
        for kind in kinds(m):
            def action():
                for copy in first_copies(m, kind):
                    copy.wait_send()

            if_there(kind, y, action)
            for slot, (dy, dx) in enumerate(directs):
                dev_y, dev_c = place(dy, dx)
                if_there(
                    kind, dev_y, lambda: gather_copy(m, kind, dev_y, dev_c, 4 + slot, sibling).wait_send()
                )

    def start_branch(m):
        high = tall[m]
        for a in range(blocks):
            ext[m][c * blocks + a, pl.ds(pl.multiple_of(high + rb * y, 16), rb)] = dz_ref[m, a]
        start_first(m, 0)

    def start_rims(m):
        def action():
            rim_copy(m, False).wait_recv()
            for copy in first_copies(m, 1):
                copy.start()

        pl.when(has_rim(y))(action)

    for m in (1, 2, 3):
        pl.when(sends_rim)(rim_copy(m, True).start)
    start_branch(1)
    start_rims(1)
    start_branch(2)
    start_rims(2)

    pool_cols = Exchange(cols, c, lambda other: (r, other), pcbuf, pcsend, pcrecv)
    pcbuf[c] = dap_ref[...]
    pool_cols.start()

    for block in range(across):
        idrep[block] = jnp.broadcast_to(ids_ref[:, block : block + 1], idrep.shape[1:])
    for m in (1, 2, 3):
        high = tall[m]

        @pl.when(z == 0)
        def _():
            @pl.loop(0, across)
            def _(block):
                ext[m][block, 0:high] = jnp.zeros((high, width), BF16)

        @pl.when(z == levels - 1)
        def _():
            @pl.loop(0, across)
            def _(block):
                ext[m][block, high + pair : 2 * high + pair] = jnp.zeros((high, width), BF16)

    for shift in range(-REACH, REACH + 1):
        for block in range(across):
            if 0 <= block - shift < across:
                same = idrep[block, own : own + 48] == idrep[block - shift, own : own + 48]
                colmask[REACH + shift, block] = wide(same.astype(F32), width).astype(BF16)
            else:
                colmask[REACH + shift, block] = jnp.zeros((48, width), BF16)

    for l in range(2):
        for a in range(blocks):
            @pl.loop(0, 2 * cols)
            def _(dev):
                x_copy(l, dev, a).wait()

        spot = pl.multiple_of(lax.rem(l + z_lo, 2) * half, half)
        for chunk in range(xall.shape[1] // 128):
            piece = slice(chunk * 128, (chunk + 1) * 128)
            xt[pl.ds(spot, half), piece] = xall[l, piece, :].astype(F32).T.astype(BF16)

    point_copy.wait()

    @pl.loop(0, wpt.shape[0] // 256)
    def _(n):
        piece = pl.ds(pl.multiple_of(n * 256, 256), 256)
        left = jnp.concatenate([dz_ref[0, a] for a in range(blocks)], axis=0)
        acc[:, piece] = contract_lanes(left, wpt[piece, :])

    def build_shifted(m):
        high = tall[m]

        @pl.loop(0, across)
        def _(block):
            whole = ext[m][block].astype(F32)
            for i in range(3):
                down = (i - 1) * 36 * m
                value = whole[high - down : high - down + pair]
                if i != 1:
                    same = idrep[block, own : own + pair] == idrep[block, own - down : own - down + pair]
                    value = jnp.where(wide(same.astype(F32), width) > 0.0, value, 0.0)
                shifted[i, block] = value.astype(BF16)

    def masked(values, mask):
        count = values.shape[0] // 48
        return jnp.concatenate([values[48 * n : 48 * (n + 1)] * mask for n in range(count)], axis=0)

    def scatter_first(n, part):
        keep[n] = part[:half]
        send1[n] = part[half:].astype(BF16)
        stage1(n).start()

    def stage1(n):
        return pltpu.make_async_remote_copy(
            src_ref=send1.at[n], dst_ref=recv1.at[n], send_sem=s1send.at[n], recv_sem=s1recv.at[n],
            device_id=(r + 2 - 4 * z_lo, c), device_id_type=MESH,
        )

    def stage2(n):
        return pltpu.make_async_remote_copy(
            src_ref=relay.at[n], dst_ref=relay.at[n], send_sem=s2send.at[n], recv_sem=s2recv.at[n],
            device_id=(lax.rem(r + rows // 2, rows), c), device_id_type=MESH,
        )

    def stage3(n, from_x, slot, target):
        piece = dw.at[n, pl.ds(pl.multiple_of(from_x * half, half), half)]
        return pltpu.make_async_remote_copy(
            src_ref=piece, dst_ref=piece, send_sem=s3send.at[slot, n], recv_sem=s3recv.at[from_x, n],
            device_id=target, device_id_type=MESH,
        )

    last = z_hi == k
    beside = (r, 2 * (1 - x) + k)

    def drain2(start, count):
        @pl.loop(start, start + count)
        def _(n):
            stage1(n).wait_recv()
            total = keep[n] + recv1[n].astype(F32)

            @pl.when(last)
            def _():
                keep[n] = total

            @pl.when(jnp.logical_not(last))
            def _():
                relay[n] = total.astype(BF16)
                stage2(n).start()

    def drain3(start, count):
        @pl.when(last)
        def _():
            @pl.loop(start, start + count)
            def _(n):
                stage2(n).wait_recv()
                dw[n, pl.ds(pl.multiple_of(x * half, half), half)] = (keep[n] + relay[n].astype(F32)).astype(BF16)
                stage3(n, x, 0, beside).start()
                stage3(n, x, 1, sibling).start()

    def drain4(start, count):
        @pl.when(last)
        def _():
            @pl.loop(start, start + count)
            def _(n):
                copy = stage3(n, 1 - x, 2, sibling)
                copy.wait_recv()
                copy.start()

        @pl.when(jnp.logical_not(last))
        def _():
            @pl.loop(start, start + count)
            def _(n):
                stage3(n, 0, 0, sibling).wait_recv()
                stage3(n, 1, 0, sibling).wait_recv()

    def weight_grad(m):
        @pl.loop(0, 9)
        def _(tap):
            i, j = tap // 3, lax.rem(tap, 3)
            shift = (j - 1) * m

            @pl.loop(0, across)
            def _(block):
                source = lax.rem(block - shift + across, across)
                gmat[pl.ds(pl.multiple_of(block * pair, 16), pair)] = masked(
                    shifted[i, source], colmask[REACH + shift, block]
                )

            scatter_first((m - 1) * 9 + tap, jnp.dot(xt[...], gmat[...], preferred_element_type=F32))

    def feature_grad(m):
        for i in range(3):
            n = (m - 1) * 3 + i
            slot = n % 2
            for j in range(3):
                shift = (j - 1) * m
                for a in range(blocks):
                    block = c * blocks + a
                    source = lax.rem(block - shift + across, across)
                    gown[a * rb : (a + 1) * rb, j * width : (j + 1) * width] = masked(
                        shifted[i, source, pl.ds(pl.multiple_of(y * rb, 16), rb)], colmask[REACH + shift, block]
                    )
            for j in range(3):
                weight_copy(jnp.int32(n), j).wait()

            @pl.loop(0, wbuf.shape[1] // 256)
            def _(chunk):
                piece = pl.ds(pl.multiple_of(chunk * 256, 256), 256)
                acc[:, piece] += contract_lanes(gown[...], wbuf[slot, piece, :])

            if n + 2 < 9:
                for j in range(3):
                    weight_copy(jnp.int32(n + 2), j).start()

    forward(1)
    start_branch(3)
    start_rims(3)
    finish_gather(1)
    build_shifted(1)
    weight_grad(1)
    forward(2)
    start_branch(0)
    feature_grad(1)
    drain2(0, 9)
    finish_gather(2)
    build_shifted(2)
    weight_grad(2)
    forward(3)
    forward(0)
    feature_grad(2)
    drain3(0, 9)
    drain2(9, 9)
    finish_gather(3)
    build_shifted(3)
    weight_grad(3)
    finish_gather(0)

    @pl.loop(0, across)
    def _(block):
        gmat[pl.ds(pl.multiple_of(block * pair, 16), pair)] = ext0[block]

    scatter_first(27, jnp.dot(xt[...], gmat[...], preferred_element_type=F32))
    drain4(0, 9)
    drain3(9, 9)

    pool_cols.finish()
    pool_rows = Exchange(rows, r, lambda other: (other, c), prbuf, prsend, prrecv)
    prbuf[r] = pool_cols.total()
    pool_rows.start()
    feature_grad(3)
    drain2(18, 10)
    drain4(9, 9)
    pool_rows.finish()
    normed = pooln_ref[...]
    grad = pool_rows.total() * pools_ref[...]
    shift_sum = jnp.sum(grad, axis=0, keepdims=True)
    gain_sum = jnp.sum(grad * normed, axis=0, keepdims=True)
    gain = gain_ref[4:5]
    grad_z = (
        stat_ref[10:11]
        * (grad * gain - gain * shift_sum / image_count - normed * (gain * gain_sum / image_count))
    ).astype(BF16)
    gpool_ref[...] = contract_rows(pooled_ref[...], grad_z)
    gstat_ref[...] = jnp.concatenate([shift_sum, gain_sum] + [jnp.zeros((1, width), F32)] * 6, axis=0)
    own_ids = jnp.concatenate([idrep[c * blocks + a, own : own + pair] for a in range(blocks)], axis=0)
    upper_row = jnp.broadcast_to((y == 0).astype(F32), (pixels, 128))
    own_ids = jnp.where(
        upper_row > 0.0,
        jnp.concatenate([own_ids[a * pair : a * pair + rb] for a in range(blocks)], axis=0),
        jnp.concatenate([own_ids[a * pair + rb : (a + 1) * pair] for a in range(blocks)], axis=0),
    )
    lanes = lax.broadcasted_iota(jnp.int32, (pixels, 128), 1).astype(F32)
    one_hot = (own_ids == lanes).astype(F32).astype(BF16)
    counts = wide(counts_ref[...], 256)

    @pl.loop(0, wpl_ref.shape[0] // 256)
    def _(n):
        piece = pl.ds(pl.multiple_of(n * 256, 256), 256)
        back = contract_lanes(grad_z, wpl_ref[piece, :]) / counts
        back = jnp.concatenate([back, jnp.zeros((128 - images, 256), F32)], axis=0).astype(BF16)
        gx_ref[:, piece] = (acc[:, piece] + jnp.dot(one_hot, back, preferred_element_type=F32)).astype(BF16)

    drain3(18, 10)
    drain4(18, 10)
    result = pltpu.make_async_copy(dw, dw_ref, outsem)
    result.start()

    for m in (1, 2, 3):
        pl.when(sends_rim)(rim_copy(m, True).wait_send)
    for m in (1, 2, 3, 0):
        finish_sends(m)

    @pl.loop(0, 28)
    def _(n):
        stage1(n).wait_send()

        @pl.when(last)
        def _():
            stage3(n, x, 0, beside).wait_send()
            stage3(n, x, 1, sibling).wait_send()
            stage3(n, 1 - x, 2, sibling).wait_send()

        @pl.when(jnp.logical_not(last))
        def _():
            stage2(n).wait_send()

    result.wait()


def backward_call(
    rows, cols, image_count, dz, xsub, ids, wat, wpt, wpl, gain, counts, pooled, pooln, pools, dap, stat
):
    _, blocks, rb, width = dz.shape
    channels = wpt.shape[0]
    share = channels // rows
    pair, across, pixels = 2 * rb, cols * blocks, blocks * rb
    images = dap.shape[0]
    group = pair * across
    vmem = pl.BlockSpec(memory_space=pltpu.VMEM)
    hbm = pl.BlockSpec(memory_space=pl.ANY)
    dma = pltpu.SemaphoreType.DMA
    taps = 28

    def ext(high):
        return pltpu.VMEM((across, 2 * high + pair, width), BF16)

    return pl.pallas_call(
        functools.partial(backward_kernel, rows, cols, float(image_count), rb),
        out_shape=(
            jax.ShapeDtypeStruct((pixels, channels), BF16),
            jax.ShapeDtypeStruct((taps, share, width), BF16),
            jax.ShapeDtypeStruct((share, width), F32),
            jax.ShapeDtypeStruct((8, width), F32),
        ),
        in_specs=[vmem, hbm, vmem, hbm, hbm] + [vmem] * 8,
        out_specs=(vmem, hbm, vmem, vmem),
        scratch_shapes=[
            ext(0), ext(HALO[1]), ext(HALO[2]), ext(HALO[3]),
            pltpu.VMEM((3, across, pair, width), BF16),
            pltpu.VMEM((2 * REACH + 1, across, 48, width), BF16),
            pltpu.VMEM((across, ids.shape[0], 128), F32),
            pltpu.VMEM((group, width), BF16),
            pltpu.VMEM((pixels, 3 * width), BF16),
            pltpu.VMEM((2, group, share // 2), BF16),
            pltpu.VMEM((share, group), BF16),
            pltpu.VMEM((pixels, channels), F32),
            pltpu.VMEM((2, channels, 3 * width), BF16),
            pltpu.VMEM((channels, width), BF16),
            pltpu.VMEM((taps, share // 2, width), BF16),
            pltpu.VMEM((taps, share // 2, width), BF16),
            pltpu.VMEM((taps, share // 2, width), F32),
            pltpu.VMEM((taps, share // 2, width), BF16),
            pltpu.VMEM((taps, share, width), BF16),
            pltpu.VMEM((cols, images, width), F32),
            pltpu.VMEM((rows, images, width), F32),
            dma((2, 2 * cols, blocks)), dma((2, 3)), dma,
            dma((4,)), dma((4,)),
            dma((4, 2, 7)), dma((4, 2, 2 * cols)),
            dma((taps,)), dma((taps,)),
            dma((taps,)), dma((taps,)),
            dma((3, taps)), dma((2, taps)),
            dma((cols,)), dma((cols,)),
            dma((rows,)), dma((rows,)),
            dma,
        ],
        compiler_params=pltpu.CompilerParams(
            collective_id=1, has_side_effects=True, vmem_limit_bytes=64 * 2**20
        ),
        cost_estimate=pl.CostEstimate(flops=4 * pixels * channels * width * 28, bytes_accessed=50_000_000, transcendentals=0),
    )(dz, xsub, ids, wat, wpt, wpl, gain, counts, pooled, pooln, pools, dap, stat)


def extended(cells, sides, width):
    for axis, dim in sides:
        count = lax.axis_size(axis)
        ends = count - 1
        head = lax.slice_in_dim(cells, 0, width, axis=dim)
        tail = lax.slice_in_dim(cells, cells.shape[dim] - width, cells.shape[dim], axis=dim)
        cells = jnp.concatenate(
            [
                lax.ppermute(tail, axis, [(i, (i + 1) % count) for i in range(ends)]),
                cells,
                lax.ppermute(head, axis, [((i + 1) % count, i) for i in range(ends)]),
            ],
            axis=dim,
        )
    return cells


def image_match(window, own_ids, row_start, col_start):
    rows_here, cols_here = own_ids.shape
    section = window[row_start : row_start + rows_here, col_start : col_start + cols_here]
    return (section == own_ids).astype(jnp.float32).reshape(rows_here * cols_here, 1)


def silu_slope(preact_in):
    sigma = jax.nn.sigmoid(preact_in)
    return sigma * (1.0 + preact_in * (1.0 - sigma))


def transposed(left, right):
    return lax.dot_general(
        left, right, (((1,), (1,)), ((), ())), preferred_element_type=jnp.float32
    )


def shards(
    features, image_ids, w_point, w_atrous, w_pool, w_proj, norm_gain, norm_shift, cotangent
):
    rows_here, cols_here, channels = features.shape
    branch_width = w_point.shape[1]
    pixels = rows_here * cols_here
    grid_rows, grid_cols = image_ids.shape
    total_pixels = float(grid_rows * grid_cols)
    image_count = grid_rows // 16 * (grid_cols // 32)
    dilations = (RATE_LOW, RATE_MID, RATE_TOP)
    margin = RATE_TOP
    row_index = lax.axis_index("rows")
    col_index = lax.axis_index("cols")
    id_padded = jnp.pad(image_ids, margin, constant_values=-1)
    window = lax.dynamic_slice(
        id_padded,
        (row_index * rows_here, col_index * cols_here),
        (rows_here + 2 * margin, cols_here + 2 * margin),
    )
    own_ids = window[margin : margin + rows_here, margin : margin + cols_here]
    own_flat = own_ids.reshape(pixels)
    flattened = features.reshape(pixels, channels)
    padded = extended(features, (("rows", 0), ("cols", 1)), margin)
    one_hot = (own_flat[:, None] == jnp.arange(image_count, dtype=jnp.int32)[None, :]).astype(
        jnp.bfloat16
    )
    local_sums = jnp.einsum("pn,pc->nc", one_hot, flattened, preferred_element_type=jnp.float32)
    counts = jax.ops.segment_sum(
        jnp.ones((grid_rows * grid_cols,), jnp.float32), image_ids.reshape(-1), image_count
    )
    image_totals = lax.psum(local_sums, ("rows", "cols"))
    branch_outs = [jnp.dot(flattened, w_point, preferred_element_type=jnp.float32)]
    for branch, dilation in enumerate(dilations):
        running = jnp.zeros((pixels, branch_width), jnp.float32)
        for stencil in range(9):
            row_shift = (stencil // 3 - 1) * dilation
            col_shift = (stencil % 3 - 1) * dilation
            source = padded[
                margin + row_shift : margin + row_shift + rows_here,
                margin + col_shift : margin + col_shift + cols_here,
            ].reshape(pixels, channels)
            same_image = image_match(window, own_ids, margin + row_shift, margin + col_shift)
            running = running + same_image * jnp.dot(
                source, w_atrous[branch, stencil], preferred_element_type=jnp.float32
            )
        branch_outs.append(running)
    spatial = jnp.stack(branch_outs, axis=1)
    first_sum = jnp.sum(spatial, axis=0)
    second_sum = jnp.sum(spatial * spatial, axis=0)
    first_sum, second_sum = lax.psum((first_sum, second_sum), ("rows", "cols"))
    average = first_sum / total_pixels
    inverse_std = lax.rsqrt(second_sum / total_pixels - average * average + epsilon)
    normed = (spatial - average) * inverse_std
    preact = norm_gain[:4] * normed + norm_shift[:4]
    active = jax.nn.silu(preact).astype(jnp.bfloat16)
    pooled = (image_totals / counts[:, None]).astype(jnp.bfloat16)
    pool_z = jnp.dot(pooled, w_pool, preferred_element_type=jnp.float32)
    pool_avg = jnp.mean(pool_z, axis=0)
    pool_square = jnp.mean(pool_z * pool_z, axis=0)
    pool_inverse = lax.rsqrt(pool_square - pool_avg * pool_avg + epsilon)
    pool_normed = (pool_z - pool_avg) * pool_inverse
    pool_pre = norm_gain[4] * pool_normed + norm_shift[4]
    pool_active = jax.nn.silu(pool_pre).astype(jnp.bfloat16)
    joined = jnp.concatenate(
        [active.reshape(pixels, 4 * branch_width), jnp.take(pool_active, own_flat, axis=0)], axis=1
    )
    final_z = jnp.dot(joined, w_proj, preferred_element_type=jnp.float32)
    final_first, final_second = lax.psum(
        (jnp.sum(final_z, axis=0), jnp.sum(final_z * final_z, axis=0)), ("rows", "cols")
    )
    final_avg = final_first / total_pixels
    final_inverse = lax.rsqrt(final_second / total_pixels - final_avg * final_avg + epsilon)
    final_normed = (final_z - final_avg) * final_inverse
    final_pre = norm_gain[5] * final_normed + norm_shift[5]
    output = jax.nn.silu(final_pre).astype(jnp.bfloat16).reshape(rows_here, cols_here, branch_width)
    upstream = cotangent.reshape(pixels, branch_width).astype(jnp.float32)
    grad_final = upstream * silu_slope(final_pre)
    shift_last, gain_last = lax.psum(
        (jnp.sum(grad_final, axis=0), jnp.sum(grad_final * final_normed, axis=0)), ("rows", "cols")
    )
    grad_final_z = (
        final_inverse
        * (
            grad_final * norm_gain[5]
            - norm_gain[5] * shift_last / total_pixels
            - final_normed * (norm_gain[5] * gain_last / total_pixels)
        )
    ).astype(jnp.bfloat16)
    proj_term = jnp.einsum("pk,pc->kc", joined, grad_final_z, preferred_element_type=jnp.float32)
    grad_joined = transposed(grad_final_z, w_proj)
    grad_pre = grad_joined[:, : 4 * branch_width].reshape(pixels, 4, branch_width) * silu_slope(
        preact
    )
    grad_pixel = grad_joined[:, 4 * branch_width :]
    shift_sums = jnp.sum(grad_pre, axis=0)
    gain_sums = jnp.sum(grad_pre * normed, axis=0)
    image_grads = jax.ops.segment_sum(grad_pixel, own_flat, image_count)
    shift_sums, gain_sums, image_grads = lax.psum(
        (shift_sums, gain_sums, image_grads), ("rows", "cols")
    )
    grad_branch = (
        inverse_std
        * (
            grad_pre * norm_gain[:4]
            - norm_gain[:4] * shift_sums / total_pixels
            - normed * (norm_gain[:4] * gain_sums / total_pixels)
        )
    ).astype(jnp.bfloat16)
    grad_pool_pre = image_grads * silu_slope(pool_pre)
    pool_shift = jnp.sum(grad_pool_pre, axis=0)
    pool_gain = jnp.sum(grad_pool_pre * pool_normed, axis=0)
    grad_pool_z = (
        pool_inverse
        * (
            grad_pool_pre * norm_gain[4]
            - norm_gain[4] * pool_shift / image_count
            - pool_normed * (norm_gain[4] * pool_gain / image_count)
        )
    ).astype(jnp.bfloat16)
    row_share = channels // lax.axis_size("rows")
    pool_columns = lax.dynamic_slice_in_dim(pooled, row_index * row_share, row_share, 1)
    grad_pool = jnp.einsum(
        "nk,nc->kc", pool_columns, grad_pool_z, preferred_element_type=jnp.float32
    )
    grad_pooled = transposed(grad_pool_z, w_pool) / counts[:, None]
    grad_input = jnp.take(grad_pooled, own_flat, axis=0) + transposed(grad_branch[:, 0], w_point)
    point_term = jnp.einsum(
        "pk,pc->kc", flattened, grad_branch[:, 0], preferred_element_type=jnp.float32
    )
    stacked = grad_branch[:, 1:].reshape(rows_here, cols_here, 3 * branch_width)
    grad_padded = extended(stacked, (("rows", 0), ("cols", 1)), margin)
    rim_list = [
        grad_padded[:, :, branch * branch_width : (branch + 1) * branch_width]
        for branch in range(3)
    ]
    rim_bases = [margin, margin, margin]
    atrous_terms = []
    for branch, dilation in enumerate(dilations):
        tap_terms = []
        rim_base = rim_bases[branch]
        for stencil in range(9):
            row_shift = (stencil // 3 - 1) * dilation
            col_shift = (stencil % 3 - 1) * dilation
            source = padded[
                margin + row_shift : margin + row_shift + rows_here,
                margin + col_shift : margin + col_shift + cols_here,
            ].reshape(pixels, channels)
            same_image = image_match(window, own_ids, margin + row_shift, margin + col_shift)
            masked = same_image.astype(jnp.bfloat16) * grad_branch[:, branch + 1]
            tap_terms.append(
                jnp.einsum("pk,pc->kc", source, masked, preferred_element_type=jnp.float32)
            )
            incoming = rim_list[branch][
                rim_base - row_shift : rim_base - row_shift + rows_here,
                rim_base - col_shift : rim_base - col_shift + cols_here,
            ].reshape(pixels, branch_width)
            back_image = image_match(window, own_ids, margin - row_shift, margin - col_shift)
            grad_input = grad_input + back_image * transposed(incoming, w_atrous[branch, stencil])
        atrous_terms.append(jnp.stack(tap_terms))
    atrous_term = jnp.stack(atrous_terms)
    shared = (
        lax.psum_scatter(
            point_term.astype(jnp.bfloat16), "rows", scatter_dimension=0, tiled=True
        ).astype(jnp.float32),
        lax.psum_scatter(
            atrous_term.astype(jnp.bfloat16), "rows", scatter_dimension=2, tiled=True
        ).astype(jnp.float32),
        lax.psum_scatter(
            proj_term.astype(jnp.bfloat16), "rows", scatter_dimension=0, tiled=True
        ).astype(jnp.float32),
    )
    shared = (
        lax.psum(shared[0].astype(jnp.bfloat16), "cols").astype(jnp.float32),
        lax.psum(shared[1].astype(jnp.bfloat16), "cols").astype(jnp.float32),
        lax.psum(shared[2].astype(jnp.bfloat16), "cols").astype(jnp.float32),
    )
    grad_gain = jnp.concatenate([gain_sums, pool_gain[None], gain_last[None]], axis=0)
    grad_shift = jnp.concatenate([shift_sums, pool_shift[None], shift_last[None]], axis=0)
    grad_features = grad_input.astype(jnp.bfloat16).reshape(rows_here, cols_here, channels)
    return (
        output,
        grad_features,
        shared[0],
        shared[1],
        grad_pool,
        shared[2],
        grad_gain,
        grad_shift,
    )


def to_blocks(cells):
    height, breadth, depth = cells.shape
    cells = cells.reshape(height, breadth // STEP, STEP, depth)
    return cells.transpose(1, 0, 2, 3).reshape(height * breadth, depth)


def from_blocks(cells, height, breadth):
    depth = cells.shape[-1]
    cells = cells.reshape(breadth // STEP, height, STEP, depth)
    return cells.transpose(1, 0, 2, 3).reshape(height, breadth, depth)


def id_columns(ids):
    height, breadth = ids.shape
    table = ids.reshape(height, breadth // STEP, STEP).transpose(0, 2, 1).reshape(height * STEP, breadth // STEP)
    return jnp.pad(table.astype(F32), ((0, 0), (0, 128 - breadth // STEP)))


def quick_shards(
    features, image_ids, w_point, w_atrous, w_pool, w_proj, norm_gain, norm_shift, cotangent
):
    rows_here, cols_here, channels = features.shape
    branch_width = w_point.shape[1]
    pixels = rows_here * cols_here
    grid_rows, grid_cols = image_ids.shape
    image_count = grid_rows // 16 * (grid_cols // 32)
    images = -(-image_count // 16) * 16
    margin = RATE_TOP
    rows, cols = lax.axis_size("rows"), lax.axis_size("cols")
    row_index = lax.axis_index("rows")
    col_index = lax.axis_index("cols")
    id_padded = jnp.pad(image_ids, margin, constant_values=-1)
    window = lax.dynamic_slice(
        id_padded,
        (row_index * rows_here, col_index * cols_here),
        (rows_here + 2 * margin, cols_here + 2 * margin),
    )
    own_ids = window[margin : margin + rows_here, margin : margin + cols_here]
    own_flat = own_ids.reshape(pixels)
    counts = jnp.sum(
        (image_ids.reshape(-1, 1) == jnp.arange(images, dtype=jnp.int32)[None, :]).astype(F32), axis=0
    )
    counts = jnp.maximum(counts, 1.0)
    count_table = jnp.broadcast_to(counts[:, None], (images, 128))
    x = to_blocks(features)
    cot = to_blocks(cotangent)
    output, dz, proj_term, stats, pooled, pool_normed, pool_slope, dap, xsub = forward_call(
        rows, cols, image_count, x, id_columns(window), w_atrous, w_point, w_pool, w_proj,
        norm_gain, norm_shift, cot, count_table,
    )
    output = from_blocks(output, rows_here, cols_here)
    pair_window = lax.dynamic_slice(
        id_padded,
        (row_index // 2 * (2 * rows_here), jnp.int32(margin)),
        (2 * rows_here + 2 * margin, grid_cols),
    )
    grad_input, weights, grad_pool, pool_sums = backward_call(
        rows, cols, image_count, dz, xsub.reshape(2, 8, 4, pixels // 4, -1), id_columns(pair_window), w_atrous, w_point, w_pool,
        norm_gain, count_table, pooled, pool_normed, pool_slope, dap, stats,
    )
    weights = weights.astype(F32)
    grad_atrous = weights[:27].reshape(3, 9, channels // rows, branch_width)

    def shared(term, dim):
        part = lax.psum_scatter(term.astype(BF16), "rows", scatter_dimension=dim, tiled=True)
        return lax.psum(part, "cols").astype(F32)

    grad_gain = jnp.concatenate([stats[4:8], pool_sums[1:2], stats[9:10]], axis=0)
    grad_shift = jnp.concatenate([stats[0:4], pool_sums[0:1], stats[8:9]], axis=0)
    grad_features = from_blocks(grad_input, rows_here, cols_here)
    return (
        output, grad_features, weights[27], grad_atrous, grad_pool,
        shared(proj_term, 0), grad_gain, grad_shift,
    )


def solution(mesh):
    placed = (P("rows", "cols", None), P(), P(), P(), P(), P(), P(), P(), P("rows", "cols", None))
    quick = mesh.shape["rows"] == 8 and mesh.shape["cols"] == 4
    return jax.shard_map(
        quick_shards if quick else shards,
        mesh=mesh,
        in_specs=placed,
        out_specs=(
            P("rows", "cols", None),
            P("rows", "cols", None),
            P("rows", None),
            P(None, None, "rows", None),
            P("rows", None),
            P("rows", None),
            P(),
            P(),
        ),
        check_vma=False,
    )
```

```python
import functools
import jax
import jax.numpy as jnp
import numpy as np
from jax import lax
from jax.experimental import pallas as pl
from jax.experimental.pallas import tpu as pltpu
from jax.sharding import PartitionSpec as P

MESH = pl.DeviceIdType.MESH
RATE_LOW = 6
RATE_MID = 12
RATE_TOP = 18
STEP = RATE_LOW
REACH = RATE_TOP // STEP
HALO = {1: 48, 2: 80, 3: 112}
SLOTS = 4
epsilon = 1e-05
F32 = jnp.float32
BF16 = jnp.bfloat16


def wide(column, width):
    return jnp.concatenate([column] * (width // column.shape[-1]), axis=-1)


def silu_parts(preact):
    sigma = jax.nn.sigmoid(preact)
    return preact * sigma, sigma * (1.0 + preact * (1.0 - sigma))


def contract_rows(left, right):
    return lax.dot_general(left, right, (((0,), (0,)), ((), ())), preferred_element_type=F32)


def contract_lanes(left, right):
    return lax.dot_general(left, right, (((1,), (1,)), ((), ())), preferred_element_type=F32)


def greet_all(rows, cols, r, c):
    barrier = pltpu.get_barrier_semaphore()
    for dr in range(rows):
        for dc in range(cols):
            if dr or dc:
                other = (lax.rem(r + dr, rows), lax.rem(c + dc, cols))
                pl.semaphore_signal(barrier, inc=1, device_id=other, device_id_type=MESH)
    pl.semaphore_wait(barrier, rows * cols - 1)


class Exchange:
    def __init__(self, axis_size, place, to_device, slots, send_sems, recv_sems):
        self.size, self.place, self.to_device = axis_size, place, to_device
        self.slots, self.send_sems, self.recv_sems = slots, send_sems, recv_sems

    def copy(self, step, source=None):
        other = lax.rem(self.place + step, self.size)
        mine = self.slots.at[self.place]
        return pltpu.make_async_remote_copy(
            src_ref=mine if source is None else source(other),
            dst_ref=mine,
            send_sem=self.send_sems.at[step],
            recv_sem=self.recv_sems.at[self.place],
            device_id=self.to_device(other),
            device_id_type=MESH,
        )

    def start(self, source=None):
        for step in range(1, self.size):
            self.copy(step, source).start()

    def arrive(self):
        for step in range(1, self.size):
            other = lax.rem(self.place + step, self.size)
            there = self.slots.at[other]
            pltpu.make_async_remote_copy(
                src_ref=there,
                dst_ref=there,
                send_sem=self.send_sems.at[step],
                recv_sem=self.recv_sems.at[other],
                device_id=self.to_device(other),
                device_id_type=MESH,
            ).wait_recv()

    def leave(self, source=None):
        for step in range(1, self.size):
            self.copy(step, source).wait_send()

    def total(self):
        value = self.slots[0]
        for other in range(1, self.size):
            value = value + self.slots[other]
        return value


def forward_kernel(
    rows, cols, image_count, total_pixels,
    raw_ref, order_ref, back_ref, ids_ref, wat_ref, wpt_ref, wpl_ref, wpj_ref, gain_ref, shift_ref, cot_ref,
    counts_ref, out_ref, dz_ref, pj_ref, stat_ref, pooled_ref, pooln_ref, pools_ref, dap_ref, xsub_ref,
    x_ref, idrep, wbuf, wplbuf, ubuf, zx1, zx2, zx3, zs1, zs2, zs3,
    halo_bufs, zn, slope, joined, zf, dzf, active, isum, cbuf, rbuf, pr_buf, pc_buf, pz_buf,
    wsem, wplsem, hsend, hrecv, csend, crecv, rsend, rrecv, psend, precv, pcsend, pcrecv, pzsend, pzrecv,
    xsend, xrecv,
):
    r, c = lax.axis_index("rows"), lax.axis_index("cols")
    blocks, rb, width = zn.shape[1], zn.shape[2], zn.shape[3]
    pixels = blocks * rb
    own = REACH * 36
    images = isum.shape[0]
    zx, zs = {1: zx1, 2: zx2, 3: zx3}, {1: zs1, 2: zs2, 3: zs3}
    order = (3, 2, 1)
    taps = 27

    def weight_copy(n):
        branch, tap = 2 - n // 9, lax.rem(n, 9)
        slot = lax.rem(n, SLOTS)
        return pltpu.make_async_copy(wat_ref.at[branch, tap], wbuf.at[slot], wsem.at[slot])

    for n in range(SLOTS - 1):
        weight_copy(jnp.int32(n)).start()
    share = x_ref.shape[1] // rows
    pool_weight = pltpu.make_async_copy(
        wpl_ref.at[pl.ds(pl.multiple_of(r * share, share), share)], wplbuf, wplsem
    )
    pool_weight.start()
    for block in range(idrep.shape[0]):
        idrep[block] = jnp.broadcast_to(ids_ref[:, block : block + 1], idrep.shape[1:])
    greet_all(rows, cols, r, c)

    @pl.loop(0, x_ref.shape[1] // 256)
    def _(n):
        piece = pl.ds(pl.multiple_of(n * 256, 256), 256)
        x_ref[:, piece] = jnp.dot(order_ref[...], raw_ref[:, piece], preferred_element_type=F32).astype(BF16)

    own_ids = jnp.concatenate([idrep[REACH + a, own : own + rb, :] for a in range(blocks)], axis=0)
    lanes = lax.broadcasted_iota(jnp.int32, (pixels, 128), 1).astype(F32)
    one_hot = jnp.concatenate(
        [(own_ids == lanes + 128.0 * part).astype(F32).astype(BF16) for part in range(pl.cdiv(images, 128))],
        axis=1,
    )
    for part in range(rows):
        piece = slice(part * share, (part + 1) * share)
        isum[:, piece] = contract_rows(one_hot, x_ref[:, piece])[:images]
    pool_rows = Exchange(rows, r, lambda other: (other, c), pr_buf, psend, precv)

    def share_of(other):
        return isum.at[:, pl.ds(pl.multiple_of(other * share, share), share)]

    pr_buf[r] = isum[:, pl.ds(pl.multiple_of(r * share, share), share)]
    pool_rows.start(share_of)

    def halo_copies(m):
        height = HALO[m]
        a_range = {-1: (0, m), 0: (m, blocks), 1: (m + blocks, m)}
        r_range = {-1: (0, height), 0: (height, rb), 1: (height + rb, height)}
        copies = []
        for place, (dr, dc) in enumerate(DIRECTIONS):
            a0, na = a_range[dc]
            r0, nr = r_range[dr]
            copies.append(
                (
                    dr,
                    dc,
                    pltpu.make_async_remote_copy(
                        src_ref=zs[m].at[pl.ds(a0, na), pl.ds(r0, nr)],
                        dst_ref=halo_bufs[(m - 1) * 8 + place],
                        send_sem=hsend.at[m - 1, place],
                        recv_sem=hrecv.at[m - 1, place],
                        device_id=(lax.rem(r + dr + rows, rows), lax.rem(c + dc + cols, cols)),
                        device_id_type=MESH,
                    ),
                )
            )
        return copies

    def inside(dr, dc):
        return (r + dr >= 0) & (r + dr < rows) & (c + dc >= 0) & (c + dc < cols)

    def conv(position, m):
        height = HALO[m]

        @pl.loop(0, blocks + 2 * m)
        def _(block):
            zx[m][block] = jnp.zeros(zx[m].shape[1:], F32)

        for i in range(3):
            @pl.loop(0, blocks + 2 * m)
            def _(block):
                ubuf[block] = jnp.zeros(ubuf.shape[1:], F32)

            @pl.loop(0, 3)
            def _(j):
                n = position * 9 + 3 * i + j
                slot = lax.rem(n, SLOTS)
                ahead = n + SLOTS - 1

                @pl.when(ahead < taps)
                def _():
                    weight_copy(ahead).start()

                weight_copy(n).wait()
                product = jnp.dot(x_ref[...], wbuf[slot], preferred_element_type=F32)
                for a in range(blocks):
                    same = idrep[REACH + a, own : own + rb] == idrep[REACH + a - (j - 1) * m, own : own + rb]
                    part = product[a * rb : (a + 1) * rb]
                    ubuf[a + (2 - j) * m] += jnp.where(wide(same.astype(F32), width) > 0.0, part, 0.0)

            up = (i - 1) * 36 * m

            @pl.loop(0, blocks + 2 * m)
            def _(block):
                value = ubuf[block]
                if i != 1:
                    here = REACH - m + block
                    same = idrep[here, own : own + rb] == idrep[here, own - up : own - up + rb]
                    value = jnp.where(wide(same.astype(F32), width) > 0.0, value, 0.0)
                zx[m][block, height - up : height - up + rb] += value

        @pl.loop(0, blocks + 2 * m)
        def _(block):
            zs[m][block] = zx[m][block].astype(BF16)

        for dr, dc, copy in halo_copies(m):
            pl.when(inside(dr, dc))(copy.start)

        @pl.loop(0, blocks)
        def _(a):
            zn[m, a] = zx[m][m + a, height : height + rb]


    members = [(dy, dx, dk) for dy in range(2) for dx in range(2) for dk in range(2)]
    half = share // 2

    def channel_slices(y, x, k):
        return [pl.multiple_of((2 * (2 * k + l) + y) * share + x * half, 128) for l in range(2)]

    def member_copies():
        mine = lax.rem(r, 2) * cols + c
        copies = []
        for step, (dy, dx, dk) in enumerate(members):
            y, x, k = lax.rem(r + dy, 2), lax.rem(c // 2 + dx, 2), lax.rem(c + dk, 2)
            for l, start in enumerate(channel_slices(y, x, k)):
                source = x_ref.at[:, pl.ds(start, half)]
                target = xsub_ref.at[l, mine]
                if step == 0:
                    copies.append(pltpu.make_async_copy(source, target, xrecv.at[l, mine]))
                else:
                    copies.append(
                        pltpu.make_async_remote_copy(
                            src_ref=source,
                            dst_ref=target,
                            send_sem=xsend.at[l, step],
                            recv_sem=xrecv.at[l, mine],
                            device_id=(2 * (r // 2) + y, 2 * x + k),
                            device_id_type=MESH,
                        )
                    )
        return copies

    pool_cols = Exchange(cols, c, lambda other: (r, other), pc_buf, pcsend, pcrecv)
    pool_z = Exchange(rows, r, lambda other: (other, c), pz_buf, pzsend, pzrecv)
    conv(0, 3)
    pool_rows.arrive()
    pc_buf[c] = pool_rows.total()
    pool_cols.start()
    conv(1, 2)
    pool_cols.arrive()
    counts = counts_ref[...]
    pooled = (pool_cols.total() / wide(counts, share)).astype(BF16)
    pooled_ref[...] = pooled
    pool_weight.wait()
    pz_buf[r] = jnp.dot(pooled, wplbuf[...], preferred_element_type=F32)
    pool_z.start()
    conv(2, 1)
    product = jnp.dot(x_ref[...], wpt_ref[...], preferred_element_type=F32)
    for a in range(blocks):
        zn[0, a] = product[a * rb : (a + 1) * rb]
    for copy in member_copies():
        copy.start()
    pool_z.arrive()
    zp = pool_z.total()
    pool_avg = jnp.sum(zp, axis=0, keepdims=True) / image_count
    pool_square = jnp.sum(zp * zp, axis=0, keepdims=True) / image_count
    pool_inverse = lax.rsqrt(pool_square - pool_avg * pool_avg + epsilon)
    pool_normed = (zp - pool_avg) * pool_inverse
    pool_active, pool_slope = silu_parts(gain_ref[4:5] * pool_normed + shift_ref[4:5])
    pooln_ref[...] = pool_normed
    pools_ref[...] = pool_slope
    spare = one_hot.shape[1] - images
    pool_active = jnp.concatenate([pool_active, jnp.zeros((spare, width), F32)], axis=0).astype(BF16)
    joined[:, 4 * width : 5 * width] = jnp.dot(one_hot, pool_active, preferred_element_type=F32).astype(BF16)

    for m in order:
        height = HALO[m]
        a_range = {-1: (blocks - m, m), 0: (0, blocks), 1: (0, m)}
        r_range = {-1: (rb - height, height), 0: (0, rb), 1: (0, height)}
        for place, (dr, dc, copy) in enumerate(halo_copies(m)):
            a0, na = a_range[dc]
            r0, nr = r_range[dr]

            @pl.when(inside(-dr, -dc))
            def _():
                copy.wait_recv()
                for a in range(na):
                    zn[m, a0 + a, r0 : r0 + nr] += halo_bufs[(m - 1) * 8 + place][a].astype(F32)

    started = []

    def all_sum(step, value):
        across = Exchange(cols, c, lambda other: (r, other), cbuf.at[step], csend.at[step], crecv.at[step])
        cbuf[step, c] = value
        across.start()
        across.arrive()
        down = Exchange(rows, r, lambda other: (other, c), rbuf.at[step], rsend.at[step], rrecv.at[step])
        rbuf[step, r] = across.total()
        down.start()
        down.arrive()
        started.extend((across, down))
        return down.total()

    zero = jnp.zeros((1, width), F32)

    def row_sum(value):
        return jnp.sum(value, axis=0, keepdims=True)

    firsts, seconds = [], []
    for k in range(4):
        first, second = zero, zero
        for a in range(blocks):
            value = zn[k, a]
            first, second = first + row_sum(value), second + row_sum(value * value)
        firsts.append(first)
        seconds.append(second)
    moments = all_sum(0, jnp.concatenate(firsts + seconds, axis=0))
    average = moments[0:4] / total_pixels
    inverse = lax.rsqrt(moments[4:8] / total_pixels - average * average + epsilon)
    for k in range(4):
        @pl.loop(0, blocks)
        def _(a):
            normed = (zn[k, a] - average[k : k + 1]) * inverse[k : k + 1]
            value, slant = silu_parts(gain_ref[k : k + 1] * normed + shift_ref[k : k + 1])
            zn[k, a] = normed
            slope[k, a] = slant
            joined[pl.ds(pl.multiple_of(a * rb, rb), rb), k * width : (k + 1) * width] = value.astype(BF16)

    zf[...] = jnp.dot(joined[...], wpj_ref[...], preferred_element_type=F32)
    first, second = zero, zero
    for a in range(blocks):
        value = zf[a * rb : (a + 1) * rb]
        first, second = first + row_sum(value), second + row_sum(value * value)
    moments = all_sum(1, jnp.concatenate([first, second] + [zero] * 6, axis=0))
    final_avg = moments[0:1] / total_pixels
    final_inverse = lax.rsqrt(moments[1:2] / total_pixels - final_avg * final_avg + epsilon)
    shift_last, gain_last = zero, zero
    upstream = jnp.dot(order_ref[...], cot_ref[...], preferred_element_type=F32)
    for a in range(blocks):
        piece = slice(a * rb, (a + 1) * rb)
        normed = (zf[piece] - final_avg) * final_inverse
        result, slant = silu_parts(gain_ref[5:6] * normed + shift_ref[5:6])
        active[piece] = result.astype(BF16)
        grad = upstream[piece] * slant
        zf[piece] = normed
        dzf[piece] = grad
        shift_last, gain_last = shift_last + row_sum(grad), gain_last + row_sum(grad * normed)
    out_ref[...] = jnp.dot(back_ref[...], active[...], preferred_element_type=F32).astype(BF16)
    sums = all_sum(2, jnp.concatenate([shift_last, gain_last] + [zero] * 6, axis=0))
    shift_last, gain_last = sums[0:1], sums[1:2]
    gain = gain_ref[5:6]
    for a in range(blocks):
        piece = slice(a * rb, (a + 1) * rb)
        dzf[piece] = final_inverse * (
            dzf[piece] * gain
            - gain * shift_last / total_pixels
            - zf[piece] * (gain * gain_last / total_pixels)
        )
    grad_final = dzf[...].astype(BF16)

    shifts, gains = [], []
    for k in range(4):
        grad = contract_lanes(grad_final, wpj_ref[k * width : (k + 1) * width])
        shift_sum, gain_sum = zero, zero
        for a in range(blocks):
            part = grad[a * rb : (a + 1) * rb] * slope[k, a]
            slope[k, a] = part
            shift_sum, gain_sum = shift_sum + row_sum(part), gain_sum + row_sum(part * zn[k, a])
        shifts.append(shift_sum)
        gains.append(gain_sum)
    grad_pixel = contract_lanes(grad_final, wpj_ref[4 * width : 5 * width])
    upper = grad_pixel.astype(BF16)
    lower = (grad_pixel - upper.astype(F32)).astype(BF16)
    dap_ref[...] = (contract_rows(one_hot, upper) + contract_rows(one_hot, lower))[:images]
    sums = all_sum(3, jnp.concatenate(shifts + gains, axis=0))
    for k in range(4):
        gain = gain_ref[k : k + 1]
        from_shift = gain * sums[k : k + 1] / total_pixels
        from_gain = gain * sums[4 + k : 5 + k] / total_pixels

        @pl.loop(0, blocks)
        def _(a):
            dz_ref[k, a] = (
                inverse[k : k + 1] * (slope[k, a] * gain - from_shift - zn[k, a] * from_gain)
            ).astype(BF16)

    for k in range(5):
        piece = slice(k * width, (k + 1) * width)
        pj_ref[piece] = contract_rows(joined[:, piece], grad_final).astype(BF16)
    stat_ref[...] = jnp.concatenate([sums, shift_last, gain_last, pool_inverse] + [zero] * 5, axis=0)

    pool_rows.leave(share_of)
    for exchange in (pool_cols, pool_z, *started):
        exchange.leave()
    for m in order:
        for dr, dc, copy in halo_copies(m):
            pl.when(inside(dr, dc))(copy.wait_send)
    for step, copy in enumerate(member_copies()):
        if step < 2:
            copy.wait()
        else:
            copy.wait_send()
    for l in range(2):
        for step, (dy, dx, dk) in enumerate(members):
            if step:
                y, x, k = lax.rem(r + dy, 2), lax.rem(c // 2 + dx, 2), lax.rem(c + dk, 2)
                there = xsub_ref.at[l, y * cols + 2 * x + k]
                pltpu.make_async_remote_copy(
                    src_ref=there,
                    dst_ref=there,
                    send_sem=xsend.at[l, step],
                    recv_sem=xrecv.at[l, y * cols + 2 * x + k],
                    device_id=(2 * (r // 2) + y, 2 * x + k),
                    device_id_type=MESH,
                ).wait_recv()


DIRECTIONS = ((-1, 0), (1, 0), (-1, -1), (-1, 1), (1, -1), (1, 1), (0, -1), (0, 1))


def forward_call(rows, cols, image_count, x, order, back, ids, wat, wpt, wpl, wpj, gain, shift, cot, counts):
    pixels, channels = x.shape
    width = wpt.shape[1]
    blocks, rb = 4, pixels // 4
    images = counts.shape[0]
    share = channels // rows
    total_pixels = float(pixels * rows * cols)
    vmem = pl.BlockSpec(memory_space=pltpu.VMEM)
    hbm = pl.BlockSpec(memory_space=pl.ANY)

    def ext(m, kind):
        return pltpu.VMEM((blocks + 2 * m, 2 * HALO[m] + rb, width), kind)

    halo_bufs = []
    for m in (1, 2, 3):
        for dr, dc in DIRECTIONS:
            halo_bufs.append(pltpu.VMEM((m if dc else blocks, HALO[m] if dr else rb, width), BF16))
    dma = pltpu.SemaphoreType.DMA
    return pl.pallas_call(
        functools.partial(forward_kernel, rows, cols, float(image_count), total_pixels),
        out_shape=(
            jax.ShapeDtypeStruct((pixels, width), BF16),
            jax.ShapeDtypeStruct((4, blocks, rb, width), BF16),
            jax.ShapeDtypeStruct((5 * width, width), BF16),
            jax.ShapeDtypeStruct((16, width), F32),
            jax.ShapeDtypeStruct((images, share), BF16),
            jax.ShapeDtypeStruct((images, width), F32),
            jax.ShapeDtypeStruct((images, width), F32),
            jax.ShapeDtypeStruct((images, width), F32),
            jax.ShapeDtypeStruct((2, 8, pixels, share // 2), BF16),
        ),
        in_specs=[vmem, vmem, vmem, vmem, hbm, vmem, hbm, vmem, vmem, vmem, vmem, vmem],
        out_specs=(vmem,) * 8 + (hbm,),
        scratch_shapes=[
            pltpu.VMEM((pixels, channels), BF16),
            pltpu.VMEM((blocks + 2 * REACH, ids.shape[0], 128), F32),
            pltpu.VMEM((SLOTS, channels, width), BF16),
            pltpu.VMEM((share, width), BF16),
            pltpu.VMEM((blocks + 2 * REACH, rb, width), F32),
            ext(1, F32), ext(2, F32), ext(3, F32),
            ext(1, BF16), ext(2, BF16), ext(3, BF16),
            halo_bufs,
            pltpu.VMEM((4, blocks, rb, width), F32),
            pltpu.VMEM((4, blocks, rb, width), F32),
            pltpu.VMEM((pixels, 5 * width), BF16),
            pltpu.VMEM((pixels, width), F32),
            pltpu.VMEM((pixels, width), F32),
            pltpu.VMEM((pixels, width), BF16),
            pltpu.VMEM((images, channels), F32),
            pltpu.VMEM((4, cols, 8, width), F32),
            pltpu.VMEM((4, rows, 8, width), F32),
            pltpu.VMEM((rows, images, share), F32),
            pltpu.VMEM((cols, images, share), F32),
            pltpu.VMEM((rows, images, width), F32),
            dma((SLOTS,)), dma,
            dma((3, 8)), dma((3, 8)),
            dma((4, cols)), dma((4, cols)),
            dma((4, rows)), dma((4, rows)),
            dma((rows,)), dma((rows,)),
            dma((cols,)), dma((cols,)),
            dma((rows,)), dma((rows,)),
            dma((2, 8)), dma((2, 8)),
        ],
        compiler_params=pltpu.CompilerParams(
            collective_id=0, has_side_effects=True, vmem_limit_bytes=60 * 2**20
        ),
        cost_estimate=pl.CostEstimate(flops=2 * pixels * channels * width * 28, bytes_accessed=40_000_000, transcendentals=0),
    )(x, order, back, ids, wat, wpt, wpl, wpj, gain, shift, cot, counts)


def backward_kernel(
    rows, cols, image_count, height,
    dz_ref, xsub_ref, ids_ref, wat_ref, wpt_ref, wpl_ref, gain_ref, counts_ref,
    pooled_ref, pooln_ref, pools_ref, dap_ref, stat_ref, back_ref,
    gx_ref, dw_ref, dpoint_ref, gpool_ref, gstat_ref,
    ext0, ext1, ext2, ext3, shifted, colmask, idrep, gmat, gown, xall, xt, acc, wbuf, wpt,
    send1, recv1, keep, relay, dw, pcbuf, prbuf,
    xsem, wsem, wptsem, zsend, zrecv, agsend, agrecv, s1send, s1recv, s2send, s2recv, s3send, s3recv,
    pcsend, pcrecv, prsend, prrecv, outsem,
):
    r, c = lax.axis_index("rows"), lax.axis_index("cols")
    z, y = r // 2, lax.rem(r, 2)
    x, k = c // 2, lax.rem(c, 2)
    levels = rows // 2
    z_lo, z_hi = lax.rem(z, 2), z // 2
    blocks, rb, width = dz_ref.shape[1:]
    pair = 2 * rb
    across = cols * blocks
    pixels = blocks * rb
    own = REACH * 36
    half = xt.shape[0] // 2
    images = dap_ref.shape[0]
    ext = {0: ext0, 1: ext1, 2: ext2, 3: ext3}
    tall = {0: 0, **HALO}

    def x_copy(l, dev, a):
        dev_y, dev_c = dev // cols, lax.rem(dev, cols)
        start = pl.multiple_of((dev_c * blocks + a) * pair + dev_y * rb, 16)
        return pltpu.make_async_copy(
            xsub_ref.at[l, dev, a], xall.at[l, pl.ds(start, rb)], xsem.at[l, dev, a]
        )

    for l in range(2):
        for a in range(blocks):
            @pl.loop(0, 2 * cols)
            def _(dev):
                x_copy(l, dev, a).start()

    def weight_copy(n, j):
        branch, i = n // 3, lax.rem(n, 3)
        slot = lax.rem(n, 2)
        return pltpu.make_async_copy(
            wat_ref.at[branch, 3 * i + j],
            wbuf.at[slot, :, pl.ds(j * width, width)],
            wsem.at[slot, j],
        )

    point_copy = pltpu.make_async_copy(wpt_ref, wpt, wptsem)
    point_copy.start()
    for n in range(2):
        for j in range(3):
            weight_copy(jnp.int32(n), j).start()

    greet_all(rows, cols, r, c)

    def has_rim(dev_y):
        return (dev_y == 1) & (z >= 1) | (dev_y == 0) & (z <= levels - 2)

    def rim_copy(m, sending):
        high = tall[m]
        start = pl.multiple_of(y * (rb - high), 16)
        target = pl.multiple_of((1 - y) * (high + pair), 16)
        return pltpu.make_async_remote_copy(
            src_ref=dz_ref.at[m, :, pl.ds(start, high)],
            dst_ref=ext[m].at[pl.ds(c * blocks, blocks), pl.ds(target, high)],
            send_sem=zsend.at[m],
            recv_sem=zrecv.at[m],
            device_id=(lax.rem(r + 4 * y - 2 + rows, rows), c),
            device_id_type=MESH,
        )

    sends_rim = (y == 1) & (z <= levels - 2) | (y == 0) & (z >= 1)

    def item(m, kind, dev_y, dev_c, first=0, count=None):
        high = tall[m]
        count = blocks if count is None else count
        start = high + rb * dev_y if kind == 0 else (1 - dev_y) * (high + pair)
        height = rb if kind == 0 else high
        return ext[m].at[pl.ds(dev_c * blocks + first, count), pl.ds(pl.multiple_of(start, 16), height)]

    def gather_copy(m, kind, dev_y, dev_c, slot, target, first=0, count=None):
        piece = item(m, kind, dev_y, dev_c, first, count)
        return pltpu.make_async_remote_copy(
            src_ref=piece,
            dst_ref=piece,
            send_sem=agsend.at[m, kind, slot],
            recv_sem=agrecv.at[m, kind, 2 * cols if first else dev_y * cols + dev_c],
            device_id=target,
            device_id_type=MESH,
        )

    most = blocks - 1
    side = 2 * (1 - x) + k
    sibling, beside, below = (r, 2 * x + 1 - k), (r, side), (2 * z + 1 - y, c)

    def if_there(kind, dev_y, action):
        if kind == 0:
            action()
        else:
            pl.when(has_rim(dev_y))(action)

    def kinds(m):
        return (0,) if m == 0 else (0, 1)

    def own_copies(m, kind):
        return [gather_copy(m, kind, y, c, slot, to) for slot, to in enumerate((beside, below, sibling))]

    def side_copies(m, kind):
        return [gather_copy(m, kind, y, side, 3, below, 0, most), gather_copy(m, kind, y, side, 5, sibling)]

    def below_copies(m, kind):
        return [
            gather_copy(m, kind, 1 - y, c, 4, beside, most, blocks - most),
            gather_copy(m, kind, 1 - y, c, 6, sibling),
        ]

    def diagonal_copies(m, kind):
        return [gather_copy(m, kind, 1 - y, side, 7, sibling)]

    def start_own(m, kind):
        if kind == 0:
            high = tall[m]
            for a in range(blocks):
                ext[m][c * blocks + a, pl.ds(pl.multiple_of(high + rb * y, 16), rb)] = dz_ref[m, a]

        def action():
            if kind == 1:
                rim_copy(m, False).wait_recv()
            for copy in own_copies(m, kind):
                copy.start()

        if_there(kind, y, action)

    def pass_on(m):
        for kind in kinds(m):
            def from_side():
                gather_copy(m, kind, y, side, 0, beside).wait_recv()
                for copy in side_copies(m, kind):
                    copy.start()

            def from_below():
                gather_copy(m, kind, 1 - y, c, 0, below).wait_recv()
                for copy in below_copies(m, kind):
                    copy.start()

            if_there(kind, y, from_side)
            if_there(kind, 1 - y, from_below)

    def pass_last(m):
        for kind in kinds(m):
            def action():
                gather_copy(m, kind, 1 - y, side, 0, below, 0, most).wait_recv()
                gather_copy(m, kind, 1 - y, side, 0, beside, most, blocks - most).wait_recv()
                for copy in diagonal_copies(m, kind):
                    copy.start()

            if_there(kind, 1 - y, action)

    def finish_gather(m):
        for kind in kinds(m):
            for dev_y in (y, 1 - y):
                for dev_c in (c, side):
                    piece = gather_copy(m, kind, dev_y, dev_c + 1 - 2 * k, 0, sibling)
                    if_there(kind, dev_y, piece.wait_recv)

    def finish_sends(m):
        for kind in kinds(m):
            def action():
                for copy in own_copies(m, kind) + side_copies(m, kind):
                    copy.wait_send()

            def below_action():
                for copy in below_copies(m, kind) + diagonal_copies(m, kind):
                    copy.wait_send()

            if_there(kind, y, action)
            if_there(kind, 1 - y, below_action)

    for m in (1, 2, 3):
        pl.when(sends_rim)(rim_copy(m, True).start)
    start_own(1, 0)

    pool_cols = Exchange(cols, c, lambda other: (r, other), pcbuf, pcsend, pcrecv)
    pcbuf[c] = dap_ref[...]
    pool_cols.start()

    for block in range(across):
        idrep[block] = jnp.broadcast_to(ids_ref[:, block : block + 1], idrep.shape[1:])
    for m in (1, 2, 3):
        high = tall[m]

        @pl.when(z == 0)
        def _():
            @pl.loop(0, across)
            def _(block):
                ext[m][block, 0:high] = jnp.zeros((high, width), BF16)

        @pl.when(z == levels - 1)
        def _():
            @pl.loop(0, across)
            def _(block):
                ext[m][block, high + pair : 2 * high + pair] = jnp.zeros((high, width), BF16)

    for shift in range(-REACH, REACH + 1):
        for block in range(across):
            if 0 <= block - shift < across:
                same = idrep[block, own : own + 48] == idrep[block - shift, own : own + 48]
                colmask[REACH + shift, block] = wide(same.astype(F32), width).astype(BF16)
            else:
                colmask[REACH + shift, block] = jnp.zeros((48, width), BF16)

    start_own(1, 1)
    start_own(2, 0)
    for l in range(2):
        for a in range(blocks):
            @pl.loop(0, 2 * cols)
            def _(dev):
                x_copy(l, dev, a).wait()

        spot = pl.multiple_of(lax.rem(l + z_lo, 2) * half, half)
        for chunk in range(xall.shape[1] // 128):
            piece = slice(chunk * 128, (chunk + 1) * 128)
            xt[pl.ds(spot, half), piece] = xall[l, piece, :].astype(F32).T.astype(BF16)

    pass_on(1)

    point_copy.wait()

    @pl.loop(0, wpt.shape[0] // 256)
    def _(n):
        piece = pl.ds(pl.multiple_of(n * 256, 256), 256)
        left = jnp.concatenate([dz_ref[0, a] for a in range(blocks)], axis=0)
        acc[:, piece] = contract_lanes(left, wpt[piece, :])

    pool_copy = pltpu.make_async_copy(wpl_ref, wpt, wptsem)
    pool_copy.start()

    def build_shifted(m):
        high = tall[m]

        @pl.loop(0, across)
        def _(block):
            whole = ext[m][block].astype(F32)
            for i in range(3):
                down = (i - 1) * 36 * m
                value = whole[high - down : high - down + pair]
                if i != 1:
                    same = idrep[block, own : own + pair] == idrep[block, own - down : own - down + pair]
                    value = jnp.where(wide(same.astype(F32), width) > 0.0, value, 0.0)
                shifted[i, block] = value.astype(BF16)

    def masked(values, mask):
        count = values.shape[0] // 48
        return jnp.concatenate([values[48 * n : 48 * (n + 1)] * mask for n in range(count)], axis=0)

    def scatter_first(n, part):
        keep[n] = part[:half]
        send1[n] = part[half:].astype(BF16)
        stage1(n).start()

    def stage1(n):
        return pltpu.make_async_remote_copy(
            src_ref=send1.at[n], dst_ref=recv1.at[n], send_sem=s1send.at[n], recv_sem=s1recv.at[n],
            device_id=(r + 2 - 4 * z_lo, c), device_id_type=MESH,
        )

    def stage2(n):
        return pltpu.make_async_remote_copy(
            src_ref=relay.at[n], dst_ref=relay.at[n], send_sem=s2send.at[n], recv_sem=s2recv.at[n],
            device_id=(lax.rem(r + rows // 2, rows), c), device_id_type=MESH,
        )

    def stage3(n, from_x, slot, target):
        piece = dw.at[n, pl.ds(pl.multiple_of(from_x * half, half), half)]
        return pltpu.make_async_remote_copy(
            src_ref=piece, dst_ref=piece, send_sem=s3send.at[slot, n], recv_sem=s3recv.at[from_x, n],
            device_id=target, device_id_type=MESH,
        )

    last = z_hi == k

    def drain2(start, count):
        @pl.loop(start, start + count)
        def _(n):
            stage1(n).wait_recv()
            total = keep[n] + recv1[n].astype(F32)

            @pl.when(last)
            def _():
                keep[n] = total

            @pl.when(jnp.logical_not(last))
            def _():
                relay[n] = total.astype(BF16)
                stage2(n).start()

    def drain3(start, count):
        @pl.when(last)
        def _():
            @pl.loop(start, start + count)
            def _(n):
                stage2(n).wait_recv()
                dw[n, pl.ds(pl.multiple_of(x * half, half), half)] = (keep[n] + relay[n].astype(F32)).astype(BF16)
                stage3(n, x, 0, beside).start()
                stage3(n, x, 1, sibling).start()

    def drain4(start, count):
        @pl.when(last)
        def _():
            @pl.loop(start, start + count)
            def _(n):
                copy = stage3(n, 1 - x, 2, sibling)
                copy.wait_recv()
                copy.start()

        @pl.when(jnp.logical_not(last))
        def _():
            @pl.loop(start, start + count)
            def _(n):
                stage3(n, 0, 0, sibling).wait_recv()
                stage3(n, 1, 0, sibling).wait_recv()

    def weight_grad(m):
        @pl.loop(0, 9)
        def _(tap):
            i, j = tap // 3, lax.rem(tap, 3)
            shift = (j - 1) * m

            @pl.loop(0, across)
            def _(block):
                source = lax.rem(block - shift + across, across)
                gmat[pl.ds(pl.multiple_of(block * pair, 16), pair)] = masked(
                    shifted[i, source], colmask[REACH + shift, block]
                )

            scatter_first((m - 1) * 9 + tap, jnp.dot(xt[...], gmat[...], preferred_element_type=F32))

    def feature_grad(m, lines):
        for i in lines:
            n = (m - 1) * 3 + i
            slot = n % 2
            for j in range(3):
                shift = (j - 1) * m
                for a in range(blocks):
                    block = c * blocks + a
                    source = lax.rem(block - shift + across, across)
                    gown[a * rb : (a + 1) * rb, j * width : (j + 1) * width] = masked(
                        shifted[i, source, pl.ds(pl.multiple_of(y * rb, 16), rb)], colmask[REACH + shift, block]
                    )
            for j in range(3):
                weight_copy(jnp.int32(n), j).wait()

            @pl.loop(0, wbuf.shape[1] // 256)
            def _(chunk):
                piece = pl.ds(pl.multiple_of(chunk * 256, 256), 256)
                acc[:, piece] += contract_lanes(gown[...], wbuf[slot, piece, :])

            if n + 2 < 9:
                for j in range(3):
                    weight_copy(jnp.int32(n + 2), j).start()

    pass_last(1)
    start_own(2, 1)
    start_own(3, 0)
    finish_gather(1)
    build_shifted(1)
    weight_grad(1)
    pass_on(2)
    feature_grad(1, (0, 1))
    pass_last(2)
    start_own(3, 1)
    start_own(0, 0)
    feature_grad(1, (2,))
    drain2(0, 9)
    finish_gather(2)
    build_shifted(2)
    weight_grad(2)
    pass_on(3)
    feature_grad(2, (0, 1))
    pass_last(3)
    pass_on(0)
    feature_grad(2, (2,))
    drain3(0, 9)
    drain2(9, 9)
    pass_last(0)
    finish_gather(3)
    build_shifted(3)
    weight_grad(3)
    finish_gather(0)

    @pl.loop(0, across)
    def _(block):
        gmat[pl.ds(pl.multiple_of(block * pair, 16), pair)] = ext0[block]

    scatter_first(27, jnp.dot(xt[...], gmat[...], preferred_element_type=F32))
    drain4(0, 9)
    drain3(9, 9)

    pool_cols.arrive()
    pool_rows = Exchange(rows, r, lambda other: (other, c), prbuf, prsend, prrecv)
    prbuf[r] = pool_cols.total()
    pool_rows.start()
    feature_grad(3, (0, 1, 2))
    drain2(18, 10)
    drain4(9, 9)
    pool_rows.arrive()
    normed = pooln_ref[...]
    grad = pool_rows.total() * pools_ref[...]
    shift_sum = jnp.sum(grad, axis=0, keepdims=True)
    gain_sum = jnp.sum(grad * normed, axis=0, keepdims=True)
    gain = gain_ref[4:5]
    grad_z = (
        stat_ref[10:11]
        * (grad * gain - gain * shift_sum / image_count - normed * (gain * gain_sum / image_count))
    ).astype(BF16)
    gpool_ref[...] = contract_rows(pooled_ref[...], grad_z)
    gstat_ref[...] = jnp.concatenate([shift_sum, gain_sum] + [jnp.zeros((1, width), F32)] * 6, axis=0)
    own_ids = jnp.concatenate([idrep[c * blocks + a, own : own + pair] for a in range(blocks)], axis=0)
    upper_row = jnp.broadcast_to((y == 0).astype(F32), (pixels, 128))
    own_ids = jnp.where(
        upper_row > 0.0,
        jnp.concatenate([own_ids[a * pair : a * pair + rb] for a in range(blocks)], axis=0),
        jnp.concatenate([own_ids[a * pair + rb : (a + 1) * pair] for a in range(blocks)], axis=0),
    )
    lanes = lax.broadcasted_iota(jnp.int32, (pixels, 128), 1).astype(F32)
    one_hot = (own_ids == lanes).astype(F32).astype(BF16)
    counts = wide(counts_ref[...], 256)
    pool_copy.wait()

    @pl.loop(0, wpt.shape[0] // 256)
    def _(n):
        piece = pl.ds(pl.multiple_of(n * 256, 256), 256)
        back = contract_lanes(grad_z, wpt[piece, :]) / counts
        back = jnp.concatenate([back, jnp.zeros((128 - images, 256), F32)], axis=0).astype(BF16)
        value = (acc[:, piece] + jnp.dot(one_hot, back, preferred_element_type=F32)).astype(BF16)
        gx_ref[:, piece] = jnp.dot(back_ref[...], value, preferred_element_type=F32).astype(BF16)

    drain3(18, 10)
    drain4(18, 10)
    results = (
        pltpu.make_async_copy(dw.at[pl.ds(0, 27)], dw_ref, outsem.at[0]),
        pltpu.make_async_copy(dw.at[27], dpoint_ref, outsem.at[1]),
    )
    for result in results:
        result.start()

    pool_cols.leave()
    pool_rows.leave()
    for m in (1, 2, 3):
        pl.when(sends_rim)(rim_copy(m, True).wait_send)
    for m in (1, 2, 3, 0):
        finish_sends(m)

    @pl.loop(0, 28)
    def _(n):
        stage1(n).wait_send()

        @pl.when(last)
        def _():
            stage3(n, x, 0, beside).wait_send()
            stage3(n, x, 1, sibling).wait_send()
            stage3(n, 1 - x, 2, sibling).wait_send()

        @pl.when(jnp.logical_not(last))
        def _():
            stage2(n).wait_send()

    for result in results:
        result.wait()


def backward_call(
    rows, cols, image_count, dz, xsub, ids, wat, wpt, wpl, gain, counts, pooled, pooln, pools, dap, stat, back
):
    _, blocks, rb, width = dz.shape
    channels = wpt.shape[0]
    share = channels // rows
    pair, across, pixels = 2 * rb, cols * blocks, blocks * rb
    images = dap.shape[0]
    group = pair * across
    vmem = pl.BlockSpec(memory_space=pltpu.VMEM)
    hbm = pl.BlockSpec(memory_space=pl.ANY)
    dma = pltpu.SemaphoreType.DMA
    taps = 28

    def ext(high):
        return pltpu.VMEM((across, 2 * high + pair, width), BF16)

    return pl.pallas_call(
        functools.partial(backward_kernel, rows, cols, float(image_count), rb),
        out_shape=(
            jax.ShapeDtypeStruct((pixels, channels), BF16),
            jax.ShapeDtypeStruct((taps - 1, share, width), BF16),
            jax.ShapeDtypeStruct((share, width), BF16),
            jax.ShapeDtypeStruct((share, width), F32),
            jax.ShapeDtypeStruct((8, width), F32),
        ),
        in_specs=[vmem, hbm, vmem, hbm, hbm, hbm] + [vmem] * 8,
        out_specs=(vmem, hbm, hbm, vmem, vmem),
        scratch_shapes=[
            ext(0), ext(HALO[1]), ext(HALO[2]), ext(HALO[3]),
            pltpu.VMEM((3, across, pair, width), BF16),
            pltpu.VMEM((2 * REACH + 1, across, 48, width), BF16),
            pltpu.VMEM((across, ids.shape[0], 128), F32),
            pltpu.VMEM((group, width), BF16),
            pltpu.VMEM((pixels, 3 * width), BF16),
            pltpu.VMEM((2, group, share // 2), BF16),
            pltpu.VMEM((share, group), BF16),
            pltpu.VMEM((pixels, channels), F32),
            pltpu.VMEM((2, channels, 3 * width), BF16),
            pltpu.VMEM((channels, width), BF16),
            pltpu.VMEM((taps, share // 2, width), BF16),
            pltpu.VMEM((taps, share // 2, width), BF16),
            pltpu.VMEM((taps, share // 2, width), F32),
            pltpu.VMEM((taps, share // 2, width), BF16),
            pltpu.VMEM((taps, share, width), BF16),
            pltpu.VMEM((cols, images, width), F32),
            pltpu.VMEM((rows, images, width), F32),
            dma((2, 2 * cols, blocks)), dma((2, 3)), dma,
            dma((4,)), dma((4,)),
            dma((4, 2, 8)), dma((4, 2, 2 * cols + 1)),
            dma((taps,)), dma((taps,)),
            dma((taps,)), dma((taps,)),
            dma((3, taps)), dma((2, taps)),
            dma((cols,)), dma((cols,)),
            dma((rows,)), dma((rows,)),
            dma((2,)),
        ],
        compiler_params=pltpu.CompilerParams(
            collective_id=1, has_side_effects=True, vmem_limit_bytes=64 * 2**20
        ),
        cost_estimate=pl.CostEstimate(flops=4 * pixels * channels * width * 28, bytes_accessed=50_000_000, transcendentals=0),
    )(dz, xsub, ids, wat, wpt, wpl, gain, counts, pooled, pooln, pools, dap, stat, back)


def extended(cells, sides, width):
    for axis, dim in sides:
        count = lax.axis_size(axis)
        ends = count - 1
        head = lax.slice_in_dim(cells, 0, width, axis=dim)
        tail = lax.slice_in_dim(cells, cells.shape[dim] - width, cells.shape[dim], axis=dim)
        cells = jnp.concatenate(
            [
                lax.ppermute(tail, axis, [(i, (i + 1) % count) for i in range(ends)]),
                cells,
                lax.ppermute(head, axis, [((i + 1) % count, i) for i in range(ends)]),
            ],
            axis=dim,
        )
    return cells


def image_match(window, own_ids, row_start, col_start):
    rows_here, cols_here = own_ids.shape
    section = window[row_start : row_start + rows_here, col_start : col_start + cols_here]
    return (section == own_ids).astype(jnp.float32).reshape(rows_here * cols_here, 1)


def silu_slope(preact_in):
    sigma = jax.nn.sigmoid(preact_in)
    return sigma * (1.0 + preact_in * (1.0 - sigma))


def transposed(left, right):
    return lax.dot_general(
        left, right, (((1,), (1,)), ((), ())), preferred_element_type=jnp.float32
    )


def shards(
    features, image_ids, w_point, w_atrous, w_pool, w_proj, norm_gain, norm_shift, cotangent
):
    rows_here, cols_here, channels = features.shape
    branch_width = w_point.shape[1]
    pixels = rows_here * cols_here
    grid_rows, grid_cols = image_ids.shape
    total_pixels = float(grid_rows * grid_cols)
    image_count = grid_rows // 16 * (grid_cols // 32)
    dilations = (RATE_LOW, RATE_MID, RATE_TOP)
    margin = RATE_TOP
    row_index = lax.axis_index("rows")
    col_index = lax.axis_index("cols")
    id_padded = jnp.pad(image_ids, margin, constant_values=-1)
    window = lax.dynamic_slice(
        id_padded,
        (row_index * rows_here, col_index * cols_here),
        (rows_here + 2 * margin, cols_here + 2 * margin),
    )
    own_ids = window[margin : margin + rows_here, margin : margin + cols_here]
    own_flat = own_ids.reshape(pixels)
    flattened = features.reshape(pixels, channels)
    padded = extended(features, (("rows", 0), ("cols", 1)), margin)
    one_hot = (own_flat[:, None] == jnp.arange(image_count, dtype=jnp.int32)[None, :]).astype(
        jnp.bfloat16
    )
    local_sums = jnp.einsum("pn,pc->nc", one_hot, flattened, preferred_element_type=jnp.float32)
    counts = jax.ops.segment_sum(
        jnp.ones((grid_rows * grid_cols,), jnp.float32), image_ids.reshape(-1), image_count
    )
    image_totals = lax.psum(local_sums, ("rows", "cols"))
    branch_outs = [jnp.dot(flattened, w_point, preferred_element_type=jnp.float32)]
    for branch, dilation in enumerate(dilations):
        running = jnp.zeros((pixels, branch_width), jnp.float32)
        for stencil in range(9):
            row_shift = (stencil // 3 - 1) * dilation
            col_shift = (stencil % 3 - 1) * dilation
            source = padded[
                margin + row_shift : margin + row_shift + rows_here,
                margin + col_shift : margin + col_shift + cols_here,
            ].reshape(pixels, channels)
            same_image = image_match(window, own_ids, margin + row_shift, margin + col_shift)
            running = running + same_image * jnp.dot(
                source, w_atrous[branch, stencil], preferred_element_type=jnp.float32
            )
        branch_outs.append(running)
    spatial = jnp.stack(branch_outs, axis=1)
    first_sum = jnp.sum(spatial, axis=0)
    second_sum = jnp.sum(spatial * spatial, axis=0)
    first_sum, second_sum = lax.psum((first_sum, second_sum), ("rows", "cols"))
    average = first_sum / total_pixels
    inverse_std = lax.rsqrt(second_sum / total_pixels - average * average + epsilon)
    normed = (spatial - average) * inverse_std
    preact = norm_gain[:4] * normed + norm_shift[:4]
    active = jax.nn.silu(preact).astype(jnp.bfloat16)
    pooled = (image_totals / counts[:, None]).astype(jnp.bfloat16)
    pool_z = jnp.dot(pooled, w_pool, preferred_element_type=jnp.float32)
    pool_avg = jnp.mean(pool_z, axis=0)
    pool_square = jnp.mean(pool_z * pool_z, axis=0)
    pool_inverse = lax.rsqrt(pool_square - pool_avg * pool_avg + epsilon)
    pool_normed = (pool_z - pool_avg) * pool_inverse
    pool_pre = norm_gain[4] * pool_normed + norm_shift[4]
    pool_active = jax.nn.silu(pool_pre).astype(jnp.bfloat16)
    joined = jnp.concatenate(
        [active.reshape(pixels, 4 * branch_width), jnp.take(pool_active, own_flat, axis=0)], axis=1
    )
    final_z = jnp.dot(joined, w_proj, preferred_element_type=jnp.float32)
    final_first, final_second = lax.psum(
        (jnp.sum(final_z, axis=0), jnp.sum(final_z * final_z, axis=0)), ("rows", "cols")
    )
    final_avg = final_first / total_pixels
    final_inverse = lax.rsqrt(final_second / total_pixels - final_avg * final_avg + epsilon)
    final_normed = (final_z - final_avg) * final_inverse
    final_pre = norm_gain[5] * final_normed + norm_shift[5]
    output = jax.nn.silu(final_pre).astype(jnp.bfloat16).reshape(rows_here, cols_here, branch_width)
    upstream = cotangent.reshape(pixels, branch_width).astype(jnp.float32)
    grad_final = upstream * silu_slope(final_pre)
    shift_last, gain_last = lax.psum(
        (jnp.sum(grad_final, axis=0), jnp.sum(grad_final * final_normed, axis=0)), ("rows", "cols")
    )
    grad_final_z = (
        final_inverse
        * (
            grad_final * norm_gain[5]
            - norm_gain[5] * shift_last / total_pixels
            - final_normed * (norm_gain[5] * gain_last / total_pixels)
        )
    ).astype(jnp.bfloat16)
    proj_term = jnp.einsum("pk,pc->kc", joined, grad_final_z, preferred_element_type=jnp.float32)
    grad_joined = transposed(grad_final_z, w_proj)
    grad_pre = grad_joined[:, : 4 * branch_width].reshape(pixels, 4, branch_width) * silu_slope(
        preact
    )
    grad_pixel = grad_joined[:, 4 * branch_width :]
    shift_sums = jnp.sum(grad_pre, axis=0)
    gain_sums = jnp.sum(grad_pre * normed, axis=0)
    image_grads = jax.ops.segment_sum(grad_pixel, own_flat, image_count)
    shift_sums, gain_sums, image_grads = lax.psum(
        (shift_sums, gain_sums, image_grads), ("rows", "cols")
    )
    grad_branch = (
        inverse_std
        * (
            grad_pre * norm_gain[:4]
            - norm_gain[:4] * shift_sums / total_pixels
            - normed * (norm_gain[:4] * gain_sums / total_pixels)
        )
    ).astype(jnp.bfloat16)
    grad_pool_pre = image_grads * silu_slope(pool_pre)
    pool_shift = jnp.sum(grad_pool_pre, axis=0)
    pool_gain = jnp.sum(grad_pool_pre * pool_normed, axis=0)
    grad_pool_z = (
        pool_inverse
        * (
            grad_pool_pre * norm_gain[4]
            - norm_gain[4] * pool_shift / image_count
            - pool_normed * (norm_gain[4] * pool_gain / image_count)
        )
    ).astype(jnp.bfloat16)
    row_share = channels // lax.axis_size("rows")
    pool_columns = lax.dynamic_slice_in_dim(pooled, row_index * row_share, row_share, 1)
    grad_pool = jnp.einsum(
        "nk,nc->kc", pool_columns, grad_pool_z, preferred_element_type=jnp.float32
    )
    grad_pooled = transposed(grad_pool_z, w_pool) / counts[:, None]
    grad_input = jnp.take(grad_pooled, own_flat, axis=0) + transposed(grad_branch[:, 0], w_point)
    point_term = jnp.einsum(
        "pk,pc->kc", flattened, grad_branch[:, 0], preferred_element_type=jnp.float32
    )
    stacked = grad_branch[:, 1:].reshape(rows_here, cols_here, 3 * branch_width)
    grad_padded = extended(stacked, (("rows", 0), ("cols", 1)), margin)
    rim_list = [
        grad_padded[:, :, branch * branch_width : (branch + 1) * branch_width]
        for branch in range(3)
    ]
    rim_bases = [margin, margin, margin]
    atrous_terms = []
    for branch, dilation in enumerate(dilations):
        tap_terms = []
        rim_base = rim_bases[branch]
        for stencil in range(9):
            row_shift = (stencil // 3 - 1) * dilation
            col_shift = (stencil % 3 - 1) * dilation
            source = padded[
                margin + row_shift : margin + row_shift + rows_here,
                margin + col_shift : margin + col_shift + cols_here,
            ].reshape(pixels, channels)
            same_image = image_match(window, own_ids, margin + row_shift, margin + col_shift)
            masked = same_image.astype(jnp.bfloat16) * grad_branch[:, branch + 1]
            tap_terms.append(
                jnp.einsum("pk,pc->kc", source, masked, preferred_element_type=jnp.float32)
            )
            incoming = rim_list[branch][
                rim_base - row_shift : rim_base - row_shift + rows_here,
                rim_base - col_shift : rim_base - col_shift + cols_here,
            ].reshape(pixels, branch_width)
            back_image = image_match(window, own_ids, margin - row_shift, margin - col_shift)
            grad_input = grad_input + back_image * transposed(incoming, w_atrous[branch, stencil])
        atrous_terms.append(jnp.stack(tap_terms))
    atrous_term = jnp.stack(atrous_terms)
    shared = (
        lax.psum_scatter(
            point_term.astype(jnp.bfloat16), "rows", scatter_dimension=0, tiled=True
        ).astype(jnp.float32),
        lax.psum_scatter(
            atrous_term.astype(jnp.bfloat16), "rows", scatter_dimension=2, tiled=True
        ).astype(jnp.float32),
        lax.psum_scatter(
            proj_term.astype(jnp.bfloat16), "rows", scatter_dimension=0, tiled=True
        ).astype(jnp.float32),
    )
    shared = (
        lax.psum(shared[0].astype(jnp.bfloat16), "cols").astype(jnp.float32),
        lax.psum(shared[1].astype(jnp.bfloat16), "cols").astype(jnp.float32),
        lax.psum(shared[2].astype(jnp.bfloat16), "cols").astype(jnp.float32),
    )
    grad_gain = jnp.concatenate([gain_sums, pool_gain[None], gain_last[None]], axis=0)
    grad_shift = jnp.concatenate([shift_sums, pool_shift[None], shift_last[None]], axis=0)
    grad_features = grad_input.astype(jnp.bfloat16).reshape(rows_here, cols_here, channels)
    return (
        output,
        grad_features,
        shared[0],
        shared[1],
        grad_pool,
        shared[2],
        grad_gain,
        grad_shift,
    )


def block_order(height, breadth):
    pixel = np.arange(height * breadth).reshape(height, breadth // STEP, STEP).transpose(1, 0, 2).reshape(-1)
    return np.eye(height * breadth, dtype=np.float32)[pixel]


def id_columns(ids):
    height, breadth = ids.shape
    table = ids.reshape(height, breadth // STEP, STEP).transpose(0, 2, 1).reshape(height * STEP, breadth // STEP)
    return jnp.pad(table.astype(F32), ((0, 0), (0, 128 - breadth // STEP)))


def quick_shards(
    features, image_ids, w_point, w_atrous, w_pool, w_proj, norm_gain, norm_shift, cotangent
):
    rows_here, cols_here, channels = features.shape
    branch_width = w_point.shape[1]
    pixels = rows_here * cols_here
    grid_rows, grid_cols = image_ids.shape
    image_count = grid_rows // 16 * (grid_cols // 32)
    images = -(-image_count // 16) * 16
    margin = RATE_TOP
    rows, cols = lax.axis_size("rows"), lax.axis_size("cols")
    row_index = lax.axis_index("rows")
    col_index = lax.axis_index("cols")
    id_padded = jnp.pad(image_ids, margin, constant_values=-1)
    window = lax.dynamic_slice(
        id_padded,
        (row_index * rows_here, col_index * cols_here),
        (rows_here + 2 * margin, cols_here + 2 * margin),
    )
    own_ids = window[margin : margin + rows_here, margin : margin + cols_here]
    own_flat = own_ids.reshape(pixels)
    counts = jnp.sum(
        (image_ids.reshape(-1, 1) == jnp.arange(images, dtype=jnp.int32)[None, :]).astype(F32), axis=0
    )
    counts = jnp.maximum(counts, 1.0)
    count_table = jnp.broadcast_to(counts[:, None], (images, 128))
    order = block_order(rows_here, cols_here)
    order, back = jnp.asarray(order, BF16), jnp.asarray(order.T, BF16)
    output, dz, proj_term, stats, pooled, pool_normed, pool_slope, dap, xsub = forward_call(
        rows, cols, image_count, features.reshape(pixels, channels), order, back, id_columns(window), w_atrous, w_point, w_pool, w_proj,
        norm_gain, norm_shift, cotangent.reshape(pixels, branch_width), count_table,
    )
    output = output.reshape(rows_here, cols_here, branch_width)
    pair_window = lax.dynamic_slice(
        id_padded,
        (row_index // 2 * (2 * rows_here), jnp.int32(margin)),
        (2 * rows_here + 2 * margin, grid_cols),
    )
    grad_input, atrous, point, grad_pool, pool_sums = backward_call(
        rows, cols, image_count, dz, xsub.reshape(2, 8, 4, pixels // 4, -1), id_columns(pair_window), w_atrous, w_point, w_pool,
        norm_gain, count_table, pooled, pool_normed, pool_slope, dap, stats, back,
    )
    grad_atrous = atrous.astype(F32).reshape(3, 9, channels // rows, branch_width)

    proj_share = proj_term.shape[0] // rows
    grad_proj = lax.psum(proj_term, ("rows", "cols"))
    grad_proj = lax.dynamic_slice_in_dim(grad_proj, row_index * proj_share, proj_share, 0).astype(F32)
    grad_gain = jnp.concatenate([stats[4:8], pool_sums[1:2], stats[9:10]], axis=0)
    grad_shift = jnp.concatenate([stats[0:4], pool_sums[0:1], stats[8:9]], axis=0)
    grad_features = grad_input.reshape(rows_here, cols_here, channels)
    return (
        output, grad_features, point.astype(F32), grad_atrous, grad_pool,
        grad_proj, grad_gain, grad_shift,
    )


def solution(mesh):
    placed = (P("rows", "cols", None), P(), P(), P(), P(), P(), P(), P(), P("rows", "cols", None))
    quick = mesh.shape["rows"] == 8 and mesh.shape["cols"] == 4
    return jax.shard_map(
        quick_shards if quick else shards,
        mesh=mesh,
        in_specs=placed,
        out_specs=(
            P("rows", "cols", None),
            P("rows", "cols", None),
            P("rows", None),
            P(None, None, "rows", None),
            P("rows", None),
            P("rows", None),
            P(),
            P(),
        ),
        check_vma=False,
    )
```

```python
import functools
import jax
import jax.numpy as jnp
import numpy as np
from jax import lax
from jax.experimental import pallas as pl
from jax.experimental.pallas import tpu as pltpu
from jax.sharding import PartitionSpec as P

MESH = pl.DeviceIdType.MESH
RATE_LOW = 6
RATE_MID = 12
RATE_TOP = 18
STEP = RATE_LOW
REACH = RATE_TOP // STEP
HALO = {1: 48, 2: 80, 3: 112}
SLOTS = 4
epsilon = 1e-05
F32 = jnp.float32
BF16 = jnp.bfloat16


def wide(column, width):
    return jnp.concatenate([column] * (width // column.shape[-1]), axis=-1)


def silu_parts(preact):
    sigma = jax.nn.sigmoid(preact)
    return preact * sigma, sigma * (1.0 + preact * (1.0 - sigma))


def contract_rows(left, right):
    return lax.dot_general(left, right, (((0,), (0,)), ((), ())), preferred_element_type=F32)


def contract_lanes(left, right):
    return lax.dot_general(left, right, (((1,), (1,)), ((), ())), preferred_element_type=F32)


def greet_all(rows, cols, r, c):
    barrier = pltpu.get_barrier_semaphore()
    for dr in range(rows):
        for dc in range(cols):
            if dr or dc:
                other = (lax.rem(r + dr, rows), lax.rem(c + dc, cols))
                pl.semaphore_signal(barrier, inc=1, device_id=other, device_id_type=MESH)
    pl.semaphore_wait(barrier, rows * cols - 1)


class Exchange:
    def __init__(self, axis_size, place, to_device, slots, send_sems, recv_sems):
        self.size, self.place, self.to_device = axis_size, place, to_device
        self.slots, self.send_sems, self.recv_sems = slots, send_sems, recv_sems

    def copy(self, step, source=None):
        other = lax.rem(self.place + step, self.size)
        mine = self.slots.at[self.place]
        return pltpu.make_async_remote_copy(
            src_ref=mine if source is None else source(other),
            dst_ref=mine,
            send_sem=self.send_sems.at[step],
            recv_sem=self.recv_sems.at[self.place],
            device_id=self.to_device(other),
            device_id_type=MESH,
        )

    def start(self, source=None):
        for step in range(1, self.size):
            self.copy(step, source).start()

    def arrive(self):
        for step in range(1, self.size):
            other = lax.rem(self.place + step, self.size)
            there = self.slots.at[other]
            pltpu.make_async_remote_copy(
                src_ref=there,
                dst_ref=there,
                send_sem=self.send_sems.at[step],
                recv_sem=self.recv_sems.at[other],
                device_id=self.to_device(other),
                device_id_type=MESH,
            ).wait_recv()

    def leave(self, source=None):
        for step in range(1, self.size):
            self.copy(step, source).wait_send()

    def total(self):
        value = self.slots[0]
        for other in range(1, self.size):
            value = value + self.slots[other]
        return value


def forward_kernel(
    rows, cols, image_count, total_pixels,
    raw_ref, order_ref, back_ref, ids_ref, wat_ref, wpt_ref, wpl_ref, wpj_ref, gain_ref, shift_ref, cot_ref,
    counts_ref, out_ref, dz_ref, pj_ref, stat_ref, pooled_ref, pooln_ref, pools_ref, dap_ref, xsub_ref,
    x_ref, idrep, wbuf, wplbuf, parts, sums_by_row, edge_out, edge_in, rim_out, rim_in, zn, slope, joined, zf, dzf, active, isum, cbuf, rbuf, pr_buf, pc_buf, pz_buf,
    wsem, wplsem, esend, erecv, hsend, hrecv, csend, crecv, rsend, rrecv, psend, precv, pcsend, pcrecv, pzsend, pzrecv,
    xsend, xrecv,
):
    r, c = lax.axis_index("rows"), lax.axis_index("cols")
    blocks, rb, width = zn.shape[1], zn.shape[2], zn.shape[3]
    pixels = blocks * rb
    own = REACH * 36
    images = isum.shape[0]
    taps = 27

    def weight_copy(n):
        branch, tap = 2 - n // 9, lax.rem(n, 9)
        slot = lax.rem(n, SLOTS)
        return pltpu.make_async_copy(wat_ref.at[branch, tap], wbuf.at[slot], wsem.at[slot])

    for n in range(SLOTS - 1):
        weight_copy(jnp.int32(n)).start()
    share = x_ref.shape[1] // rows
    pool_weight = pltpu.make_async_copy(
        wpl_ref.at[pl.ds(pl.multiple_of(r * share, share), share)], wplbuf, wplsem
    )
    pool_weight.start()
    for block in range(idrep.shape[0]):
        idrep[block] = jnp.broadcast_to(ids_ref[:, block : block + 1], idrep.shape[1:])
    greet_all(rows, cols, r, c)

    @pl.loop(0, x_ref.shape[1] // 256)
    def _(n):
        piece = pl.ds(pl.multiple_of(n * 256, 256), 256)
        x_ref[:, piece] = jnp.dot(order_ref[...], raw_ref[:, piece], preferred_element_type=F32).astype(BF16)

    own_ids = jnp.concatenate([idrep[REACH + a, own : own + rb, :] for a in range(blocks)], axis=0)
    lanes = lax.broadcasted_iota(jnp.int32, (pixels, 128), 1).astype(F32)
    one_hot = jnp.concatenate(
        [(own_ids == lanes + 128.0 * part).astype(F32).astype(BF16) for part in range(pl.cdiv(images, 128))],
        axis=1,
    )
    for part in range(rows):
        piece = slice(part * share, (part + 1) * share)
        isum[:, piece] = contract_rows(one_hot, x_ref[:, piece])[:images]
    pool_rows = Exchange(rows, r, lambda other: (other, c), pr_buf, psend, precv)

    def share_of(other):
        return isum.at[:, pl.ds(pl.multiple_of(other * share, share), share)]

    pr_buf[r] = isum[:, pl.ds(pl.multiple_of(r * share, share), share)]
    pool_rows.start(share_of)

    def side_copies(m):
        return [
            (
                (c > 0, c < cols - 1)[way],
                (c < cols - 1, c > 0)[way],
                pltpu.make_async_remote_copy(
                    src_ref=edge_out[m - 1].at[way],
                    dst_ref=edge_in[m - 1].at[way],
                    send_sem=esend.at[m - 1, way],
                    recv_sem=erecv.at[m - 1, way],
                    device_id=(r, lax.rem(c + (cols - 1, 1)[way], cols)),
                    device_id_type=MESH,
                ),
            )
            for way in range(2)
        ]

    def rim_copies(m):
        return [
            (
                (r > 0, r < rows - 1)[way],
                (r < rows - 1, r > 0)[way],
                pltpu.make_async_remote_copy(
                    src_ref=rim_out[m - 1].at[way],
                    dst_ref=rim_in[m - 1].at[way],
                    send_sem=hsend.at[m - 1, way],
                    recv_sem=hrecv.at[m - 1, way],
                    device_id=(lax.rem(r + (rows - 1, 1)[way], rows), c),
                    device_id_type=MESH,
                ),
            )
            for way in range(2)
        ]

    def conv(position, m):
        lines = parts[m - 1]
        for i in range(3):
            @pl.loop(0, blocks + 2 * m)
            def _(block):
                lines[i, block] = jnp.zeros(lines.shape[2:], F32)

            @pl.loop(0, 3)
            def _(j):
                n = position * 9 + 3 * i + j
                slot = lax.rem(n, SLOTS)
                ahead = n + SLOTS - 1

                @pl.when(ahead < taps)
                def _():
                    weight_copy(ahead).start()

                weight_copy(n).wait()
                product = jnp.dot(x_ref[...], wbuf[slot], preferred_element_type=F32)
                for a in range(blocks):
                    same = idrep[REACH + a, own : own + rb] == idrep[REACH + a - (j - 1) * m, own : own + rb]
                    part = product[a * rb : (a + 1) * rb]
                    lines[i, a + (2 - j) * m] += jnp.where(wide(same.astype(F32), width) > 0.0, part, 0.0)

            for a in range(m):
                edge_out[m - 1][0, i, a] = lines[i, a].astype(BF16)
                edge_out[m - 1][1, i, a] = lines[i, m + blocks + a].astype(BF16)
        for sends, _, copy in side_copies(m):
            pl.when(sends)(copy.start)

    def absorb(m):
        height, lines, whole = HALO[m], parts[m - 1], sums_by_row[m - 1]
        for way, (_, receives, copy) in enumerate(side_copies(m)):
            @pl.when(receives)
            def _():
                copy.wait_recv()
                for i in range(3):
                    for a in range(m):
                        lines[i, (blocks, m)[way] + a] += edge_in[m - 1][way, i, a].astype(F32)

        @pl.loop(0, blocks)
        def _(a):
            whole[a, 0:height] = jnp.zeros((height, width), F32)
            whole[a, height : height + rb] = lines[1, m + a]
            whole[a, height + rb : 2 * height + rb] = jnp.zeros((height, width), F32)
            for i in (0, 2):
                up = (i - 1) * 36 * m
                same = idrep[REACH + a, own : own + rb] == idrep[REACH + a, own - up : own - up + rb]
                whole[a, height - up : height - up + rb] += jnp.where(
                    wide(same.astype(F32), width) > 0.0, lines[i, m + a], 0.0
                )
            rim_out[m - 1][0, a] = whole[a, 0:height].astype(BF16)
            rim_out[m - 1][1, a] = whole[a, height + rb : 2 * height + rb].astype(BF16)

        for sends, _, copy in rim_copies(m):
            pl.when(sends)(copy.start)

    def finish(m):
        height, whole = HALO[m], sums_by_row[m - 1]

        @pl.loop(0, blocks)
        def _(a):
            zn[m, a] = whole[a, height : height + rb]

        for way, (_, receives, copy) in enumerate(rim_copies(m)):
            @pl.when(receives)
            def _():
                copy.wait_recv()
                start = (rb - height, 0)[way]
                for a in range(blocks):
                    zn[m, a, start : start + height] += rim_in[m - 1][way, a].astype(F32)

    members = [(dy, dx, dk) for dy in range(2) for dx in range(2) for dk in range(2)]
    half = share // 2

    def channel_slices(y, x, k):
        return [pl.multiple_of((2 * (2 * k + l) + y) * share + x * half, 128) for l in range(2)]

    def member_copies(steps, slices):
        mine = lax.rem(r, 2) * cols + c
        copies = []
        for step in steps:
            dy, dx, dk = members[step]
            y, x, k = lax.rem(r + dy, 2), lax.rem(c // 2 + dx, 2), lax.rem(c + dk, 2)
            starts = channel_slices(y, x, k)
            for l in slices:
                source = x_ref.at[:, pl.ds(starts[l], half)]
                target = xsub_ref.at[l, mine]
                if step == 0:
                    copies.append(pltpu.make_async_copy(source, target, xrecv.at[l, mine]))
                else:
                    copies.append(
                        pltpu.make_async_remote_copy(
                            src_ref=source,
                            dst_ref=target,
                            send_sem=xsend.at[l, step],
                            recv_sem=xrecv.at[l, mine],
                            device_id=(2 * (r // 2) + y, 2 * x + k),
                            device_id_type=MESH,
                        )
                    )
        return copies

    def send_members(steps, slices):
        for copy in member_copies(steps, slices):
            copy.start()

    pool_cols = Exchange(cols, c, lambda other: (r, other), pc_buf, pcsend, pcrecv)
    pool_z = Exchange(rows, r, lambda other: (other, c), pz_buf, pzsend, pzrecv)
    send_members(range(8), (0,))
    send_members((0, 1), (1,))
    conv(0, 3)
    pool_rows.arrive()
    pc_buf[c] = pool_rows.total()
    pool_cols.start()
    conv(1, 2)
    absorb(3)
    pool_cols.arrive()
    counts = counts_ref[...]
    pooled = (pool_cols.total() / wide(counts, share)).astype(BF16)
    pooled_ref[...] = pooled
    pool_weight.wait()
    pz_buf[r] = jnp.dot(pooled, wplbuf[...], preferred_element_type=F32)
    pool_z.start()
    conv(2, 1)
    absorb(2)
    product = jnp.dot(x_ref[...], wpt_ref[...], preferred_element_type=F32)
    for a in range(blocks):
        zn[0, a] = product[a * rb : (a + 1) * rb]
    absorb(1)
    pool_z.arrive()
    zp = pool_z.total()
    pool_avg = jnp.sum(zp, axis=0, keepdims=True) / image_count
    pool_square = jnp.sum(zp * zp, axis=0, keepdims=True) / image_count
    pool_inverse = lax.rsqrt(pool_square - pool_avg * pool_avg + epsilon)
    pool_normed = (zp - pool_avg) * pool_inverse
    pool_active, pool_slope = silu_parts(gain_ref[4:5] * pool_normed + shift_ref[4:5])
    pooln_ref[...] = pool_normed
    pools_ref[...] = pool_slope
    spare = one_hot.shape[1] - images
    pool_active = jnp.concatenate([pool_active, jnp.zeros((spare, width), F32)], axis=0).astype(BF16)
    joined[:, 4 * width : 5 * width] = jnp.dot(one_hot, pool_active, preferred_element_type=F32).astype(BF16)

    for m in (3, 2, 1):
        finish(m)

    started = []

    def all_sum(step, value):
        across = Exchange(cols, c, lambda other: (r, other), cbuf.at[step], csend.at[step], crecv.at[step])
        cbuf[step, c] = value
        across.start()
        across.arrive()
        down = Exchange(rows, r, lambda other: (other, c), rbuf.at[step], rsend.at[step], rrecv.at[step])
        rbuf[step, r] = across.total()
        down.start()
        down.arrive()
        started.extend((across, down))
        return down.total()

    zero = jnp.zeros((1, width), F32)

    def row_sum(value):
        return jnp.sum(value, axis=0, keepdims=True)

    firsts, seconds = [], []
    for k in range(4):
        first, second = zero, zero
        for a in range(blocks):
            value = zn[k, a]
            first, second = first + row_sum(value), second + row_sum(value * value)
        firsts.append(first)
        seconds.append(second)
    moments = all_sum(0, jnp.concatenate(firsts + seconds, axis=0))
    send_members((2, 4), (1,))
    average = moments[0:4] / total_pixels
    inverse = lax.rsqrt(moments[4:8] / total_pixels - average * average + epsilon)
    for k in range(4):
        @pl.loop(0, blocks)
        def _(a):
            normed = (zn[k, a] - average[k : k + 1]) * inverse[k : k + 1]
            value, slant = silu_parts(gain_ref[k : k + 1] * normed + shift_ref[k : k + 1])
            zn[k, a] = normed
            slope[k, a] = slant
            joined[pl.ds(pl.multiple_of(a * rb, rb), rb), k * width : (k + 1) * width] = value.astype(BF16)

    zf[...] = jnp.dot(joined[...], wpj_ref[...], preferred_element_type=F32)
    first, second = zero, zero
    for a in range(blocks):
        value = zf[a * rb : (a + 1) * rb]
        first, second = first + row_sum(value), second + row_sum(value * value)
    moments = all_sum(1, jnp.concatenate([first, second] + [zero] * 6, axis=0))
    send_members((3, 5), (1,))
    final_avg = moments[0:1] / total_pixels
    final_inverse = lax.rsqrt(moments[1:2] / total_pixels - final_avg * final_avg + epsilon)
    shift_last, gain_last = zero, zero
    upstream = jnp.dot(order_ref[...], cot_ref[...], preferred_element_type=F32)
    for a in range(blocks):
        piece = slice(a * rb, (a + 1) * rb)
        normed = (zf[piece] - final_avg) * final_inverse
        result, slant = silu_parts(gain_ref[5:6] * normed + shift_ref[5:6])
        active[piece] = result.astype(BF16)
        grad = upstream[piece] * slant
        zf[piece] = normed
        dzf[piece] = grad
        shift_last, gain_last = shift_last + row_sum(grad), gain_last + row_sum(grad * normed)
    out_ref[...] = jnp.dot(back_ref[...], active[...], preferred_element_type=F32).astype(BF16)
    sums = all_sum(2, jnp.concatenate([shift_last, gain_last] + [zero] * 6, axis=0))
    send_members((6, 7), (1,))
    shift_last, gain_last = sums[0:1], sums[1:2]
    gain = gain_ref[5:6]
    for a in range(blocks):
        piece = slice(a * rb, (a + 1) * rb)
        dzf[piece] = final_inverse * (
            dzf[piece] * gain
            - gain * shift_last / total_pixels
            - zf[piece] * (gain * gain_last / total_pixels)
        )
    grad_final = dzf[...].astype(BF16)

    shifts, gains = [], []
    for k in range(4):
        grad = contract_lanes(grad_final, wpj_ref[k * width : (k + 1) * width])
        shift_sum, gain_sum = zero, zero
        for a in range(blocks):
            part = grad[a * rb : (a + 1) * rb] * slope[k, a]
            slope[k, a] = part
            shift_sum, gain_sum = shift_sum + row_sum(part), gain_sum + row_sum(part * zn[k, a])
        shifts.append(shift_sum)
        gains.append(gain_sum)
    grad_pixel = contract_lanes(grad_final, wpj_ref[4 * width : 5 * width])
    upper = grad_pixel.astype(BF16)
    lower = (grad_pixel - upper.astype(F32)).astype(BF16)
    dap_ref[...] = (contract_rows(one_hot, upper) + contract_rows(one_hot, lower))[:images]
    sums = all_sum(3, jnp.concatenate(shifts + gains, axis=0))
    for k in range(4):
        gain = gain_ref[k : k + 1]
        from_shift = gain * sums[k : k + 1] / total_pixels
        from_gain = gain * sums[4 + k : 5 + k] / total_pixels

        @pl.loop(0, blocks)
        def _(a):
            dz_ref[k, a] = (
                inverse[k : k + 1] * (slope[k, a] * gain - from_shift - zn[k, a] * from_gain)
            ).astype(BF16)

    for k in range(5):
        piece = slice(k * width, (k + 1) * width)
        pj_ref[piece] = contract_rows(joined[:, piece], grad_final).astype(BF16)
    stat_ref[...] = jnp.concatenate([sums, shift_last, gain_last, pool_inverse] + [zero] * 5, axis=0)

    pool_rows.leave(share_of)
    for exchange in (pool_cols, pool_z, *started):
        exchange.leave()
    for m in (3, 2, 1):
        for sends, _, copy in side_copies(m) + rim_copies(m):
            pl.when(sends)(copy.wait_send)
    for copy in member_copies((0,), (0, 1)):
        copy.wait()
    for copy in member_copies(range(1, 8), (0, 1)):
        copy.wait_send()
    for l in range(2):
        for step, (dy, dx, dk) in enumerate(members):
            if step:
                y, x, k = lax.rem(r + dy, 2), lax.rem(c // 2 + dx, 2), lax.rem(c + dk, 2)
                there = xsub_ref.at[l, y * cols + 2 * x + k]
                pltpu.make_async_remote_copy(
                    src_ref=there,
                    dst_ref=there,
                    send_sem=xsend.at[l, step],
                    recv_sem=xrecv.at[l, y * cols + 2 * x + k],
                    device_id=(2 * (r // 2) + y, 2 * x + k),
                    device_id_type=MESH,
                ).wait_recv()


def forward_call(rows, cols, image_count, x, order, back, ids, wat, wpt, wpl, wpj, gain, shift, cot, counts):
    pixels, channels = x.shape
    width = wpt.shape[1]
    blocks, rb = 4, pixels // 4
    images = counts.shape[0]
    share = channels // rows
    total_pixels = float(pixels * rows * cols)
    vmem = pl.BlockSpec(memory_space=pltpu.VMEM)
    hbm = pl.BlockSpec(memory_space=pl.ANY)

    def each(shape, kind):
        return [pltpu.VMEM(shape(m) + (width,), kind) for m in (1, 2, 3)]

    dma = pltpu.SemaphoreType.DMA
    return pl.pallas_call(
        functools.partial(forward_kernel, rows, cols, float(image_count), total_pixels),
        out_shape=(
            jax.ShapeDtypeStruct((pixels, width), BF16),
            jax.ShapeDtypeStruct((4, blocks, rb, width), BF16),
            jax.ShapeDtypeStruct((5 * width, width), BF16),
            jax.ShapeDtypeStruct((16, width), F32),
            jax.ShapeDtypeStruct((images, share), BF16),
            jax.ShapeDtypeStruct((images, width), F32),
            jax.ShapeDtypeStruct((images, width), F32),
            jax.ShapeDtypeStruct((images, width), F32),
            jax.ShapeDtypeStruct((2, 8, pixels, share // 2), BF16),
        ),
        in_specs=[vmem, vmem, vmem, vmem, hbm, vmem, hbm, vmem, vmem, vmem, vmem, vmem],
        out_specs=(vmem,) * 8 + (hbm,),
        scratch_shapes=[
            pltpu.VMEM((pixels, channels), BF16),
            pltpu.VMEM((blocks + 2 * REACH, ids.shape[0], 128), F32),
            pltpu.VMEM((SLOTS, channels, width), BF16),
            pltpu.VMEM((share, width), BF16),
            each(lambda m: (3, blocks + 2 * m, rb), F32),
            each(lambda m: (blocks, 2 * HALO[m] + rb), F32),
            each(lambda m: (2, 3, m, rb), BF16), each(lambda m: (2, 3, m, rb), BF16),
            each(lambda m: (2, blocks, HALO[m]), BF16), each(lambda m: (2, blocks, HALO[m]), BF16),
            pltpu.VMEM((4, blocks, rb, width), F32),
            pltpu.VMEM((4, blocks, rb, width), F32),
            pltpu.VMEM((pixels, 5 * width), BF16),
            pltpu.VMEM((pixels, width), F32),
            pltpu.VMEM((pixels, width), F32),
            pltpu.VMEM((pixels, width), BF16),
            pltpu.VMEM((images, channels), F32),
            pltpu.VMEM((4, cols, 8, width), F32),
            pltpu.VMEM((4, rows, 8, width), F32),
            pltpu.VMEM((rows, images, share), F32),
            pltpu.VMEM((cols, images, share), F32),
            pltpu.VMEM((rows, images, width), F32),
            dma((SLOTS,)), dma,
            dma((3, 2)), dma((3, 2)), dma((3, 2)), dma((3, 2)),
            dma((4, cols)), dma((4, cols)),
            dma((4, rows)), dma((4, rows)),
            dma((rows,)), dma((rows,)),
            dma((cols,)), dma((cols,)),
            dma((rows,)), dma((rows,)),
            dma((2, 8)), dma((2, 8)),
        ],
        compiler_params=pltpu.CompilerParams(
            collective_id=0, has_side_effects=True, vmem_limit_bytes=60 * 2**20
        ),
        cost_estimate=pl.CostEstimate(flops=2 * pixels * channels * width * 28, bytes_accessed=40_000_000, transcendentals=0),
    )(x, order, back, ids, wat, wpt, wpl, wpj, gain, shift, cot, counts)


def backward_kernel(
    rows, cols, image_count, height,
    dz_ref, xsub_ref, ids_ref, wat_ref, wpt_ref, wpl_ref, gain_ref, counts_ref,
    pooled_ref, pooln_ref, pools_ref, dap_ref, stat_ref, back_ref, pj_ref,
    gx_ref, dw_ref, dpoint_ref, gpool_ref, gstat_ref, gproj_ref,
    ext0, ext1, ext2, ext3, shifted, colmask, idrep, gmat, gown, xt, acc, wbuf, wpt,
    send1, recv1, keep, relay, dw, pcbuf, prbuf, quarters, quarter_sums, row_parts, final_parts,
    xsem, wsem, wptsem, zsend, zrecv, agsend, agrecv, s1send, s1recv, s2send, s2recv, s3send, s3recv,
    pcsend, pcrecv, prsend, prrecv, qsend, qrecv, rqsend, rqrecv, fqsend, fqrecv, outsem,
):
    r, c = lax.axis_index("rows"), lax.axis_index("cols")
    z, y = r // 2, lax.rem(r, 2)
    x, k = c // 2, lax.rem(c, 2)
    levels = rows // 2
    z_lo, z_hi = lax.rem(z, 2), z // 2
    blocks, rb, width = dz_ref.shape[1:]
    pair = 2 * rb
    across = cols * blocks
    pixels = blocks * rb
    own = REACH * 36
    half = xt.shape[0] // 2
    images = dap_ref.shape[0]
    ext = {0: ext0, 1: ext1, 2: ext2, 3: ext3}
    tall = {0: 0, **HALO}

    def x_copy(l, dev, a):
        dev_y, dev_c = dev // cols, lax.rem(dev, cols)
        start = pl.multiple_of((dev_c * blocks + a) * pair + dev_y * rb, 16)
        return pltpu.make_async_copy(
            xsub_ref.at[l, dev, a], gmat.at[pl.ds(start, rb), pl.ds(l * half, half)], xsem.at[l, dev, a]
        )

    for l in range(2):
        for a in range(blocks):
            @pl.loop(0, 2 * cols)
            def _(dev):
                x_copy(l, dev, a).start()

    groups = [[(0, 4), (1, 4), (2, 4)]]
    for m in (1, 2, 3):
        groups += [[(m - 1, 0), (m - 1, 1), (m - 1, 2)], [(m - 1, 6), (m - 1, 7), (m - 1, 8)], [(m - 1, 3), (m - 1, 5)]]

    def weight_copies(n):
        return [
            pltpu.make_async_copy(
                wat_ref.at[branch, tap], wbuf.at[n % 2, :, pl.ds(place * width, width)], wsem.at[n % 2, place]
            )
            for place, (branch, tap) in enumerate(groups[n])
        ]

    point_copy = pltpu.make_async_copy(wpt_ref, wpt, wptsem)
    point_copy.start()
    for n in range(2):
        for copy in weight_copies(n):
            copy.start()

    greet_all(rows, cols, r, c)

    def has_rim(dev_y):
        return (dev_y == 1) & (z >= 1) | (dev_y == 0) & (z <= levels - 2)

    def rim_copy(m, sending):
        high = tall[m]
        start = pl.multiple_of(y * (rb - high), 16)
        target = pl.multiple_of((1 - y) * (high + pair), 16)
        return pltpu.make_async_remote_copy(
            src_ref=dz_ref.at[m, :, pl.ds(start, high)],
            dst_ref=ext[m].at[pl.ds(c * blocks, blocks), pl.ds(target, high)],
            send_sem=zsend.at[m],
            recv_sem=zrecv.at[m],
            device_id=(lax.rem(r + 4 * y - 2 + rows, rows), c),
            device_id_type=MESH,
        )

    sends_rim = (y == 1) & (z <= levels - 2) | (y == 0) & (z >= 1)

    def item(m, kind, dev_y, dev_c, first=0, count=None):
        high = tall[m]
        count = blocks if count is None else count
        start = high + rb * dev_y if kind == 0 else (1 - dev_y) * (high + pair)
        height = rb if kind == 0 else high
        return ext[m].at[pl.ds(dev_c * blocks + first, count), pl.ds(pl.multiple_of(start, 16), height)]

    def gather_copy(m, kind, dev_y, dev_c, slot, target, first=0, count=None):
        piece = item(m, kind, dev_y, dev_c, first, count)
        return pltpu.make_async_remote_copy(
            src_ref=piece,
            dst_ref=piece,
            send_sem=agsend.at[m, kind, slot],
            recv_sem=agrecv.at[m, kind, 2 * cols if first else dev_y * cols + dev_c],
            device_id=target,
            device_id_type=MESH,
        )

    most = blocks // 2
    side = 2 * (1 - x) + k
    sibling, beside, below = (r, 2 * x + 1 - k), (r, side), (2 * z + 1 - y, c)

    def if_there(kind, dev_y, action):
        if kind == 0:
            action()
        else:
            pl.when(has_rim(dev_y))(action)

    def kinds(m):
        return (0,) if m == 0 else (0, 1)

    def own_copies(m, kind):
        return [gather_copy(m, kind, y, c, slot, to) for slot, to in enumerate((beside, below, sibling))]

    def side_copies(m, kind):
        return [gather_copy(m, kind, y, side, 3, below, 0, most), gather_copy(m, kind, y, side, 5, sibling)]

    def below_copies(m, kind):
        return [
            gather_copy(m, kind, 1 - y, c, 4, beside, most, blocks - most),
            gather_copy(m, kind, 1 - y, c, 6, sibling),
        ]

    def diagonal_copies(m, kind):
        return [gather_copy(m, kind, 1 - y, side, 7, sibling)]

    def start_own(m, kind):
        if kind == 0:
            high = tall[m]
            for a in range(blocks):
                ext[m][c * blocks + a, pl.ds(pl.multiple_of(high + rb * y, 16), rb)] = dz_ref[m, a]

        def action():
            if kind == 1:
                rim_copy(m, False).wait_recv()
            for copy in own_copies(m, kind):
                copy.start()

        if_there(kind, y, action)

    def pass_on(m):
        for kind in kinds(m):
            def from_side():
                gather_copy(m, kind, y, side, 0, beside).wait_recv()
                for copy in side_copies(m, kind):
                    copy.start()

            def from_below():
                gather_copy(m, kind, 1 - y, c, 0, below).wait_recv()
                for copy in below_copies(m, kind):
                    copy.start()

            if_there(kind, y, from_side)
            if_there(kind, 1 - y, from_below)

    def pass_last(m):
        for kind in kinds(m):
            def action():
                gather_copy(m, kind, 1 - y, side, 0, below, 0, most).wait_recv()
                gather_copy(m, kind, 1 - y, side, 0, beside, most, blocks - most).wait_recv()
                for copy in diagonal_copies(m, kind):
                    copy.start()

            if_there(kind, 1 - y, action)

    def finish_gather(m):
        for kind in kinds(m):
            for dev_y in (y, 1 - y):
                for dev_c in (c, side):
                    piece = gather_copy(m, kind, dev_y, dev_c + 1 - 2 * k, 0, sibling)
                    if_there(kind, dev_y, piece.wait_recv)

    def finish_sends(m):
        for kind in kinds(m):
            def action():
                for copy in own_copies(m, kind) + side_copies(m, kind):
                    copy.wait_send()

            def below_action():
                for copy in below_copies(m, kind) + diagonal_copies(m, kind):
                    copy.wait_send()

            if_there(kind, y, action)
            if_there(kind, 1 - y, below_action)

    for m in (1, 2, 3):
        pl.when(sends_rim)(rim_copy(m, True).start)
    start_own(1, 0)

    pool_cols = Exchange(cols, c, lambda other: (r, other), pcbuf, pcsend, pcrecv)
    pcbuf[c] = dap_ref[...]
    pool_cols.start()

    tall_piece, wide_piece = quarters.shape[2], quarters.shape[3]

    def quarter(other):
        rows_of = pl.ds(pl.multiple_of(lax.rem(other, 2) * tall_piece, 16), tall_piece)
        return pj_ref.at[:, rows_of, pl.ds(pl.multiple_of(other // 2 * wide_piece, 128), wide_piece)]

    proj_cols = Exchange(cols, c, lambda other: (r, other), quarters, qsend, qrecv)
    proj_rows = Exchange(rows, r, lambda other: (other, c), row_parts, rqsend, rqrecv)
    proj_last = Exchange(cols, c, lambda other: (r, other), final_parts, fqsend, fqrecv)
    own_rows = pl.ds(pl.multiple_of(k * tall_piece, 16), tall_piece)
    quarters[c] = pj_ref[:, own_rows, pl.ds(pl.multiple_of(x * wide_piece, 128), wide_piece)]
    proj_cols.start(quarter)

    def whole_sum(slots, count):
        value = slots[0].astype(F32)
        for other in range(1, count):
            value = value + slots[other].astype(F32)
        return value

    def proj_down():
        proj_cols.arrive()
        quarter_sums[...] = whole_sum(quarters, cols).astype(BF16)
        row_parts[r] = quarter_sums[r]
        proj_rows.start(lambda other: quarter_sums.at[other])

    def proj_spread():
        proj_rows.arrive()
        final_parts[c] = whole_sum(row_parts, rows).astype(BF16)
        proj_last.start()

    for block in range(across):
        idrep[block] = jnp.broadcast_to(ids_ref[:, block : block + 1], idrep.shape[1:])
    for m in (1, 2, 3):
        high = tall[m]

        @pl.when(z == 0)
        def _():
            @pl.loop(0, across)
            def _(block):
                ext[m][block, 0:high] = jnp.zeros((high, width), BF16)

        @pl.when(z == levels - 1)
        def _():
            @pl.loop(0, across)
            def _(block):
                ext[m][block, high + pair : 2 * high + pair] = jnp.zeros((high, width), BF16)

    for shift in range(-REACH, REACH + 1):
        for block in range(across):
            if 0 <= block - shift < across:
                same = idrep[block, own : own + 48] == idrep[block - shift, own : own + 48]
                colmask[REACH + shift, block] = wide(same.astype(F32), width).astype(BF16)
            else:
                colmask[REACH + shift, block] = jnp.zeros((48, width), BF16)

    start_own(1, 1)
    start_own(2, 0)
    start_own(2, 1)
    for l in range(2):
        for a in range(blocks):
            @pl.loop(0, 2 * cols)
            def _(dev):
                x_copy(l, dev, a).wait()

        spot = pl.multiple_of(lax.rem(l + z_lo, 2) * half, half)
        for chunk in range(gmat.shape[0] // 128):
            piece = slice(chunk * 128, (chunk + 1) * 128)
            xt[pl.ds(spot, half), piece] = gmat[piece, l * half : (l + 1) * half].astype(F32).T.astype(BF16)

    pass_on(1)
    start_own(3, 0)
    start_own(3, 1)

    point_copy.wait()

    @pl.loop(0, wpt.shape[0] // 256)
    def _(n):
        piece = pl.ds(pl.multiple_of(n * 256, 256), 256)
        left = jnp.concatenate([dz_ref[0, a] for a in range(blocks)], axis=0)
        acc[:, piece] = contract_lanes(left, wpt[piece, :])

    pool_copy = pltpu.make_async_copy(wpl_ref, wpt, wptsem)
    pool_copy.start()

    def build_shifted(m):
        high = tall[m]

        @pl.loop(0, across)
        def _(block):
            whole = ext[m][block].astype(F32)
            for i in range(3):
                down = (i - 1) * 36 * m
                value = whole[high - down : high - down + pair]
                if i != 1:
                    same = idrep[block, own : own + pair] == idrep[block, own - down : own - down + pair]
                    value = jnp.where(wide(same.astype(F32), width) > 0.0, value, 0.0)
                shifted[i, block] = value.astype(BF16)

    def masked(values, mask):
        count = values.shape[0] // 48
        return jnp.concatenate([values[48 * n : 48 * (n + 1)] * mask for n in range(count)], axis=0)

    def scatter_first(n, part):
        keep[n] = part[:half]
        send1[n] = part[half:].astype(BF16)
        stage1(n).start()

    def stage1(n):
        return pltpu.make_async_remote_copy(
            src_ref=send1.at[n], dst_ref=recv1.at[n], send_sem=s1send.at[n], recv_sem=s1recv.at[n],
            device_id=(r + 2 - 4 * z_lo, c), device_id_type=MESH,
        )

    def stage2(n):
        return pltpu.make_async_remote_copy(
            src_ref=relay.at[n], dst_ref=relay.at[n], send_sem=s2send.at[n], recv_sem=s2recv.at[n],
            device_id=(lax.rem(r + rows // 2, rows), c), device_id_type=MESH,
        )

    def stage3(n, from_x, slot, target):
        piece = dw.at[n, pl.ds(pl.multiple_of(from_x * half, half), half)]
        return pltpu.make_async_remote_copy(
            src_ref=piece, dst_ref=piece, send_sem=s3send.at[slot, n], recv_sem=s3recv.at[from_x, n],
            device_id=target, device_id_type=MESH,
        )

    last = z_hi == k

    def drain2(start, count):
        @pl.loop(start, start + count)
        def _(n):
            stage1(n).wait_recv()
            total = keep[n] + recv1[n].astype(F32)

            @pl.when(last)
            def _():
                keep[n] = total

            @pl.when(jnp.logical_not(last))
            def _():
                relay[n] = total.astype(BF16)
                stage2(n).start()

    def drain3(start, count):
        @pl.when(last)
        def _():
            @pl.loop(start, start + count)
            def _(n):
                stage2(n).wait_recv()
                dw[n, pl.ds(pl.multiple_of(x * half, half), half)] = (keep[n] + relay[n].astype(F32)).astype(BF16)
                stage3(n, x, 0, beside).start()
                stage3(n, x, 1, sibling).start()

    def drain4(start, count):
        @pl.when(last)
        def _():
            @pl.loop(start, start + count)
            def _(n):
                copy = stage3(n, 1 - x, 2, sibling)
                copy.wait_recv()
                copy.start()

        @pl.when(jnp.logical_not(last))
        def _():
            @pl.loop(start, start + count)
            def _(n):
                stage3(n, 0, 0, sibling).wait_recv()
                stage3(n, 1, 0, sibling).wait_recv()

    def weight_grad(m, between):
        @pl.loop(0, 9)
        def _(tap):
            for when, action in between.items():
                pl.when(tap == when)(action)
            i, j = tap // 3, lax.rem(tap, 3)
            shift = (j - 1) * m

            @pl.loop(0, across)
            def _(block):
                source = lax.rem(block - shift + across, across)
                gmat[pl.ds(pl.multiple_of(block * pair, 16), pair)] = masked(
                    shifted[i, source], colmask[REACH + shift, block]
                )

            scatter_first((m - 1) * 9 + tap, jnp.dot(xt[...], gmat[...], preferred_element_type=F32))

    def add_products(n, depth):
        for copy in weight_copies(n):
            copy.wait()

        @pl.loop(0, wbuf.shape[1] // 256)
        def _(chunk):
            piece = pl.ds(pl.multiple_of(chunk * 256, 256), 256)
            acc[:, piece] += contract_lanes(gown[:, :depth], wbuf[n % 2, piece, :depth])

        if n + 2 < len(groups):
            for copy in weight_copies(n + 2):
                copy.start()

    def feature_grad(m, lines):
        for line in lines:
            n = 1 + (m - 1) * 3 + line
            for place, (_, tap) in enumerate(groups[n]):
                i, j = tap // 3, tap % 3
                shift = (j - 1) * m
                for a in range(blocks):
                    block = c * blocks + a
                    source = lax.rem(block - shift + across, across)
                    gown[a * rb : (a + 1) * rb, place * width : (place + 1) * width] = masked(
                        shifted[i, source, pl.ds(pl.multiple_of(y * rb, 16), rb)], colmask[REACH + shift, block]
                    )
            add_products(n, len(groups[n]) * width)

    for m in (1, 2, 3):
        for a in range(blocks):
            gown[a * rb : (a + 1) * rb, (m - 1) * width : m * width] = dz_ref[m, a]
    add_products(0, 3 * width)
    pass_last(1)
    finish_gather(1)
    build_shifted(1)

    def second_on():
        pass_on(2)
        start_own(0, 0)

    weight_grad(1, {4: second_on, 7: proj_down})
    pass_last(2)
    feature_grad(1, (0,))
    pass_on(3)
    drain2(0, 9)
    feature_grad(1, (1, 2))
    finish_gather(2)
    build_shifted(2)

    def third_last():
        pass_on(0)
        pass_last(3)

    weight_grad(2, {2: proj_spread, 5: third_last})
    pass_last(0)
    drain3(0, 9)
    feature_grad(2, (0,))
    drain2(9, 9)
    feature_grad(2, (1, 2))
    finish_gather(3)
    build_shifted(3)
    weight_grad(3, {})
    finish_gather(0)

    @pl.loop(0, across)
    def _(block):
        gmat[pl.ds(pl.multiple_of(block * pair, 16), pair)] = ext0[block]

    scatter_first(27, jnp.dot(xt[...], gmat[...], preferred_element_type=F32))
    drain4(0, 9)
    drain3(9, 9)

    pool_cols.arrive()
    pool_rows = Exchange(rows, r, lambda other: (other, c), prbuf, prsend, prrecv)
    prbuf[r] = pool_cols.total()
    pool_rows.start()
    feature_grad(3, (0, 1))
    drain2(18, 10)
    feature_grad(3, (2,))
    drain4(9, 9)
    pool_rows.arrive()
    normed = pooln_ref[...]
    grad = pool_rows.total() * pools_ref[...]
    shift_sum = jnp.sum(grad, axis=0, keepdims=True)
    gain_sum = jnp.sum(grad * normed, axis=0, keepdims=True)
    gain = gain_ref[4:5]
    grad_z = (
        stat_ref[10:11]
        * (grad * gain - gain * shift_sum / image_count - normed * (gain * gain_sum / image_count))
    ).astype(BF16)
    gpool_ref[...] = contract_rows(pooled_ref[...], grad_z)
    gstat_ref[...] = jnp.concatenate([shift_sum, gain_sum] + [jnp.zeros((1, width), F32)] * 6, axis=0)
    own_ids = jnp.concatenate([idrep[c * blocks + a, own : own + pair] for a in range(blocks)], axis=0)
    upper_row = jnp.broadcast_to((y == 0).astype(F32), (pixels, 128))
    own_ids = jnp.where(
        upper_row > 0.0,
        jnp.concatenate([own_ids[a * pair : a * pair + rb] for a in range(blocks)], axis=0),
        jnp.concatenate([own_ids[a * pair + rb : (a + 1) * pair] for a in range(blocks)], axis=0),
    )
    lanes = lax.broadcasted_iota(jnp.int32, (pixels, 128), 1).astype(F32)
    one_hot = (own_ids == lanes).astype(F32).astype(BF16)
    counts = wide(counts_ref[...], 256)
    pool_copy.wait()

    @pl.loop(0, wpt.shape[0] // 256)
    def _(n):
        piece = pl.ds(pl.multiple_of(n * 256, 256), 256)
        back = contract_lanes(grad_z, wpt[piece, :]) / counts
        back = jnp.concatenate([back, jnp.zeros((128 - images, 256), F32)], axis=0).astype(BF16)
        value = (acc[:, piece] + jnp.dot(one_hot, back, preferred_element_type=F32)).astype(BF16)
        gx_ref[:, piece] = jnp.dot(back_ref[...], value, preferred_element_type=F32).astype(BF16)

    drain3(18, 10)
    drain4(18, 10)
    results = (
        pltpu.make_async_copy(dw.at[pl.ds(0, 27)], dw_ref, outsem.at[0]),
        pltpu.make_async_copy(dw.at[27], dpoint_ref, outsem.at[1]),
    )
    for result in results:
        result.start()

    pool_cols.leave()
    pool_rows.leave()
    proj_last.arrive()
    for other in range(cols):
        piece_rows = slice(other % 2 * tall_piece, (other % 2 + 1) * tall_piece)
        gproj_ref[piece_rows, other // 2 * wide_piece : (other // 2 + 1) * wide_piece] = final_parts[other].astype(F32)
    proj_cols.leave(quarter)
    proj_rows.leave(lambda other: quarter_sums.at[other])
    proj_last.leave()
    for m in (1, 2, 3):
        pl.when(sends_rim)(rim_copy(m, True).wait_send)
    for m in (1, 2, 3, 0):
        finish_sends(m)

    @pl.loop(0, 28)
    def _(n):
        stage1(n).wait_send()

        @pl.when(last)
        def _():
            stage3(n, x, 0, beside).wait_send()
            stage3(n, x, 1, sibling).wait_send()
            stage3(n, 1 - x, 2, sibling).wait_send()

        @pl.when(jnp.logical_not(last))
        def _():
            stage2(n).wait_send()

    for result in results:
        result.wait()


def backward_call(
    rows, cols, image_count, dz, xsub, ids, wat, wpt, wpl, gain, counts, pooled, pooln, pools, dap, stat, back, proj
):
    _, blocks, rb, width = dz.shape
    channels = wpt.shape[0]
    share = channels // rows
    pair, across, pixels = 2 * rb, cols * blocks, blocks * rb
    images = dap.shape[0]
    group = pair * across
    vmem = pl.BlockSpec(memory_space=pltpu.VMEM)
    hbm = pl.BlockSpec(memory_space=pl.ANY)
    dma = pltpu.SemaphoreType.DMA
    taps = 28

    def ext(high):
        return pltpu.VMEM((across, 2 * high + pair, width), BF16)

    return pl.pallas_call(
        functools.partial(backward_kernel, rows, cols, float(image_count), rb),
        out_shape=(
            jax.ShapeDtypeStruct((pixels, channels), BF16),
            jax.ShapeDtypeStruct((taps - 1, share, width), BF16),
            jax.ShapeDtypeStruct((share, width), BF16),
            jax.ShapeDtypeStruct((share, width), F32),
            jax.ShapeDtypeStruct((8, width), F32),
            jax.ShapeDtypeStruct(proj.shape[1:], F32),
        ),
        in_specs=[vmem, hbm, vmem, hbm, hbm, hbm] + [vmem] * 9,
        out_specs=(vmem, hbm, hbm, vmem, vmem, vmem),
        scratch_shapes=[
            ext(0), ext(HALO[1]), ext(HALO[2]), ext(HALO[3]),
            pltpu.VMEM((3, across, pair, width), BF16),
            pltpu.VMEM((2 * REACH + 1, across, 48, width), BF16),
            pltpu.VMEM((across, ids.shape[0], 128), F32),
            pltpu.VMEM((group, width), BF16),
            pltpu.VMEM((pixels, 3 * width), BF16),
            pltpu.VMEM((share, group), BF16),
            pltpu.VMEM((pixels, channels), F32),
            pltpu.VMEM((2, channels, 3 * width), BF16),
            pltpu.VMEM((channels, width), BF16),
            pltpu.VMEM((taps, share // 2, width), BF16),
            pltpu.VMEM((taps, share // 2, width), BF16),
            pltpu.VMEM((taps, share // 2, width), F32),
            pltpu.VMEM((taps, share // 2, width), BF16),
            pltpu.VMEM((taps, share, width), BF16),
            pltpu.VMEM((cols, images, width), F32),
            pltpu.VMEM((rows, images, width), F32),
            pltpu.VMEM((cols, rows, proj.shape[1] // 2, width // 2), BF16),
            pltpu.VMEM((rows, proj.shape[1] // 2, width // 2), BF16),
            pltpu.VMEM((rows, proj.shape[1] // 2, width // 2), BF16),
            pltpu.VMEM((cols, proj.shape[1] // 2, width // 2), BF16),
            dma((2, 2 * cols, blocks)), dma((2, 3)), dma,
            dma((4,)), dma((4,)),
            dma((4, 2, 8)), dma((4, 2, 2 * cols + 1)),
            dma((taps,)), dma((taps,)),
            dma((taps,)), dma((taps,)),
            dma((3, taps)), dma((2, taps)),
            dma((cols,)), dma((cols,)),
            dma((rows,)), dma((rows,)),
            dma((cols,)), dma((cols,)),
            dma((rows,)), dma((rows,)),
            dma((cols,)), dma((cols,)),
            dma((2,)),
        ],
        compiler_params=pltpu.CompilerParams(
            collective_id=1, has_side_effects=True, vmem_limit_bytes=64 * 2**20
        ),
        cost_estimate=pl.CostEstimate(flops=4 * pixels * channels * width * 28, bytes_accessed=50_000_000, transcendentals=0),
    )(dz, xsub, ids, wat, wpt, wpl, gain, counts, pooled, pooln, pools, dap, stat, back, proj)


def extended(cells, sides, width):
    for axis, dim in sides:
        count = lax.axis_size(axis)
        ends = count - 1
        head = lax.slice_in_dim(cells, 0, width, axis=dim)
        tail = lax.slice_in_dim(cells, cells.shape[dim] - width, cells.shape[dim], axis=dim)
        cells = jnp.concatenate(
            [
                lax.ppermute(tail, axis, [(i, (i + 1) % count) for i in range(ends)]),
                cells,
                lax.ppermute(head, axis, [((i + 1) % count, i) for i in range(ends)]),
            ],
            axis=dim,
        )
    return cells


def image_match(window, own_ids, row_start, col_start):
    rows_here, cols_here = own_ids.shape
    section = window[row_start : row_start + rows_here, col_start : col_start + cols_here]
    return (section == own_ids).astype(jnp.float32).reshape(rows_here * cols_here, 1)


def silu_slope(preact_in):
    sigma = jax.nn.sigmoid(preact_in)
    return sigma * (1.0 + preact_in * (1.0 - sigma))


def transposed(left, right):
    return lax.dot_general(
        left, right, (((1,), (1,)), ((), ())), preferred_element_type=jnp.float32
    )


def shards(
    features, image_ids, w_point, w_atrous, w_pool, w_proj, norm_gain, norm_shift, cotangent
):
    rows_here, cols_here, channels = features.shape
    branch_width = w_point.shape[1]
    pixels = rows_here * cols_here
    grid_rows, grid_cols = image_ids.shape
    total_pixels = float(grid_rows * grid_cols)
    image_count = grid_rows // 16 * (grid_cols // 32)
    dilations = (RATE_LOW, RATE_MID, RATE_TOP)
    margin = RATE_TOP
    row_index = lax.axis_index("rows")
    col_index = lax.axis_index("cols")
    id_padded = jnp.pad(image_ids, margin, constant_values=-1)
    window = lax.dynamic_slice(
        id_padded,
        (row_index * rows_here, col_index * cols_here),
        (rows_here + 2 * margin, cols_here + 2 * margin),
    )
    own_ids = window[margin : margin + rows_here, margin : margin + cols_here]
    own_flat = own_ids.reshape(pixels)
    flattened = features.reshape(pixels, channels)
    padded = extended(features, (("rows", 0), ("cols", 1)), margin)
    one_hot = (own_flat[:, None] == jnp.arange(image_count, dtype=jnp.int32)[None, :]).astype(
        jnp.bfloat16
    )
    local_sums = jnp.einsum("pn,pc->nc", one_hot, flattened, preferred_element_type=jnp.float32)
    counts = jax.ops.segment_sum(
        jnp.ones((grid_rows * grid_cols,), jnp.float32), image_ids.reshape(-1), image_count
    )
    image_totals = lax.psum(local_sums, ("rows", "cols"))
    branch_outs = [jnp.dot(flattened, w_point, preferred_element_type=jnp.float32)]
    for branch, dilation in enumerate(dilations):
        running = jnp.zeros((pixels, branch_width), jnp.float32)
        for stencil in range(9):
            row_shift = (stencil // 3 - 1) * dilation
            col_shift = (stencil % 3 - 1) * dilation
            source = padded[
                margin + row_shift : margin + row_shift + rows_here,
                margin + col_shift : margin + col_shift + cols_here,
            ].reshape(pixels, channels)
            same_image = image_match(window, own_ids, margin + row_shift, margin + col_shift)
            running = running + same_image * jnp.dot(
                source, w_atrous[branch, stencil], preferred_element_type=jnp.float32
            )
        branch_outs.append(running)
    spatial = jnp.stack(branch_outs, axis=1)
    first_sum = jnp.sum(spatial, axis=0)
    second_sum = jnp.sum(spatial * spatial, axis=0)
    first_sum, second_sum = lax.psum((first_sum, second_sum), ("rows", "cols"))
    average = first_sum / total_pixels
    inverse_std = lax.rsqrt(second_sum / total_pixels - average * average + epsilon)
    normed = (spatial - average) * inverse_std
    preact = norm_gain[:4] * normed + norm_shift[:4]
    active = jax.nn.silu(preact).astype(jnp.bfloat16)
    pooled = (image_totals / counts[:, None]).astype(jnp.bfloat16)
    pool_z = jnp.dot(pooled, w_pool, preferred_element_type=jnp.float32)
    pool_avg = jnp.mean(pool_z, axis=0)
    pool_square = jnp.mean(pool_z * pool_z, axis=0)
    pool_inverse = lax.rsqrt(pool_square - pool_avg * pool_avg + epsilon)
    pool_normed = (pool_z - pool_avg) * pool_inverse
    pool_pre = norm_gain[4] * pool_normed + norm_shift[4]
    pool_active = jax.nn.silu(pool_pre).astype(jnp.bfloat16)
    joined = jnp.concatenate(
        [active.reshape(pixels, 4 * branch_width), jnp.take(pool_active, own_flat, axis=0)], axis=1
    )
    final_z = jnp.dot(joined, w_proj, preferred_element_type=jnp.float32)
    final_first, final_second = lax.psum(
        (jnp.sum(final_z, axis=0), jnp.sum(final_z * final_z, axis=0)), ("rows", "cols")
    )
    final_avg = final_first / total_pixels
    final_inverse = lax.rsqrt(final_second / total_pixels - final_avg * final_avg + epsilon)
    final_normed = (final_z - final_avg) * final_inverse
    final_pre = norm_gain[5] * final_normed + norm_shift[5]
    output = jax.nn.silu(final_pre).astype(jnp.bfloat16).reshape(rows_here, cols_here, branch_width)
    upstream = cotangent.reshape(pixels, branch_width).astype(jnp.float32)
    grad_final = upstream * silu_slope(final_pre)
    shift_last, gain_last = lax.psum(
        (jnp.sum(grad_final, axis=0), jnp.sum(grad_final * final_normed, axis=0)), ("rows", "cols")
    )
    grad_final_z = (
        final_inverse
        * (
            grad_final * norm_gain[5]
            - norm_gain[5] * shift_last / total_pixels
            - final_normed * (norm_gain[5] * gain_last / total_pixels)
        )
    ).astype(jnp.bfloat16)
    proj_term = jnp.einsum("pk,pc->kc", joined, grad_final_z, preferred_element_type=jnp.float32)
    grad_joined = transposed(grad_final_z, w_proj)
    grad_pre = grad_joined[:, : 4 * branch_width].reshape(pixels, 4, branch_width) * silu_slope(
        preact
    )
    grad_pixel = grad_joined[:, 4 * branch_width :]
    shift_sums = jnp.sum(grad_pre, axis=0)
    gain_sums = jnp.sum(grad_pre * normed, axis=0)
    image_grads = jax.ops.segment_sum(grad_pixel, own_flat, image_count)
    shift_sums, gain_sums, image_grads = lax.psum(
        (shift_sums, gain_sums, image_grads), ("rows", "cols")
    )
    grad_branch = (
        inverse_std
        * (
            grad_pre * norm_gain[:4]
            - norm_gain[:4] * shift_sums / total_pixels
            - normed * (norm_gain[:4] * gain_sums / total_pixels)
        )
    ).astype(jnp.bfloat16)
    grad_pool_pre = image_grads * silu_slope(pool_pre)
    pool_shift = jnp.sum(grad_pool_pre, axis=0)
    pool_gain = jnp.sum(grad_pool_pre * pool_normed, axis=0)
    grad_pool_z = (
        pool_inverse
        * (
            grad_pool_pre * norm_gain[4]
            - norm_gain[4] * pool_shift / image_count
            - pool_normed * (norm_gain[4] * pool_gain / image_count)
        )
    ).astype(jnp.bfloat16)
    row_share = channels // lax.axis_size("rows")
    pool_columns = lax.dynamic_slice_in_dim(pooled, row_index * row_share, row_share, 1)
    grad_pool = jnp.einsum(
        "nk,nc->kc", pool_columns, grad_pool_z, preferred_element_type=jnp.float32
    )
    grad_pooled = transposed(grad_pool_z, w_pool) / counts[:, None]
    grad_input = jnp.take(grad_pooled, own_flat, axis=0) + transposed(grad_branch[:, 0], w_point)
    point_term = jnp.einsum(
        "pk,pc->kc", flattened, grad_branch[:, 0], preferred_element_type=jnp.float32
    )
    stacked = grad_branch[:, 1:].reshape(rows_here, cols_here, 3 * branch_width)
    grad_padded = extended(stacked, (("rows", 0), ("cols", 1)), margin)
    rim_list = [
        grad_padded[:, :, branch * branch_width : (branch + 1) * branch_width]
        for branch in range(3)
    ]
    rim_bases = [margin, margin, margin]
    atrous_terms = []
    for branch, dilation in enumerate(dilations):
        tap_terms = []
        rim_base = rim_bases[branch]
        for stencil in range(9):
            row_shift = (stencil // 3 - 1) * dilation
            col_shift = (stencil % 3 - 1) * dilation
            source = padded[
                margin + row_shift : margin + row_shift + rows_here,
                margin + col_shift : margin + col_shift + cols_here,
            ].reshape(pixels, channels)
            same_image = image_match(window, own_ids, margin + row_shift, margin + col_shift)
            masked = same_image.astype(jnp.bfloat16) * grad_branch[:, branch + 1]
            tap_terms.append(
                jnp.einsum("pk,pc->kc", source, masked, preferred_element_type=jnp.float32)
            )
            incoming = rim_list[branch][
                rim_base - row_shift : rim_base - row_shift + rows_here,
                rim_base - col_shift : rim_base - col_shift + cols_here,
            ].reshape(pixels, branch_width)
            back_image = image_match(window, own_ids, margin - row_shift, margin - col_shift)
            grad_input = grad_input + back_image * transposed(incoming, w_atrous[branch, stencil])
        atrous_terms.append(jnp.stack(tap_terms))
    atrous_term = jnp.stack(atrous_terms)
    shared = (
        lax.psum_scatter(
            point_term.astype(jnp.bfloat16), "rows", scatter_dimension=0, tiled=True
        ).astype(jnp.float32),
        lax.psum_scatter(
            atrous_term.astype(jnp.bfloat16), "rows", scatter_dimension=2, tiled=True
        ).astype(jnp.float32),
        lax.psum_scatter(
            proj_term.astype(jnp.bfloat16), "rows", scatter_dimension=0, tiled=True
        ).astype(jnp.float32),
    )
    shared = (
        lax.psum(shared[0].astype(jnp.bfloat16), "cols").astype(jnp.float32),
        lax.psum(shared[1].astype(jnp.bfloat16), "cols").astype(jnp.float32),
        lax.psum(shared[2].astype(jnp.bfloat16), "cols").astype(jnp.float32),
    )
    grad_gain = jnp.concatenate([gain_sums, pool_gain[None], gain_last[None]], axis=0)
    grad_shift = jnp.concatenate([shift_sums, pool_shift[None], shift_last[None]], axis=0)
    grad_features = grad_input.astype(jnp.bfloat16).reshape(rows_here, cols_here, channels)
    return (
        output,
        grad_features,
        shared[0],
        shared[1],
        grad_pool,
        shared[2],
        grad_gain,
        grad_shift,
    )


def block_order(height, breadth):
    pixel = np.arange(height * breadth).reshape(height, breadth // STEP, STEP).transpose(1, 0, 2).reshape(-1)
    return np.eye(height * breadth, dtype=np.float32)[pixel]


def id_columns(ids):
    height, breadth = ids.shape
    table = ids.reshape(height, breadth // STEP, STEP).transpose(0, 2, 1).reshape(height * STEP, breadth // STEP)
    return jnp.pad(table.astype(F32), ((0, 0), (0, 128 - breadth // STEP)))


def quick_shards(
    features, image_ids, w_point, w_atrous, w_pool, w_proj, norm_gain, norm_shift, cotangent
):
    rows_here, cols_here, channels = features.shape
    branch_width = w_point.shape[1]
    pixels = rows_here * cols_here
    grid_rows, grid_cols = image_ids.shape
    image_count = grid_rows // 16 * (grid_cols // 32)
    images = -(-image_count // 16) * 16
    margin = RATE_TOP
    rows, cols = lax.axis_size("rows"), lax.axis_size("cols")
    row_index = lax.axis_index("rows")
    col_index = lax.axis_index("cols")
    id_padded = jnp.pad(image_ids, margin, constant_values=-1)
    window = lax.dynamic_slice(
        id_padded,
        (row_index * rows_here, col_index * cols_here),
        (rows_here + 2 * margin, cols_here + 2 * margin),
    )
    own_ids = window[margin : margin + rows_here, margin : margin + cols_here]
    own_flat = own_ids.reshape(pixels)
    counts = jnp.sum(
        (image_ids.reshape(-1, 1) == jnp.arange(images, dtype=jnp.int32)[None, :]).astype(F32), axis=0
    )
    counts = jnp.maximum(counts, 1.0)
    count_table = jnp.broadcast_to(counts[:, None], (images, 128))
    order = block_order(rows_here, cols_here)
    order, back = jnp.asarray(order, BF16), jnp.asarray(order.T, BF16)
    output, dz, proj_term, stats, pooled, pool_normed, pool_slope, dap, xsub = forward_call(
        rows, cols, image_count, features.reshape(pixels, channels), order, back, id_columns(window), w_atrous, w_point, w_pool, w_proj,
        norm_gain, norm_shift, cotangent.reshape(pixels, branch_width), count_table,
    )
    output = output.reshape(rows_here, cols_here, branch_width)
    pair_window = lax.dynamic_slice(
        id_padded,
        (row_index // 2 * (2 * rows_here), jnp.int32(margin)),
        (2 * rows_here + 2 * margin, grid_cols),
    )
    grad_input, atrous, point, grad_pool, pool_sums, grad_proj = backward_call(
        rows, cols, image_count, dz, xsub.reshape(2, 8, 4, pixels // 4, -1), id_columns(pair_window), w_atrous, w_point, w_pool,
        norm_gain, count_table, pooled, pool_normed, pool_slope, dap, stats, back, proj_term.reshape(rows, -1, branch_width),
    )
    grad_atrous = atrous.astype(F32).reshape(3, 9, channels // rows, branch_width)

    grad_gain = jnp.concatenate([stats[4:8], pool_sums[1:2], stats[9:10]], axis=0)
    grad_shift = jnp.concatenate([stats[0:4], pool_sums[0:1], stats[8:9]], axis=0)
    grad_features = grad_input.reshape(rows_here, cols_here, channels)
    return (
        output, grad_features, point.astype(F32), grad_atrous, grad_pool,
        grad_proj, grad_gain, grad_shift,
    )


def solution(mesh):
    placed = (P("rows", "cols", None), P(), P(), P(), P(), P(), P(), P(), P("rows", "cols", None))
    quick = mesh.shape["rows"] == 8 and mesh.shape["cols"] == 4
    return jax.shard_map(
        quick_shards if quick else shards,
        mesh=mesh,
        in_specs=placed,
        out_specs=(
            P("rows", "cols", None),
            P("rows", "cols", None),
            P("rows", None),
            P(None, None, "rows", None),
            P("rows", None),
            P("rows", None),
            P(),
            P(),
        ),
        check_vma=False,
    )
```

```python
import functools
import jax
import jax.numpy as jnp
import numpy as np
from jax import lax
from jax.experimental import pallas as pl
from jax.experimental.pallas import tpu as pltpu
from jax.sharding import PartitionSpec as P

MESH = pl.DeviceIdType.MESH
RATE_LOW = 6
RATE_MID = 12
RATE_TOP = 18
STEP = RATE_LOW
REACH = RATE_TOP // STEP
HALO = {1: 48, 2: 80, 3: 112}
SLOTS = 4
epsilon = 1e-05
F32 = jnp.float32
BF16 = jnp.bfloat16


def wide(column, width):
    return jnp.concatenate([column] * (width // column.shape[-1]), axis=-1)


def silu_parts(preact):
    sigma = jax.nn.sigmoid(preact)
    return preact * sigma, sigma * (1.0 + preact * (1.0 - sigma))


def contract_rows(left, right):
    return lax.dot_general(left, right, (((0,), (0,)), ((), ())), preferred_element_type=F32)


def contract_lanes(left, right):
    return lax.dot_general(left, right, (((1,), (1,)), ((), ())), preferred_element_type=F32)


def greet(rows, cols, r, c):
    barrier = pltpu.get_barrier_semaphore()
    near = r + 1 - 2 * lax.rem(r, 2)
    others = [(lax.rem(r + step, rows), c) for step in range(1, rows)]
    for step in range(1, cols):
        others += [(r, lax.rem(c + step, cols)), (near, lax.rem(c + step, cols))]
    for other in others:
        pl.semaphore_signal(barrier, inc=1, device_id=other, device_id_type=MESH)
    pl.semaphore_wait(barrier, len(others))


class Exchange:
    def __init__(self, axis_size, place, to_device, slots, send_sems, recv_sems):
        self.size, self.place, self.to_device = axis_size, place, to_device
        self.slots, self.send_sems, self.recv_sems = slots, send_sems, recv_sems

    def copy(self, step, source=None):
        other = lax.rem(self.place + step, self.size)
        mine = self.slots.at[self.place]
        return pltpu.make_async_remote_copy(
            src_ref=mine if source is None else source(other),
            dst_ref=mine,
            send_sem=self.send_sems.at[step],
            recv_sem=self.recv_sems.at[self.place],
            device_id=self.to_device(other),
            device_id_type=MESH,
        )

    def start(self, source=None):
        for step in range(1, self.size):
            self.copy(step, source).start()

    def arrive(self):
        for step in range(1, self.size):
            other = lax.rem(self.place + step, self.size)
            there = self.slots.at[other]
            pltpu.make_async_remote_copy(
                src_ref=there,
                dst_ref=there,
                send_sem=self.send_sems.at[step],
                recv_sem=self.recv_sems.at[other],
                device_id=self.to_device(other),
                device_id_type=MESH,
            ).wait_recv()

    def leave(self, source=None):
        for step in range(1, self.size):
            self.copy(step, source).wait_send()

    def total(self):
        value = self.slots[0]
        for other in range(1, self.size):
            value = value + self.slots[other]
        return value


def forward_kernel(
    rows, cols, image_count, total_pixels,
    raw_ref, order_ref, back_ref, ids_ref, wat_ref, wpt_ref, wpl_ref, wpj_ref, gain_ref, shift_ref, cot_ref,
    counts_ref, out_ref, dz_ref, pj_ref, stat_ref, pooled_ref, pooln_ref, pools_ref, dap_ref, xsub_ref,
    x_ref, idrep, wbuf, wplbuf, parts, sums_by_row, edge_out, edge_in, rim_out, rim_in, zn, slope, joined, zf, dzf, active, upstream, isum, cbuf, rbuf, pr_buf, pc_buf, pz_buf,
    wsem, wplsem, esend, erecv, hsend, hrecv, csend, crecv, rsend, rrecv, psend, precv, pcsend, pcrecv, pzsend, pzrecv,
    xsend, xrecv,
):
    r, c = lax.axis_index("rows"), lax.axis_index("cols")
    blocks, rb, width = zn.shape[1], zn.shape[2], zn.shape[3]
    pixels = blocks * rb
    own = REACH * 36
    images = isum.shape[0]
    taps = 27

    def weight_copy(n):
        branch, tap = 2 - n // 9, lax.rem(n, 9)
        slot = lax.rem(n, SLOTS)
        return pltpu.make_async_copy(wat_ref.at[branch, tap], wbuf.at[slot], wsem.at[slot])

    for n in range(SLOTS - 1):
        weight_copy(jnp.int32(n)).start()
    share = x_ref.shape[1] // rows
    pool_weight = pltpu.make_async_copy(
        wpl_ref.at[pl.ds(pl.multiple_of(r * share, share), share)], wplbuf, wplsem
    )
    pool_weight.start()
    for block in range(idrep.shape[0]):
        idrep[block] = jnp.broadcast_to(ids_ref[:, block : block + 1], idrep.shape[1:])
    greet(rows, cols, r, c)

    @pl.loop(0, x_ref.shape[1] // 256)
    def _(n):
        piece = pl.ds(pl.multiple_of(n * 256, 256), 256)
        x_ref[:, piece] = jnp.dot(order_ref[...], raw_ref[:, piece], preferred_element_type=F32).astype(BF16)

    own_ids = jnp.concatenate([idrep[REACH + a, own : own + rb, :] for a in range(blocks)], axis=0)
    lanes = lax.broadcasted_iota(jnp.int32, (pixels, 128), 1).astype(F32)
    one_hot = jnp.concatenate(
        [(own_ids == lanes + 128.0 * part).astype(F32).astype(BF16) for part in range(pl.cdiv(images, 128))],
        axis=1,
    )
    for part in range(rows):
        piece = slice(part * share, (part + 1) * share)
        isum[:, piece] = contract_rows(one_hot, x_ref[:, piece])[:images]
    pool_rows = Exchange(rows, r, lambda other: (other, c), pr_buf, psend, precv)

    def share_of(other):
        return isum.at[:, pl.ds(pl.multiple_of(other * share, share), share)]

    pr_buf[r] = isum[:, pl.ds(pl.multiple_of(r * share, share), share)]
    pool_rows.start(share_of)

    def side_copies(m):
        return [
            (
                (c > 0, c < cols - 1)[way],
                (c < cols - 1, c > 0)[way],
                pltpu.make_async_remote_copy(
                    src_ref=edge_out[m - 1].at[way],
                    dst_ref=edge_in[m - 1].at[way],
                    send_sem=esend.at[m - 1, way],
                    recv_sem=erecv.at[m - 1, way],
                    device_id=(r, lax.rem(c + (cols - 1, 1)[way], cols)),
                    device_id_type=MESH,
                ),
            )
            for way in range(2)
        ]

    def rim_copies(m):
        return [
            (
                (r > 0, r < rows - 1)[way],
                (r < rows - 1, r > 0)[way],
                pltpu.make_async_remote_copy(
                    src_ref=rim_out[m - 1].at[way],
                    dst_ref=rim_in[m - 1].at[way],
                    send_sem=hsend.at[m - 1, way],
                    recv_sem=hrecv.at[m - 1, way],
                    device_id=(lax.rem(r + (rows - 1, 1)[way], rows), c),
                    device_id_type=MESH,
                ),
            )
            for way in range(2)
        ]

    def conv(position, m):
        lines = parts[m - 1]

        @pl.loop(0, blocks + 2 * m)
        def _(block):
            for i in range(3):
                lines[i, block] = jnp.zeros(lines.shape[2:], F32)

        @pl.loop(0, 9)
        def _(tap):
            i, j = tap // 3, lax.rem(tap, 3)
            n = position * 9 + tap
            slot = lax.rem(n, SLOTS)
            ahead = n + SLOTS - 1

            @pl.when(ahead < taps)
            def _():
                weight_copy(ahead).start()

            weight_copy(n).wait()
            product = jnp.dot(x_ref[...], wbuf[slot], preferred_element_type=F32)
            for a in range(blocks):
                same = idrep[REACH + a, own : own + rb] == idrep[REACH + a - (j - 1) * m, own : own + rb]
                part = product[a * rb : (a + 1) * rb]
                lines[i, a + (2 - j) * m] += jnp.where(wide(same.astype(F32), width) > 0.0, part, 0.0)

        @pl.loop(0, 3)
        def _(i):
            for a in range(m):
                edge_out[m - 1][0, i, a] = lines[i, a].astype(BF16)
                edge_out[m - 1][1, i, a] = lines[i, m + blocks + a].astype(BF16)

        for sends, _, copy in side_copies(m):
            pl.when(sends)(copy.start)

    def absorb(m):
        height, lines, whole = HALO[m], parts[m - 1], sums_by_row[m - 1]
        for way, (_, receives, copy) in enumerate(side_copies(m)):
            @pl.when(receives)
            def _():
                copy.wait_recv()
                for i in range(3):
                    for a in range(m):
                        lines[i, (blocks, m)[way] + a] += edge_in[m - 1][way, i, a].astype(F32)

        @pl.loop(0, blocks)
        def _(a):
            whole[a, 0:height] = jnp.zeros((height, width), F32)
            whole[a, height : height + rb] = lines[1, m + a]
            whole[a, height + rb : 2 * height + rb] = jnp.zeros((height, width), F32)
            for i in (0, 2):
                up = (i - 1) * 36 * m
                same = idrep[REACH + a, own : own + rb] == idrep[REACH + a, own - up : own - up + rb]
                whole[a, height - up : height - up + rb] += jnp.where(
                    wide(same.astype(F32), width) > 0.0, lines[i, m + a], 0.0
                )
            rim_out[m - 1][0, a] = whole[a, 0:height].astype(BF16)
            rim_out[m - 1][1, a] = whole[a, height + rb : 2 * height + rb].astype(BF16)

        for sends, _, copy in rim_copies(m):
            pl.when(sends)(copy.start)

    def finish(m):
        height, whole = HALO[m], sums_by_row[m - 1]

        @pl.loop(0, blocks)
        def _(a):
            zn[m, a] = whole[a, height : height + rb]

        for way, (_, receives, copy) in enumerate(rim_copies(m)):
            @pl.when(receives)
            def _():
                copy.wait_recv()
                start = (rb - height, 0)[way]
                for a in range(blocks):
                    zn[m, a, start : start + height] += rim_in[m - 1][way, a].astype(F32)

    members = [(dy, dx, dk) for dy in range(2) for dx in range(2) for dk in range(2)]
    half = share // 2

    def channel_slices(y, x, k):
        return [pl.multiple_of((2 * (2 * k + l) + y) * share + x * half, 128) for l in range(2)]

    def member_copies(steps, slices):
        mine = lax.rem(r, 2) * cols + c
        copies = []
        for step in steps:
            dy, dx, dk = members[step]
            y, x, k = lax.rem(r + dy, 2), lax.rem(c // 2 + dx, 2), lax.rem(c + dk, 2)
            starts = channel_slices(y, x, k)
            for l in slices:
                source = x_ref.at[:, pl.ds(starts[l], half)]
                target = xsub_ref.at[l, mine]
                if step == 0:
                    copies.append(pltpu.make_async_copy(source, target, xrecv.at[l, mine]))
                else:
                    copies.append(
                        pltpu.make_async_remote_copy(
                            src_ref=source,
                            dst_ref=target,
                            send_sem=xsend.at[l, step],
                            recv_sem=xrecv.at[l, mine],
                            device_id=(2 * (r // 2) + y, 2 * x + k),
                            device_id_type=MESH,
                        )
                    )
        return copies

    def send_members(steps, slices):
        for copy in member_copies(steps, slices):
            copy.start()

    pool_cols = Exchange(cols, c, lambda other: (r, other), pc_buf, pcsend, pcrecv)
    pool_z = Exchange(rows, r, lambda other: (other, c), pz_buf, pzsend, pzrecv)
    send_members(range(8), (0,))
    send_members((0, 1), (1,))
    conv(0, 3)
    pool_rows.arrive()
    pc_buf[c] = pool_rows.total()
    pool_cols.start()
    conv(1, 2)
    absorb(3)
    pool_cols.arrive()
    counts = counts_ref[...]
    pooled = (pool_cols.total() / wide(counts, share)).astype(BF16)
    pooled_ref[...] = pooled
    pool_weight.wait()
    pz_buf[r] = jnp.dot(pooled, wplbuf[...], preferred_element_type=F32)
    pool_z.start()
    conv(2, 1)
    absorb(2)
    product = jnp.dot(x_ref[...], wpt_ref[...], preferred_element_type=F32)
    for a in range(blocks):
        zn[0, a] = product[a * rb : (a + 1) * rb]
    absorb(1)
    pool_z.arrive()
    zp = pool_z.total()
    pool_avg = jnp.sum(zp, axis=0, keepdims=True) / image_count
    pool_square = jnp.sum(zp * zp, axis=0, keepdims=True) / image_count
    pool_inverse = lax.rsqrt(pool_square - pool_avg * pool_avg + epsilon)
    pool_normed = (zp - pool_avg) * pool_inverse
    pool_active, pool_slope = silu_parts(gain_ref[4:5] * pool_normed + shift_ref[4:5])
    pooln_ref[...] = pool_normed
    pools_ref[...] = pool_slope
    spare = one_hot.shape[1] - images
    pool_active = jnp.concatenate([pool_active, jnp.zeros((spare, width), F32)], axis=0).astype(BF16)
    joined[:, 4 * width : 5 * width] = jnp.dot(one_hot, pool_active, preferred_element_type=F32).astype(BF16)

    for m in (3, 2, 1):
        finish(m)

    started = []

    def all_sum(step, value, meanwhile=(None, None)):
        across = Exchange(cols, c, lambda other: (r, other), cbuf.at[step], csend.at[step], crecv.at[step])
        cbuf[step, c] = value
        across.start()
        if meanwhile[0]:
            meanwhile[0]()
        across.arrive()
        down = Exchange(rows, r, lambda other: (other, c), rbuf.at[step], rsend.at[step], rrecv.at[step])
        rbuf[step, r] = across.total()
        down.start()
        if meanwhile[1]:
            meanwhile[1]()
        down.arrive()
        started.extend((across, down))
        return down.total()

    zero = jnp.zeros((1, width), F32)

    def row_sum(value):
        return jnp.sum(value, axis=0, keepdims=True)

    firsts, seconds = [], []
    for k in range(4):
        first, second = zero, zero
        for a in range(blocks):
            value = zn[k, a]
            first, second = first + row_sum(value), second + row_sum(value * value)
        firsts.append(first)
        seconds.append(second)
    moments = all_sum(0, jnp.concatenate(firsts + seconds, axis=0))
    send_members((2, 4), (1,))
    average = moments[0:4] / total_pixels
    inverse = lax.rsqrt(moments[4:8] / total_pixels - average * average + epsilon)
    for k in range(4):
        @pl.loop(0, blocks)
        def _(a):
            normed = (zn[k, a] - average[k : k + 1]) * inverse[k : k + 1]
            value, slant = silu_parts(gain_ref[k : k + 1] * normed + shift_ref[k : k + 1])
            zn[k, a] = normed
            slope[k, a] = slant
            joined[pl.ds(pl.multiple_of(a * rb, rb), rb), k * width : (k + 1) * width] = value.astype(BF16)

    zf[...] = jnp.dot(joined[...], wpj_ref[...], preferred_element_type=F32)
    first, second = zero, zero
    for a in range(blocks):
        value = zf[a * rb : (a + 1) * rb]
        first, second = first + row_sum(value), second + row_sum(value * value)

    def put_upstream():
        upstream[...] = jnp.dot(order_ref[...], cot_ref[...], preferred_element_type=F32)

    moments = all_sum(1, jnp.concatenate([first, second] + [zero] * 6, axis=0), (None, put_upstream))
    send_members((3, 5), (1,))
    final_avg = moments[0:1] / total_pixels
    final_inverse = lax.rsqrt(moments[1:2] / total_pixels - final_avg * final_avg + epsilon)
    shift_last, gain_last = zero, zero
    for a in range(blocks):
        piece = slice(a * rb, (a + 1) * rb)
        normed = (zf[piece] - final_avg) * final_inverse
        result, slant = silu_parts(gain_ref[5:6] * normed + shift_ref[5:6])
        active[piece] = result.astype(BF16)
        grad = upstream[piece] * slant
        zf[piece] = normed
        dzf[piece] = grad
        shift_last, gain_last = shift_last + row_sum(grad), gain_last + row_sum(grad * normed)

    def put_output():
        out_ref[...] = jnp.dot(back_ref[...], active[...], preferred_element_type=F32).astype(BF16)

    sums = all_sum(2, jnp.concatenate([shift_last, gain_last] + [zero] * 6, axis=0), (None, put_output))
    send_members((6, 7), (1,))
    shift_last, gain_last = sums[0:1], sums[1:2]
    gain = gain_ref[5:6]
    for a in range(blocks):
        piece = slice(a * rb, (a + 1) * rb)
        dzf[piece] = final_inverse * (
            dzf[piece] * gain
            - gain * shift_last / total_pixels
            - zf[piece] * (gain * gain_last / total_pixels)
        )
    grad_final = dzf[...].astype(BF16)

    shifts, gains = [], []
    for k in range(4):
        grad = contract_lanes(grad_final, wpj_ref[k * width : (k + 1) * width])
        shift_sum, gain_sum = zero, zero
        for a in range(blocks):
            part = grad[a * rb : (a + 1) * rb] * slope[k, a]
            slope[k, a] = part
            shift_sum, gain_sum = shift_sum + row_sum(part), gain_sum + row_sum(part * zn[k, a])
        shifts.append(shift_sum)
        gains.append(gain_sum)

    def put_images():
        grad_pixel = contract_lanes(grad_final, wpj_ref[4 * width : 5 * width])
        upper = grad_pixel.astype(BF16)
        lower = (grad_pixel - upper.astype(F32)).astype(BF16)
        dap_ref[...] = (contract_rows(one_hot, upper) + contract_rows(one_hot, lower))[:images]

    def put_projection():
        for k in range(5):
            piece = slice(k * width, (k + 1) * width)
            pj_ref[piece] = contract_rows(joined[:, piece], grad_final).astype(BF16)

    sums = all_sum(3, jnp.concatenate(shifts + gains, axis=0), (put_images, put_projection))
    for k in range(4):
        gain = gain_ref[k : k + 1]
        from_shift = gain * sums[k : k + 1] / total_pixels
        from_gain = gain * sums[4 + k : 5 + k] / total_pixels

        @pl.loop(0, blocks)
        def _(a):
            dz_ref[k, a] = (
                inverse[k : k + 1] * (slope[k, a] * gain - from_shift - zn[k, a] * from_gain)
            ).astype(BF16)

    stat_ref[...] = jnp.concatenate([sums, shift_last, gain_last, pool_inverse] + [zero] * 5, axis=0)

    pool_rows.leave(share_of)
    for exchange in (pool_cols, pool_z, *started):
        exchange.leave()
    for m in (3, 2, 1):
        for sends, _, copy in side_copies(m) + rim_copies(m):
            pl.when(sends)(copy.wait_send)
    for copy in member_copies((0,), (0, 1)):
        copy.wait()
    for copy in member_copies(range(1, 8), (0, 1)):
        copy.wait_send()
    for l in range(2):
        for step, (dy, dx, dk) in enumerate(members):
            if step:
                y, x, k = lax.rem(r + dy, 2), lax.rem(c // 2 + dx, 2), lax.rem(c + dk, 2)
                there = xsub_ref.at[l, y * cols + 2 * x + k]
                pltpu.make_async_remote_copy(
                    src_ref=there,
                    dst_ref=there,
                    send_sem=xsend.at[l, step],
                    recv_sem=xrecv.at[l, y * cols + 2 * x + k],
                    device_id=(2 * (r // 2) + y, 2 * x + k),
                    device_id_type=MESH,
                ).wait_recv()


def forward_call(rows, cols, image_count, x, order, back, ids, wat, wpt, wpl, wpj, gain, shift, cot, counts):
    pixels, channels = x.shape
    width = wpt.shape[1]
    blocks, rb = 4, pixels // 4
    images = counts.shape[0]
    share = channels // rows
    total_pixels = float(pixels * rows * cols)
    vmem = pl.BlockSpec(memory_space=pltpu.VMEM)
    hbm = pl.BlockSpec(memory_space=pl.ANY)

    def each(shape, kind):
        return [pltpu.VMEM(shape(m) + (width,), kind) for m in (1, 2, 3)]

    dma = pltpu.SemaphoreType.DMA
    return pl.pallas_call(
        functools.partial(forward_kernel, rows, cols, float(image_count), total_pixels),
        out_shape=(
            jax.ShapeDtypeStruct((pixels, width), BF16),
            jax.ShapeDtypeStruct((4, blocks, rb, width), BF16),
            jax.ShapeDtypeStruct((5 * width, width), BF16),
            jax.ShapeDtypeStruct((16, width), F32),
            jax.ShapeDtypeStruct((images, share), BF16),
            jax.ShapeDtypeStruct((images, width), F32),
            jax.ShapeDtypeStruct((images, width), F32),
            jax.ShapeDtypeStruct((images, width), F32),
            jax.ShapeDtypeStruct((2, 8, pixels, share // 2), BF16),
        ),
        in_specs=[vmem, vmem, vmem, vmem, hbm, vmem, hbm, vmem, vmem, vmem, vmem, vmem],
        out_specs=(vmem,) * 8 + (hbm,),
        scratch_shapes=[
            pltpu.VMEM((pixels, channels), BF16),
            pltpu.VMEM((blocks + 2 * REACH, ids.shape[0], 128), F32),
            pltpu.VMEM((SLOTS, channels, width), BF16),
            pltpu.VMEM((share, width), BF16),
            each(lambda m: (3, blocks + 2 * m, rb), F32),
            each(lambda m: (blocks, 2 * HALO[m] + rb), F32),
            each(lambda m: (2, 3, m, rb), BF16), each(lambda m: (2, 3, m, rb), BF16),
            each(lambda m: (2, blocks, HALO[m]), BF16), each(lambda m: (2, blocks, HALO[m]), BF16),
            pltpu.VMEM((4, blocks, rb, width), F32),
            pltpu.VMEM((4, blocks, rb, width), F32),
            pltpu.VMEM((pixels, 5 * width), BF16),
            pltpu.VMEM((pixels, width), F32),
            pltpu.VMEM((pixels, width), F32),
            pltpu.VMEM((pixels, width), BF16),
            pltpu.VMEM((pixels, width), F32),
            pltpu.VMEM((images, channels), F32),
            pltpu.VMEM((4, cols, 8, width), F32),
            pltpu.VMEM((4, rows, 8, width), F32),
            pltpu.VMEM((rows, images, share), F32),
            pltpu.VMEM((cols, images, share), F32),
            pltpu.VMEM((rows, images, width), F32),
            dma((SLOTS,)), dma,
            dma((3, 2)), dma((3, 2)), dma((3, 2)), dma((3, 2)),
            dma((4, cols)), dma((4, cols)),
            dma((4, rows)), dma((4, rows)),
            dma((rows,)), dma((rows,)),
            dma((cols,)), dma((cols,)),
            dma((rows,)), dma((rows,)),
            dma((2, 8)), dma((2, 8)),
        ],
        compiler_params=pltpu.CompilerParams(
            collective_id=0, has_side_effects=True, vmem_limit_bytes=60 * 2**20
        ),
        cost_estimate=pl.CostEstimate(flops=2 * pixels * channels * width * 28, bytes_accessed=40_000_000, transcendentals=0),
    )(x, order, back, ids, wat, wpt, wpl, wpj, gain, shift, cot, counts)


def backward_kernel(
    rows, cols, image_count, height,
    dz_ref, xsub_ref, ids_ref, wat_ref, wpt_ref, wpl_ref, gain_ref, counts_ref,
    pooled_ref, pooln_ref, pools_ref, dap_ref, stat_ref, back_ref, pj_ref,
    gx_ref, dw_ref, dpoint_ref, gpool_ref, gstat_ref, gproj_ref,
    ext0, ext1, ext2, ext3, shifted, colmask, idrep, gmat, gown, xt, acc, wbuf, wpt,
    send1, recv1, keep, relay, dw, pcbuf, prbuf, quarters, quarter_sums, row_parts, final_parts,
    xsem, wsem, wptsem, zsend, zrecv, agsend, agrecv, s1send, s1recv, s2send, s2recv, s3send, s3recv,
    pcsend, pcrecv, prsend, prrecv, qsend, qrecv, rqsend, rqrecv, fqsend, fqrecv, outsem,
):
    r, c = lax.axis_index("rows"), lax.axis_index("cols")
    z, y = r // 2, lax.rem(r, 2)
    x, k = c // 2, lax.rem(c, 2)
    levels = rows // 2
    z_lo, z_hi = lax.rem(z, 2), z // 2
    blocks, rb, width = dz_ref.shape[1:]
    pair = 2 * rb
    across = cols * blocks
    pixels = blocks * rb
    own = REACH * 36
    half = xt.shape[0] // 2
    images = dap_ref.shape[0]
    ext = {0: ext0, 1: ext1, 2: ext2, 3: ext3}
    tall = {0: 0, **HALO}

    def x_copy(l, dev, a):
        dev_y, dev_c = dev // cols, lax.rem(dev, cols)
        start = pl.multiple_of((dev_c * blocks + a) * pair + dev_y * rb, 16)
        return pltpu.make_async_copy(
            xsub_ref.at[l, dev, a], gmat.at[pl.ds(start, rb), pl.ds(l * half, half)], xsem.at[l, dev, a]
        )

    for l in range(2):
        for a in range(blocks):
            @pl.loop(0, 2 * cols)
            def _(dev):
                x_copy(l, dev, a).start()

    groups = [[(0, 4), (1, 4), (2, 4)]]
    for m in (1, 2, 3):
        groups += [[(m - 1, 0), (m - 1, 1), (m - 1, 2)], [(m - 1, 6), (m - 1, 7), (m - 1, 8)], [(m - 1, 3), (m - 1, 5)]]

    def weight_copies(n):
        return [
            pltpu.make_async_copy(
                wat_ref.at[branch, tap], wbuf.at[n % 2, :, pl.ds(place * width, width)], wsem.at[n % 2, place]
            )
            for place, (branch, tap) in enumerate(groups[n])
        ]

    point_copy = pltpu.make_async_copy(wpt_ref, wpt, wptsem)
    point_copy.start()
    for n in range(2):
        for copy in weight_copies(n):
            copy.start()

    greet(rows, cols, r, c)

    def has_rim(dev_y):
        return (dev_y == 1) & (z >= 1) | (dev_y == 0) & (z <= levels - 2)

    def rim_copy(m, sending):
        high = tall[m]
        start = pl.multiple_of(y * (rb - high), 16)
        target = pl.multiple_of((1 - y) * (high + pair), 16)
        return pltpu.make_async_remote_copy(
            src_ref=dz_ref.at[m, :, pl.ds(start, high)],
            dst_ref=ext[m].at[pl.ds(c * blocks, blocks), pl.ds(target, high)],
            send_sem=zsend.at[m],
            recv_sem=zrecv.at[m],
            device_id=(lax.rem(r + 4 * y - 2 + rows, rows), c),
            device_id_type=MESH,
        )

    sends_rim = (y == 1) & (z <= levels - 2) | (y == 0) & (z >= 1)

    def item(m, kind, dev_y, dev_c, first=0, count=None):
        high = tall[m]
        count = blocks if count is None else count
        start = high + rb * dev_y if kind == 0 else (1 - dev_y) * (high + pair)
        height = rb if kind == 0 else high
        return ext[m].at[pl.ds(dev_c * blocks + first, count), pl.ds(pl.multiple_of(start, 16), height)]

    def gather_copy(m, kind, dev_y, dev_c, slot, target, first=0, count=None):
        piece = item(m, kind, dev_y, dev_c, first, count)
        return pltpu.make_async_remote_copy(
            src_ref=piece,
            dst_ref=piece,
            send_sem=agsend.at[m, kind, slot],
            recv_sem=agrecv.at[m, kind, 2 * cols if first else dev_y * cols + dev_c],
            device_id=target,
            device_id_type=MESH,
        )

    most = blocks // 2
    side = 2 * (1 - x) + k
    sibling, beside, below = (r, 2 * x + 1 - k), (r, side), (2 * z + 1 - y, c)

    def if_there(kind, dev_y, action):
        if kind == 0:
            action()
        else:
            pl.when(has_rim(dev_y))(action)

    def kinds(m):
        return (0,) if m == 0 else (0, 1)

    def own_copies(m, kind):
        return [gather_copy(m, kind, y, c, slot, to) for slot, to in enumerate((beside, below, sibling))]

    def side_copies(m, kind):
        return [gather_copy(m, kind, y, side, 3, below, 0, most), gather_copy(m, kind, y, side, 5, sibling)]

    def below_copies(m, kind):
        return [
            gather_copy(m, kind, 1 - y, c, 4, beside, most, blocks - most),
            gather_copy(m, kind, 1 - y, c, 6, sibling),
        ]

    def diagonal_copies(m, kind):
        return [gather_copy(m, kind, 1 - y, side, 7, sibling)]

    def start_own(m, kind):
        if kind == 0:
            high = tall[m]
            for a in range(blocks):
                ext[m][c * blocks + a, pl.ds(pl.multiple_of(high + rb * y, 16), rb)] = dz_ref[m, a]

        def action():
            if kind == 1:
                rim_copy(m, False).wait_recv()
            for copy in own_copies(m, kind):
                copy.start()

        if_there(kind, y, action)

    def pass_on(m):
        for kind in kinds(m):
            def from_side():
                gather_copy(m, kind, y, side, 0, beside).wait_recv()
                for copy in side_copies(m, kind):
                    copy.start()

            def from_below():
                gather_copy(m, kind, 1 - y, c, 0, below).wait_recv()
                for copy in below_copies(m, kind):
                    copy.start()

            if_there(kind, y, from_side)
            if_there(kind, 1 - y, from_below)

    def pass_last(m):
        for kind in kinds(m):
            def action():
                gather_copy(m, kind, 1 - y, side, 0, below, 0, most).wait_recv()
                gather_copy(m, kind, 1 - y, side, 0, beside, most, blocks - most).wait_recv()
                for copy in diagonal_copies(m, kind):
                    copy.start()

            if_there(kind, 1 - y, action)

    def finish_gather(m):
        for kind in kinds(m):
            for dev_y in (y, 1 - y):
                for dev_c in (c, side):
                    piece = gather_copy(m, kind, dev_y, dev_c + 1 - 2 * k, 0, sibling)
                    if_there(kind, dev_y, piece.wait_recv)

    def finish_sends(m):
        for kind in kinds(m):
            def action():
                for copy in own_copies(m, kind) + side_copies(m, kind):
                    copy.wait_send()

            def below_action():
                for copy in below_copies(m, kind) + diagonal_copies(m, kind):
                    copy.wait_send()

            if_there(kind, y, action)
            if_there(kind, 1 - y, below_action)

    for m in (1, 2, 3):
        pl.when(sends_rim)(rim_copy(m, True).start)
    start_own(1, 0)

    pool_cols = Exchange(cols, c, lambda other: (r, other), pcbuf, pcsend, pcrecv)
    pcbuf[c] = dap_ref[...]
    pool_cols.start()

    tall_piece, wide_piece = quarters.shape[2], quarters.shape[3]

    def quarter(other):
        rows_of = pl.ds(pl.multiple_of(lax.rem(other, 2) * tall_piece, 16), tall_piece)
        return pj_ref.at[:, rows_of, pl.ds(pl.multiple_of(other // 2 * wide_piece, 128), wide_piece)]

    proj_cols = Exchange(cols, c, lambda other: (r, other), quarters, qsend, qrecv)
    proj_rows = Exchange(rows, r, lambda other: (other, c), row_parts, rqsend, rqrecv)
    proj_last = Exchange(cols, c, lambda other: (r, other), final_parts, fqsend, fqrecv)
    own_rows = pl.ds(pl.multiple_of(k * tall_piece, 16), tall_piece)
    quarters[c] = pj_ref[:, own_rows, pl.ds(pl.multiple_of(x * wide_piece, 128), wide_piece)]
    proj_cols.start(quarter)

    def whole_sum(slots, count):
        value = slots[0].astype(F32)
        for other in range(1, count):
            value = value + slots[other].astype(F32)
        return value

    def proj_down():
        proj_cols.arrive()
        quarter_sums[...] = whole_sum(quarters, cols).astype(BF16)
        row_parts[r] = quarter_sums[r]
        proj_rows.start(lambda other: quarter_sums.at[other])

    def proj_spread():
        proj_rows.arrive()
        final_parts[c] = whole_sum(row_parts, rows).astype(BF16)
        proj_last.start()

    for block in range(across):
        idrep[block] = jnp.broadcast_to(ids_ref[:, block : block + 1], idrep.shape[1:])
    for m in (1, 2, 3):
        high = tall[m]

        @pl.when(z == 0)
        def _():
            @pl.loop(0, across)
            def _(block):
                ext[m][block, 0:high] = jnp.zeros((high, width), BF16)

        @pl.when(z == levels - 1)
        def _():
            @pl.loop(0, across)
            def _(block):
                ext[m][block, high + pair : 2 * high + pair] = jnp.zeros((high, width), BF16)

    for shift in range(-REACH, REACH + 1):
        for block in range(across):
            if 0 <= block - shift < across:
                same = idrep[block, own : own + 48] == idrep[block - shift, own : own + 48]
                colmask[REACH + shift, block] = wide(same.astype(F32), width).astype(BF16)
            else:
                colmask[REACH + shift, block] = jnp.zeros((48, width), BF16)

    start_own(1, 1)
    start_own(2, 0)
    start_own(2, 1)
    for l in range(2):
        for a in range(blocks):
            @pl.loop(0, 2 * cols)
            def _(dev):
                x_copy(l, dev, a).wait()

        spot = pl.multiple_of(lax.rem(l + z_lo, 2) * half, half)
        for chunk in range(gmat.shape[0] // 128):
            piece = slice(chunk * 128, (chunk + 1) * 128)
            xt[pl.ds(spot, half), piece] = gmat[piece, l * half : (l + 1) * half].astype(F32).T.astype(BF16)

    pass_on(1)
    start_own(3, 0)
    start_own(3, 1)

    point_copy.wait()

    @pl.loop(0, wpt.shape[0] // 256)
    def _(n):
        piece = pl.ds(pl.multiple_of(n * 256, 256), 256)
        left = jnp.concatenate([dz_ref[0, a] for a in range(blocks)], axis=0)
        acc[:, piece] = contract_lanes(left, wpt[piece, :])

    pool_copy = pltpu.make_async_copy(wpl_ref, wpt, wptsem)
    pool_copy.start()

    def build_shifted(m):
        high = tall[m]

        @pl.loop(0, across)
        def _(block):
            whole = ext[m][block].astype(F32)
            for i in range(3):
                down = (i - 1) * 36 * m
                value = whole[high - down : high - down + pair]
                if i != 1:
                    same = idrep[block, own : own + pair] == idrep[block, own - down : own - down + pair]
                    value = jnp.where(wide(same.astype(F32), width) > 0.0, value, 0.0)
                shifted[i, block] = value.astype(BF16)

    def masked(values, mask):
        count = values.shape[0] // 48
        return jnp.concatenate([values[48 * n : 48 * (n + 1)] * mask for n in range(count)], axis=0)

    def scatter_first(n, part):
        keep[n] = part[:half]
        send1[n] = part[half:].astype(BF16)
        stage1(n).start()

    def stage1(n):
        return pltpu.make_async_remote_copy(
            src_ref=send1.at[n], dst_ref=recv1.at[n], send_sem=s1send.at[n], recv_sem=s1recv.at[n],
            device_id=(r + 2 - 4 * z_lo, c), device_id_type=MESH,
        )

    def stage2(n):
        return pltpu.make_async_remote_copy(
            src_ref=relay.at[n], dst_ref=relay.at[n], send_sem=s2send.at[n], recv_sem=s2recv.at[n],
            device_id=(lax.rem(r + rows // 2, rows), c), device_id_type=MESH,
        )

    def stage3(n, from_x, slot, target):
        piece = dw.at[n, pl.ds(pl.multiple_of(from_x * half, half), half)]
        return pltpu.make_async_remote_copy(
            src_ref=piece, dst_ref=piece, send_sem=s3send.at[slot, n], recv_sem=s3recv.at[from_x, n],
            device_id=target, device_id_type=MESH,
        )

    last = z_hi == k

    def drain2(start, count):
        @pl.loop(start, start + count)
        def _(n):
            stage1(n).wait_recv()
            total = keep[n] + recv1[n].astype(F32)

            @pl.when(last)
            def _():
                keep[n] = total

            @pl.when(jnp.logical_not(last))
            def _():
                relay[n] = total.astype(BF16)
                stage2(n).start()

    def drain3(start, count):
        @pl.when(last)
        def _():
            @pl.loop(start, start + count)
            def _(n):
                stage2(n).wait_recv()
                dw[n, pl.ds(pl.multiple_of(x * half, half), half)] = (keep[n] + relay[n].astype(F32)).astype(BF16)
                stage3(n, x, 0, beside).start()
                stage3(n, x, 1, sibling).start()

    def drain4(start, count):
        @pl.when(last)
        def _():
            @pl.loop(start, start + count)
            def _(n):
                copy = stage3(n, 1 - x, 2, sibling)
                copy.wait_recv()
                copy.start()

        @pl.when(jnp.logical_not(last))
        def _():
            @pl.loop(start, start + count)
            def _(n):
                stage3(n, 0, 0, sibling).wait_recv()
                stage3(n, 1, 0, sibling).wait_recv()

    def weight_grad(m, between):
        @pl.loop(0, 9)
        def _(tap):
            for when, action in between.items():
                pl.when(tap == when)(action)
            i, j = tap // 3, lax.rem(tap, 3)
            shift = (j - 1) * m

            @pl.loop(0, across)
            def _(block):
                source = lax.rem(block - shift + across, across)
                gmat[pl.ds(pl.multiple_of(block * pair, 16), pair)] = masked(
                    shifted[i, source], colmask[REACH + shift, block]
                )

            scatter_first((m - 1) * 9 + tap, jnp.dot(xt[...], gmat[...], preferred_element_type=F32))

    def add_products(n, depth):
        for copy in weight_copies(n):
            copy.wait()

        @pl.loop(0, wbuf.shape[1] // 256)
        def _(chunk):
            piece = pl.ds(pl.multiple_of(chunk * 256, 256), 256)
            acc[:, piece] += contract_lanes(gown[:, :depth], wbuf[n % 2, piece, :depth])

        if n + 2 < len(groups):
            for copy in weight_copies(n + 2):
                copy.start()

    def feature_grad(m, lines):
        for line in lines:
            n = 1 + (m - 1) * 3 + line
            first, step = groups[n][0][1], groups[n][1][1] - groups[n][0][1]

            @pl.loop(0, len(groups[n]))
            def _(place):
                tap = first + step * place
                shift = (lax.rem(tap, 3) - 1) * m
                for a in range(blocks):
                    block = c * blocks + a
                    source = lax.rem(block - shift + across, across)
                    gown[a * rb : (a + 1) * rb, pl.ds(pl.multiple_of(place * width, width), width)] = masked(
                        shifted[tap // 3, source, pl.ds(pl.multiple_of(y * rb, 16), rb)],
                        colmask[REACH + shift, block],
                    )

            add_products(n, len(groups[n]) * width)

    for m in (1, 2, 3):
        for a in range(blocks):
            gown[a * rb : (a + 1) * rb, (m - 1) * width : m * width] = dz_ref[m, a]
    add_products(0, 3 * width)
    pass_last(1)
    finish_gather(1)
    build_shifted(1)

    def second_on():
        pass_on(2)
        start_own(0, 0)

    weight_grad(1, {4: second_on, 7: proj_down})
    pass_last(2)
    feature_grad(1, (0,))
    pass_on(3)
    drain2(0, 9)
    feature_grad(1, (1, 2))
    finish_gather(2)
    build_shifted(2)

    def third_last():
        pass_on(0)
        pass_last(3)

    weight_grad(2, {2: proj_spread, 5: third_last})
    pass_last(0)
    drain3(0, 9)
    feature_grad(2, (0,))
    drain2(9, 9)
    feature_grad(2, (1, 2))
    finish_gather(3)
    build_shifted(3)
    weight_grad(3, {})
    finish_gather(0)

    @pl.loop(0, across)
    def _(block):
        gmat[pl.ds(pl.multiple_of(block * pair, 16), pair)] = ext0[block]

    scatter_first(27, jnp.dot(xt[...], gmat[...], preferred_element_type=F32))
    drain4(0, 9)
    drain3(9, 9)

    pool_cols.arrive()
    pool_rows = Exchange(rows, r, lambda other: (other, c), prbuf, prsend, prrecv)
    prbuf[r] = pool_cols.total()
    pool_rows.start()
    feature_grad(3, (0, 1))
    drain2(18, 10)
    feature_grad(3, (2,))
    drain4(9, 9)
    pool_rows.arrive()
    normed = pooln_ref[...]
    grad = pool_rows.total() * pools_ref[...]
    shift_sum = jnp.sum(grad, axis=0, keepdims=True)
    gain_sum = jnp.sum(grad * normed, axis=0, keepdims=True)
    gain = gain_ref[4:5]
    grad_z = (
        stat_ref[10:11]
        * (grad * gain - gain * shift_sum / image_count - normed * (gain * gain_sum / image_count))
    ).astype(BF16)
    gpool_ref[...] = contract_rows(pooled_ref[...], grad_z)
    gstat_ref[...] = jnp.concatenate([shift_sum, gain_sum] + [jnp.zeros((1, width), F32)] * 6, axis=0)
    own_ids = jnp.concatenate([idrep[c * blocks + a, own : own + pair] for a in range(blocks)], axis=0)
    upper_row = jnp.broadcast_to((y == 0).astype(F32), (pixels, 128))
    own_ids = jnp.where(
        upper_row > 0.0,
        jnp.concatenate([own_ids[a * pair : a * pair + rb] for a in range(blocks)], axis=0),
        jnp.concatenate([own_ids[a * pair + rb : (a + 1) * pair] for a in range(blocks)], axis=0),
    )
    lanes = lax.broadcasted_iota(jnp.int32, (pixels, 128), 1).astype(F32)
    one_hot = (own_ids == lanes).astype(F32).astype(BF16)
    counts = wide(counts_ref[...], 256)
    pool_copy.wait()

    @pl.loop(0, wpt.shape[0] // 256)
    def _(n):
        piece = pl.ds(pl.multiple_of(n * 256, 256), 256)
        back = contract_lanes(grad_z, wpt[piece, :]) / counts
        back = jnp.concatenate([back, jnp.zeros((128 - images, 256), F32)], axis=0).astype(BF16)
        value = (acc[:, piece] + jnp.dot(one_hot, back, preferred_element_type=F32)).astype(BF16)
        gx_ref[:, piece] = jnp.dot(back_ref[...], value, preferred_element_type=F32).astype(BF16)

    drain3(18, 10)
    drain4(18, 10)
    results = (
        pltpu.make_async_copy(dw.at[pl.ds(0, 27)], dw_ref, outsem.at[0]),
        pltpu.make_async_copy(dw.at[27], dpoint_ref, outsem.at[1]),
    )
    for result in results:
        result.start()

    pool_cols.leave()
    pool_rows.leave()
    proj_last.arrive()
    for other in range(cols):
        piece_rows = slice(other % 2 * tall_piece, (other % 2 + 1) * tall_piece)
        gproj_ref[piece_rows, other // 2 * wide_piece : (other // 2 + 1) * wide_piece] = final_parts[other].astype(F32)
    proj_cols.leave(quarter)
    proj_rows.leave(lambda other: quarter_sums.at[other])
    proj_last.leave()
    for m in (1, 2, 3):
        pl.when(sends_rim)(rim_copy(m, True).wait_send)
    for m in (1, 2, 3, 0):
        finish_sends(m)

    @pl.loop(0, 28)
    def _(n):
        stage1(n).wait_send()

        @pl.when(last)
        def _():
            stage3(n, x, 0, beside).wait_send()
            stage3(n, x, 1, sibling).wait_send()
            stage3(n, 1 - x, 2, sibling).wait_send()

        @pl.when(jnp.logical_not(last))
        def _():
            stage2(n).wait_send()

    for result in results:
        result.wait()


def backward_call(
    rows, cols, image_count, dz, xsub, ids, wat, wpt, wpl, gain, counts, pooled, pooln, pools, dap, stat, back, proj
):
    _, blocks, rb, width = dz.shape
    channels = wpt.shape[0]
    share = channels // rows
    pair, across, pixels = 2 * rb, cols * blocks, blocks * rb
    images = dap.shape[0]
    group = pair * across
    vmem = pl.BlockSpec(memory_space=pltpu.VMEM)
    hbm = pl.BlockSpec(memory_space=pl.ANY)
    dma = pltpu.SemaphoreType.DMA
    taps = 28

    def ext(high):
        return pltpu.VMEM((across, 2 * high + pair, width), BF16)

    return pl.pallas_call(
        functools.partial(backward_kernel, rows, cols, float(image_count), rb),
        out_shape=(
            jax.ShapeDtypeStruct((pixels, channels), BF16),
            jax.ShapeDtypeStruct((taps - 1, share, width), BF16),
            jax.ShapeDtypeStruct((share, width), BF16),
            jax.ShapeDtypeStruct((share, width), F32),
            jax.ShapeDtypeStruct((8, width), F32),
            jax.ShapeDtypeStruct(proj.shape[1:], F32),
        ),
        in_specs=[vmem, hbm, vmem, hbm, hbm, hbm] + [vmem] * 9,
        out_specs=(vmem, hbm, hbm, vmem, vmem, vmem),
        scratch_shapes=[
            ext(0), ext(HALO[1]), ext(HALO[2]), ext(HALO[3]),
            pltpu.VMEM((3, across, pair, width), BF16),
            pltpu.VMEM((2 * REACH + 1, across, 48, width), BF16),
            pltpu.VMEM((across, ids.shape[0], 128), F32),
            pltpu.VMEM((group, width), BF16),
            pltpu.VMEM((pixels, 3 * width), BF16),
            pltpu.VMEM((share, group), BF16),
            pltpu.VMEM((pixels, channels), F32),
            pltpu.VMEM((2, channels, 3 * width), BF16),
            pltpu.VMEM((channels, width), BF16),
            pltpu.VMEM((taps, share // 2, width), BF16),
            pltpu.VMEM((taps, share // 2, width), BF16),
            pltpu.VMEM((taps, share // 2, width), F32),
            pltpu.VMEM((taps, share // 2, width), BF16),
            pltpu.VMEM((taps, share, width), BF16),
            pltpu.VMEM((cols, images, width), F32),
            pltpu.VMEM((rows, images, width), F32),
            pltpu.VMEM((cols, rows, proj.shape[1] // 2, width // 2), BF16),
            pltpu.VMEM((rows, proj.shape[1] // 2, width // 2), BF16),
            pltpu.VMEM((rows, proj.shape[1] // 2, width // 2), BF16),
            pltpu.VMEM((cols, proj.shape[1] // 2, width // 2), BF16),
            dma((2, 2 * cols, blocks)), dma((2, 3)), dma,
            dma((4,)), dma((4,)),
            dma((4, 2, 8)), dma((4, 2, 2 * cols + 1)),
            dma((taps,)), dma((taps,)),
            dma((taps,)), dma((taps,)),
            dma((3, taps)), dma((2, taps)),
            dma((cols,)), dma((cols,)),
            dma((rows,)), dma((rows,)),
            dma((cols,)), dma((cols,)),
            dma((rows,)), dma((rows,)),
            dma((cols,)), dma((cols,)),
            dma((2,)),
        ],
        compiler_params=pltpu.CompilerParams(
            collective_id=1, has_side_effects=True, vmem_limit_bytes=64 * 2**20
        ),
        cost_estimate=pl.CostEstimate(flops=4 * pixels * channels * width * 28, bytes_accessed=50_000_000, transcendentals=0),
    )(dz, xsub, ids, wat, wpt, wpl, gain, counts, pooled, pooln, pools, dap, stat, back, proj)


def extended(cells, sides, width):
    for axis, dim in sides:
        count = lax.axis_size(axis)
        ends = count - 1
        head = lax.slice_in_dim(cells, 0, width, axis=dim)
        tail = lax.slice_in_dim(cells, cells.shape[dim] - width, cells.shape[dim], axis=dim)
        cells = jnp.concatenate(
            [
                lax.ppermute(tail, axis, [(i, (i + 1) % count) for i in range(ends)]),
                cells,
                lax.ppermute(head, axis, [((i + 1) % count, i) for i in range(ends)]),
            ],
            axis=dim,
        )
    return cells


def image_match(window, own_ids, row_start, col_start):
    rows_here, cols_here = own_ids.shape
    section = window[row_start : row_start + rows_here, col_start : col_start + cols_here]
    return (section == own_ids).astype(jnp.float32).reshape(rows_here * cols_here, 1)


def silu_slope(preact_in):
    sigma = jax.nn.sigmoid(preact_in)
    return sigma * (1.0 + preact_in * (1.0 - sigma))


def transposed(left, right):
    return lax.dot_general(
        left, right, (((1,), (1,)), ((), ())), preferred_element_type=jnp.float32
    )


def shards(
    features, image_ids, w_point, w_atrous, w_pool, w_proj, norm_gain, norm_shift, cotangent
):
    rows_here, cols_here, channels = features.shape
    branch_width = w_point.shape[1]
    pixels = rows_here * cols_here
    grid_rows, grid_cols = image_ids.shape
    total_pixels = float(grid_rows * grid_cols)
    image_count = grid_rows // 16 * (grid_cols // 32)
    dilations = (RATE_LOW, RATE_MID, RATE_TOP)
    margin = RATE_TOP
    row_index = lax.axis_index("rows")
    col_index = lax.axis_index("cols")
    id_padded = jnp.pad(image_ids, margin, constant_values=-1)
    window = lax.dynamic_slice(
        id_padded,
        (row_index * rows_here, col_index * cols_here),
        (rows_here + 2 * margin, cols_here + 2 * margin),
    )
    own_ids = window[margin : margin + rows_here, margin : margin + cols_here]
    own_flat = own_ids.reshape(pixels)
    flattened = features.reshape(pixels, channels)
    padded = extended(features, (("rows", 0), ("cols", 1)), margin)
    one_hot = (own_flat[:, None] == jnp.arange(image_count, dtype=jnp.int32)[None, :]).astype(
        jnp.bfloat16
    )
    local_sums = jnp.einsum("pn,pc->nc", one_hot, flattened, preferred_element_type=jnp.float32)
    counts = jax.ops.segment_sum(
        jnp.ones((grid_rows * grid_cols,), jnp.float32), image_ids.reshape(-1), image_count
    )
    image_totals = lax.psum(local_sums, ("rows", "cols"))
    branch_outs = [jnp.dot(flattened, w_point, preferred_element_type=jnp.float32)]
    for branch, dilation in enumerate(dilations):
        running = jnp.zeros((pixels, branch_width), jnp.float32)
        for stencil in range(9):
            row_shift = (stencil // 3 - 1) * dilation
            col_shift = (stencil % 3 - 1) * dilation
            source = padded[
                margin + row_shift : margin + row_shift + rows_here,
                margin + col_shift : margin + col_shift + cols_here,
            ].reshape(pixels, channels)
            same_image = image_match(window, own_ids, margin + row_shift, margin + col_shift)
            running = running + same_image * jnp.dot(
                source, w_atrous[branch, stencil], preferred_element_type=jnp.float32
            )
        branch_outs.append(running)
    spatial = jnp.stack(branch_outs, axis=1)
    first_sum = jnp.sum(spatial, axis=0)
    second_sum = jnp.sum(spatial * spatial, axis=0)
    first_sum, second_sum = lax.psum((first_sum, second_sum), ("rows", "cols"))
    average = first_sum / total_pixels
    inverse_std = lax.rsqrt(second_sum / total_pixels - average * average + epsilon)
    normed = (spatial - average) * inverse_std
    preact = norm_gain[:4] * normed + norm_shift[:4]
    active = jax.nn.silu(preact).astype(jnp.bfloat16)
    pooled = (image_totals / counts[:, None]).astype(jnp.bfloat16)
    pool_z = jnp.dot(pooled, w_pool, preferred_element_type=jnp.float32)
    pool_avg = jnp.mean(pool_z, axis=0)
    pool_square = jnp.mean(pool_z * pool_z, axis=0)
    pool_inverse = lax.rsqrt(pool_square - pool_avg * pool_avg + epsilon)
    pool_normed = (pool_z - pool_avg) * pool_inverse
    pool_pre = norm_gain[4] * pool_normed + norm_shift[4]
    pool_active = jax.nn.silu(pool_pre).astype(jnp.bfloat16)
    joined = jnp.concatenate(
        [active.reshape(pixels, 4 * branch_width), jnp.take(pool_active, own_flat, axis=0)], axis=1
    )
    final_z = jnp.dot(joined, w_proj, preferred_element_type=jnp.float32)
    final_first, final_second = lax.psum(
        (jnp.sum(final_z, axis=0), jnp.sum(final_z * final_z, axis=0)), ("rows", "cols")
    )
    final_avg = final_first / total_pixels
    final_inverse = lax.rsqrt(final_second / total_pixels - final_avg * final_avg + epsilon)
    final_normed = (final_z - final_avg) * final_inverse
    final_pre = norm_gain[5] * final_normed + norm_shift[5]
    output = jax.nn.silu(final_pre).astype(jnp.bfloat16).reshape(rows_here, cols_here, branch_width)
    upstream = cotangent.reshape(pixels, branch_width).astype(jnp.float32)
    grad_final = upstream * silu_slope(final_pre)
    shift_last, gain_last = lax.psum(
        (jnp.sum(grad_final, axis=0), jnp.sum(grad_final * final_normed, axis=0)), ("rows", "cols")
    )
    grad_final_z = (
        final_inverse
        * (
            grad_final * norm_gain[5]
            - norm_gain[5] * shift_last / total_pixels
            - final_normed * (norm_gain[5] * gain_last / total_pixels)
        )
    ).astype(jnp.bfloat16)
    proj_term = jnp.einsum("pk,pc->kc", joined, grad_final_z, preferred_element_type=jnp.float32)
    grad_joined = transposed(grad_final_z, w_proj)
    grad_pre = grad_joined[:, : 4 * branch_width].reshape(pixels, 4, branch_width) * silu_slope(
        preact
    )
    grad_pixel = grad_joined[:, 4 * branch_width :]
    shift_sums = jnp.sum(grad_pre, axis=0)
    gain_sums = jnp.sum(grad_pre * normed, axis=0)
    image_grads = jax.ops.segment_sum(grad_pixel, own_flat, image_count)
    shift_sums, gain_sums, image_grads = lax.psum(
        (shift_sums, gain_sums, image_grads), ("rows", "cols")
    )
    grad_branch = (
        inverse_std
        * (
            grad_pre * norm_gain[:4]
            - norm_gain[:4] * shift_sums / total_pixels
            - normed * (norm_gain[:4] * gain_sums / total_pixels)
        )
    ).astype(jnp.bfloat16)
    grad_pool_pre = image_grads * silu_slope(pool_pre)
    pool_shift = jnp.sum(grad_pool_pre, axis=0)
    pool_gain = jnp.sum(grad_pool_pre * pool_normed, axis=0)
    grad_pool_z = (
        pool_inverse
        * (
            grad_pool_pre * norm_gain[4]
            - norm_gain[4] * pool_shift / image_count
            - pool_normed * (norm_gain[4] * pool_gain / image_count)
        )
    ).astype(jnp.bfloat16)
    row_share = channels // lax.axis_size("rows")
    pool_columns = lax.dynamic_slice_in_dim(pooled, row_index * row_share, row_share, 1)
    grad_pool = jnp.einsum(
        "nk,nc->kc", pool_columns, grad_pool_z, preferred_element_type=jnp.float32
    )
    grad_pooled = transposed(grad_pool_z, w_pool) / counts[:, None]
    grad_input = jnp.take(grad_pooled, own_flat, axis=0) + transposed(grad_branch[:, 0], w_point)
    point_term = jnp.einsum(
        "pk,pc->kc", flattened, grad_branch[:, 0], preferred_element_type=jnp.float32
    )
    stacked = grad_branch[:, 1:].reshape(rows_here, cols_here, 3 * branch_width)
    grad_padded = extended(stacked, (("rows", 0), ("cols", 1)), margin)
    rim_list = [
        grad_padded[:, :, branch * branch_width : (branch + 1) * branch_width]
        for branch in range(3)
    ]
    rim_bases = [margin, margin, margin]
    atrous_terms = []
    for branch, dilation in enumerate(dilations):
        tap_terms = []
        rim_base = rim_bases[branch]
        for stencil in range(9):
            row_shift = (stencil // 3 - 1) * dilation
            col_shift = (stencil % 3 - 1) * dilation
            source = padded[
                margin + row_shift : margin + row_shift + rows_here,
                margin + col_shift : margin + col_shift + cols_here,
            ].reshape(pixels, channels)
            same_image = image_match(window, own_ids, margin + row_shift, margin + col_shift)
            masked = same_image.astype(jnp.bfloat16) * grad_branch[:, branch + 1]
            tap_terms.append(
                jnp.einsum("pk,pc->kc", source, masked, preferred_element_type=jnp.float32)
            )
            incoming = rim_list[branch][
                rim_base - row_shift : rim_base - row_shift + rows_here,
                rim_base - col_shift : rim_base - col_shift + cols_here,
            ].reshape(pixels, branch_width)
            back_image = image_match(window, own_ids, margin - row_shift, margin - col_shift)
            grad_input = grad_input + back_image * transposed(incoming, w_atrous[branch, stencil])
        atrous_terms.append(jnp.stack(tap_terms))
    atrous_term = jnp.stack(atrous_terms)
    shared = (
        lax.psum_scatter(
            point_term.astype(jnp.bfloat16), "rows", scatter_dimension=0, tiled=True
        ).astype(jnp.float32),
        lax.psum_scatter(
            atrous_term.astype(jnp.bfloat16), "rows", scatter_dimension=2, tiled=True
        ).astype(jnp.float32),
        lax.psum_scatter(
            proj_term.astype(jnp.bfloat16), "rows", scatter_dimension=0, tiled=True
        ).astype(jnp.float32),
    )
    shared = (
        lax.psum(shared[0].astype(jnp.bfloat16), "cols").astype(jnp.float32),
        lax.psum(shared[1].astype(jnp.bfloat16), "cols").astype(jnp.float32),
        lax.psum(shared[2].astype(jnp.bfloat16), "cols").astype(jnp.float32),
    )
    grad_gain = jnp.concatenate([gain_sums, pool_gain[None], gain_last[None]], axis=0)
    grad_shift = jnp.concatenate([shift_sums, pool_shift[None], shift_last[None]], axis=0)
    grad_features = grad_input.astype(jnp.bfloat16).reshape(rows_here, cols_here, channels)
    return (
        output,
        grad_features,
        shared[0],
        shared[1],
        grad_pool,
        shared[2],
        grad_gain,
        grad_shift,
    )


def block_order(height, breadth):
    pixel = np.arange(height * breadth).reshape(height, breadth // STEP, STEP).transpose(1, 0, 2).reshape(-1)
    return np.eye(height * breadth, dtype=np.float32)[pixel]


def id_columns(ids):
    height, breadth = ids.shape
    table = ids.reshape(height, breadth // STEP, STEP).transpose(0, 2, 1).reshape(height * STEP, breadth // STEP)
    return jnp.pad(table.astype(F32), ((0, 0), (0, 128 - breadth // STEP)))


def quick_shards(
    features, image_ids, w_point, w_atrous, w_pool, w_proj, norm_gain, norm_shift, cotangent
):
    rows_here, cols_here, channels = features.shape
    branch_width = w_point.shape[1]
    pixels = rows_here * cols_here
    grid_rows, grid_cols = image_ids.shape
    image_count = grid_rows // 16 * (grid_cols // 32)
    images = -(-image_count // 16) * 16
    margin = RATE_TOP
    rows, cols = lax.axis_size("rows"), lax.axis_size("cols")
    row_index = lax.axis_index("rows")
    col_index = lax.axis_index("cols")
    id_padded = jnp.pad(image_ids, margin, constant_values=-1)
    window = lax.dynamic_slice(
        id_padded,
        (row_index * rows_here, col_index * cols_here),
        (rows_here + 2 * margin, cols_here + 2 * margin),
    )
    own_ids = window[margin : margin + rows_here, margin : margin + cols_here]
    own_flat = own_ids.reshape(pixels)
    counts = jnp.sum(
        (image_ids.reshape(-1, 1) == jnp.arange(images, dtype=jnp.int32)[None, :]).astype(F32), axis=0
    )
    counts = jnp.maximum(counts, 1.0)
    count_table = jnp.broadcast_to(counts[:, None], (images, 128))
    order = block_order(rows_here, cols_here)
    order, back = jnp.asarray(order, BF16), jnp.asarray(order.T, BF16)
    output, dz, proj_term, stats, pooled, pool_normed, pool_slope, dap, xsub = forward_call(
        rows, cols, image_count, features.reshape(pixels, channels), order, back, id_columns(window), w_atrous, w_point, w_pool, w_proj,
        norm_gain, norm_shift, cotangent.reshape(pixels, branch_width), count_table,
    )
    output = output.reshape(rows_here, cols_here, branch_width)
    pair_window = lax.dynamic_slice(
        id_padded,
        (row_index // 2 * (2 * rows_here), jnp.int32(margin)),
        (2 * rows_here + 2 * margin, grid_cols),
    )
    grad_input, atrous, point, grad_pool, pool_sums, grad_proj = backward_call(
        rows, cols, image_count, dz, xsub.reshape(2, 8, 4, pixels // 4, -1), id_columns(pair_window), w_atrous, w_point, w_pool,
        norm_gain, count_table, pooled, pool_normed, pool_slope, dap, stats, back, proj_term.reshape(rows, -1, branch_width),
    )
    grad_atrous = atrous.astype(F32).reshape(3, 9, channels // rows, branch_width)

    grad_gain = jnp.concatenate([stats[4:8], pool_sums[1:2], stats[9:10]], axis=0)
    grad_shift = jnp.concatenate([stats[0:4], pool_sums[0:1], stats[8:9]], axis=0)
    grad_features = grad_input.reshape(rows_here, cols_here, channels)
    return (
        output, grad_features, point.astype(F32), grad_atrous, grad_pool,
        grad_proj, grad_gain, grad_shift,
    )


def solution(mesh):
    placed = (P("rows", "cols", None), P(), P(), P(), P(), P(), P(), P(), P("rows", "cols", None))
    quick = mesh.shape["rows"] == 8 and mesh.shape["cols"] == 4
    return jax.shard_map(
        quick_shards if quick else shards,
        mesh=mesh,
        in_specs=placed,
        out_specs=(
            P("rows", "cols", None),
            P("rows", "cols", None),
            P("rows", None),
            P(None, None, "rows", None),
            P("rows", None),
            P("rows", None),
            P(),
            P(),
        ),
        check_vma=False,
    )
```

```python
import functools
import jax
import jax.numpy as jnp
import numpy as np
from jax import lax
from jax.experimental import pallas as pl
from jax.experimental.pallas import tpu as pltpu
from jax.sharding import PartitionSpec as P

MESH = pl.DeviceIdType.MESH
RATE_LOW = 6
RATE_MID = 12
RATE_TOP = 18
STEP = RATE_LOW
REACH = RATE_TOP // STEP
HALO = {1: 48, 2: 80, 3: 112}
SLOTS = 4
epsilon = 1e-05
F32 = jnp.float32
BF16 = jnp.bfloat16


def wide(column, width):
    return jnp.concatenate([column] * (width // column.shape[-1]), axis=-1)


def silu_parts(preact):
    sigma = jax.nn.sigmoid(preact)
    return preact * sigma, sigma * (1.0 + preact * (1.0 - sigma))


def contract_rows(left, right):
    return lax.dot_general(left, right, (((0,), (0,)), ((), ())), preferred_element_type=F32)


def contract_lanes(left, right):
    return lax.dot_general(left, right, (((1,), (1,)), ((), ())), preferred_element_type=F32)


def greet(rows, cols, r, c):
    barrier = pltpu.get_barrier_semaphore()
    near = r + 1 - 2 * lax.rem(r, 2)
    others = [(lax.rem(r + step, rows), c) for step in range(1, rows)]
    for step in range(1, cols):
        others += [(r, lax.rem(c + step, cols)), (near, lax.rem(c + step, cols))]
    for other in others:
        pl.semaphore_signal(barrier, inc=1, device_id=other, device_id_type=MESH)
    pl.semaphore_wait(barrier, len(others))


class Exchange:
    def __init__(self, axis_size, place, to_device, slots, send_sems, recv_sems):
        self.size, self.place, self.to_device = axis_size, place, to_device
        self.slots, self.send_sems, self.recv_sems = slots, send_sems, recv_sems

    def copy(self, step, source=None):
        other = lax.rem(self.place + step, self.size)
        mine = self.slots.at[self.place]
        return pltpu.make_async_remote_copy(
            src_ref=mine if source is None else source(other),
            dst_ref=mine,
            send_sem=self.send_sems.at[step],
            recv_sem=self.recv_sems.at[self.place],
            device_id=self.to_device(other),
            device_id_type=MESH,
        )

    def start(self, source=None):
        for step in range(1, self.size):
            self.copy(step, source).start()

    def arrive(self):
        for step in range(1, self.size):
            other = lax.rem(self.place + step, self.size)
            there = self.slots.at[other]
            pltpu.make_async_remote_copy(
                src_ref=there,
                dst_ref=there,
                send_sem=self.send_sems.at[step],
                recv_sem=self.recv_sems.at[other],
                device_id=self.to_device(other),
                device_id_type=MESH,
            ).wait_recv()

    def leave(self, source=None):
        for step in range(1, self.size):
            self.copy(step, source).wait_send()

    def total(self):
        value = self.slots[0]
        for other in range(1, self.size):
            value = value + self.slots[other]
        return value


def forward_kernel(
    rows, cols, image_count, total_pixels,
    raw_ref, order_ref, back_ref, ids_ref, wat_ref, wpt_ref, wpl_ref, wpj_ref, gain_ref, shift_ref, cot_ref,
    counts_ref, out_ref, dz_ref, pj_ref, stat_ref, pooled_ref, pooln_ref, pools_ref, dap_ref, xsub_ref,
    x_ref, idrep, wbuf, wplbuf, parts, sums_by_row, edge_out, edge_in, rim_out, rim_in, zn, slope, joined, zf, dzf, active, upstream, isum, cbuf, rbuf, pr_buf, pc_buf, pz_buf,
    wsem, wplsem, esend, erecv, hsend, hrecv, csend, crecv, rsend, rrecv, psend, precv, pcsend, pcrecv, pzsend, pzrecv,
    xsend, xrecv,
):
    r, c = lax.axis_index("rows"), lax.axis_index("cols")
    blocks, rb, width = zn.shape[1], zn.shape[2], zn.shape[3]
    pixels = blocks * rb
    own = REACH * 36
    images = isum.shape[0]
    taps = 27

    def weight_copy(n):
        branch, tap = 2 - n // 9, lax.rem(n, 9)
        slot = lax.rem(n, SLOTS)
        return pltpu.make_async_copy(wat_ref.at[branch, tap], wbuf.at[slot], wsem.at[slot])

    for n in range(SLOTS - 1):
        weight_copy(jnp.int32(n)).start()
    share = x_ref.shape[1] // rows
    pool_weight = pltpu.make_async_copy(
        wpl_ref.at[pl.ds(pl.multiple_of(r * share, share), share)], wplbuf, wplsem
    )
    pool_weight.start()
    for block in range(idrep.shape[0]):
        idrep[block] = jnp.broadcast_to(ids_ref[:, block : block + 1], idrep.shape[1:])
    greet(rows, cols, r, c)

    @pl.loop(0, x_ref.shape[1] // 256)
    def _(n):
        piece = pl.ds(pl.multiple_of(n * 256, 256), 256)
        x_ref[:, piece] = jnp.dot(order_ref[...], raw_ref[:, piece], preferred_element_type=F32).astype(BF16)

    own_ids = jnp.concatenate([idrep[REACH + a, own : own + rb, :] for a in range(blocks)], axis=0)
    lanes = lax.broadcasted_iota(jnp.int32, (pixels, 128), 1).astype(F32)
    one_hot = jnp.concatenate(
        [(own_ids == lanes + 128.0 * part).astype(F32).astype(BF16) for part in range(pl.cdiv(images, 128))],
        axis=1,
    )
    for part in range(rows):
        piece = slice(part * share, (part + 1) * share)
        isum[:, piece] = contract_rows(one_hot, x_ref[:, piece])[:images]
    pool_rows = Exchange(rows, r, lambda other: (other, c), pr_buf, psend, precv)

    def share_of(other):
        return isum.at[:, pl.ds(pl.multiple_of(other * share, share), share)]

    pr_buf[r] = isum[:, pl.ds(pl.multiple_of(r * share, share), share)]
    pool_rows.start(share_of)

    def side_copies(m):
        return [
            (
                (c > 0, c < cols - 1)[way],
                (c < cols - 1, c > 0)[way],
                pltpu.make_async_remote_copy(
                    src_ref=edge_out[m - 1].at[way],
                    dst_ref=edge_in[m - 1].at[way],
                    send_sem=esend.at[m - 1, way],
                    recv_sem=erecv.at[m - 1, way],
                    device_id=(r, lax.rem(c + (cols - 1, 1)[way], cols)),
                    device_id_type=MESH,
                ),
            )
            for way in range(2)
        ]

    def rim_copies(m):
        return [
            (
                (r > 0, r < rows - 1)[way],
                (r < rows - 1, r > 0)[way],
                pltpu.make_async_remote_copy(
                    src_ref=rim_out[m - 1].at[way],
                    dst_ref=rim_in[m - 1].at[way],
                    send_sem=hsend.at[m - 1, way],
                    recv_sem=hrecv.at[m - 1, way],
                    device_id=(lax.rem(r + (rows - 1, 1)[way], rows), c),
                    device_id_type=MESH,
                ),
            )
            for way in range(2)
        ]

    def conv(position, m):
        lines = parts[m - 1]

        @pl.loop(0, blocks + 2 * m)
        def _(block):
            for i in range(3):
                lines[i, block] = jnp.zeros(lines.shape[2:], F32)

        @pl.loop(0, 9)
        def _(tap):
            i, j = tap // 3, lax.rem(tap, 3)
            n = position * 9 + tap
            slot = lax.rem(n, SLOTS)
            ahead = n + SLOTS - 1

            @pl.when(ahead < taps)
            def _():
                weight_copy(ahead).start()

            weight_copy(n).wait()
            product = jnp.dot(x_ref[...], wbuf[slot], preferred_element_type=F32)
            for a in range(blocks):
                same = idrep[REACH + a, own : own + rb] == idrep[REACH + a - (j - 1) * m, own : own + rb]
                part = product[a * rb : (a + 1) * rb]
                lines[i, a + (2 - j) * m] += jnp.where(wide(same.astype(F32), width) > 0.0, part, 0.0)

        @pl.loop(0, 3)
        def _(i):
            for a in range(m):
                edge_out[m - 1][0, i, a] = lines[i, a].astype(BF16)
                edge_out[m - 1][1, i, a] = lines[i, m + blocks + a].astype(BF16)

        for sends, _, copy in side_copies(m):
            pl.when(sends)(copy.start)

    def absorb(m):
        height, lines, whole = HALO[m], parts[m - 1], sums_by_row[m - 1]
        for way, (_, receives, copy) in enumerate(side_copies(m)):
            @pl.when(receives)
            def _():
                copy.wait_recv()
                for i in range(3):
                    for a in range(m):
                        lines[i, (blocks, m)[way] + a] += edge_in[m - 1][way, i, a].astype(F32)

        @pl.loop(0, blocks)
        def _(a):
            whole[a, 0:height] = jnp.zeros((height, width), F32)
            whole[a, height : height + rb] = lines[1, m + a]
            whole[a, height + rb : 2 * height + rb] = jnp.zeros((height, width), F32)
            for i in (0, 2):
                up = (i - 1) * 36 * m
                same = idrep[REACH + a, own : own + rb] == idrep[REACH + a, own - up : own - up + rb]
                whole[a, height - up : height - up + rb] += jnp.where(
                    wide(same.astype(F32), width) > 0.0, lines[i, m + a], 0.0
                )
            rim_out[m - 1][0, a] = whole[a, 0:height].astype(BF16)
            rim_out[m - 1][1, a] = whole[a, height + rb : 2 * height + rb].astype(BF16)

        for sends, _, copy in rim_copies(m):
            pl.when(sends)(copy.start)

    def finish(m):
        height, whole = HALO[m], sums_by_row[m - 1]

        @pl.loop(0, blocks)
        def _(a):
            zn[m, a] = whole[a, height : height + rb]

        for way, (_, receives, copy) in enumerate(rim_copies(m)):
            @pl.when(receives)
            def _():
                copy.wait_recv()
                start = (rb - height, 0)[way]
                for a in range(blocks):
                    zn[m, a, start : start + height] += rim_in[m - 1][way, a].astype(F32)

    members = [(dy, dx, dk) for dy in range(2) for dx in range(2) for dk in range(2)]
    half = share // 2

    def channel_slices(y, x, k):
        return [pl.multiple_of((2 * (2 * k + l) + y) * share + x * half, 128) for l in range(2)]

    def member_copies(steps, slices):
        mine = lax.rem(r, 2) * cols + c
        copies = []
        for step in steps:
            dy, dx, dk = members[step]
            y, x, k = lax.rem(r + dy, 2), lax.rem(c // 2 + dx, 2), lax.rem(c + dk, 2)
            starts = channel_slices(y, x, k)
            for l in slices:
                source = x_ref.at[:, pl.ds(starts[l], half)]
                target = xsub_ref.at[l, mine]
                if step == 0:
                    copies.append(pltpu.make_async_copy(source, target, xrecv.at[l, mine]))
                else:
                    copies.append(
                        pltpu.make_async_remote_copy(
                            src_ref=source,
                            dst_ref=target,
                            send_sem=xsend.at[l, step],
                            recv_sem=xrecv.at[l, mine],
                            device_id=(2 * (r // 2) + y, 2 * x + k),
                            device_id_type=MESH,
                        )
                    )
        return copies

    def send_members(steps, slices):
        for copy in member_copies(steps, slices):
            copy.start()

    pool_cols = Exchange(cols, c, lambda other: (r, other), pc_buf, pcsend, pcrecv)
    pool_z = Exchange(rows, r, lambda other: (other, c), pz_buf, pzsend, pzrecv)
    send_members(range(8), (0,))
    send_members((0, 1), (1,))
    conv(0, 3)
    pool_rows.arrive()
    pc_buf[c] = pool_rows.total()
    pool_cols.start()
    conv(1, 2)
    absorb(3)
    pool_cols.arrive()
    counts = counts_ref[...]
    pooled = (pool_cols.total() / wide(counts, share)).astype(BF16)
    pooled_ref[...] = pooled
    pool_weight.wait()
    pz_buf[r] = jnp.dot(pooled, wplbuf[...], preferred_element_type=F32)
    pool_z.start()
    conv(2, 1)
    absorb(2)
    product = jnp.dot(x_ref[...], wpt_ref[...], preferred_element_type=F32)
    for a in range(blocks):
        zn[0, a] = product[a * rb : (a + 1) * rb]
    absorb(1)
    pool_z.arrive()
    zp = pool_z.total()
    pool_avg = jnp.sum(zp, axis=0, keepdims=True) / image_count
    pool_square = jnp.sum(zp * zp, axis=0, keepdims=True) / image_count
    pool_inverse = lax.rsqrt(pool_square - pool_avg * pool_avg + epsilon)
    pool_normed = (zp - pool_avg) * pool_inverse
    pool_active, pool_slope = silu_parts(gain_ref[4:5] * pool_normed + shift_ref[4:5])
    pooln_ref[...] = pool_normed
    pools_ref[...] = pool_slope
    spare = one_hot.shape[1] - images
    pool_active = jnp.concatenate([pool_active, jnp.zeros((spare, width), F32)], axis=0).astype(BF16)
    joined[:, 4 * width : 5 * width] = jnp.dot(one_hot, pool_active, preferred_element_type=F32).astype(BF16)

    for m in (3, 2, 1):
        finish(m)

    started = []

    def all_sum(step, value, meanwhile=(None, None)):
        across = Exchange(cols, c, lambda other: (r, other), cbuf.at[step], csend.at[step], crecv.at[step])
        cbuf[step, c] = value
        across.start()
        if meanwhile[0]:
            meanwhile[0]()
        across.arrive()
        down = Exchange(rows, r, lambda other: (other, c), rbuf.at[step], rsend.at[step], rrecv.at[step])
        rbuf[step, r] = across.total()
        down.start()
        if meanwhile[1]:
            meanwhile[1]()
        down.arrive()
        started.extend((across, down))
        return down.total()

    zero = jnp.zeros((1, width), F32)

    def row_sum(value):
        return jnp.sum(value, axis=0, keepdims=True)

    firsts, seconds = [], []
    for k in range(4):
        first, second = zero, zero
        for a in range(blocks):
            value = zn[k, a]
            first, second = first + row_sum(value), second + row_sum(value * value)
        firsts.append(first)
        seconds.append(second)
    moments = all_sum(0, jnp.concatenate(firsts + seconds, axis=0))
    send_members((6, 7), (1,))
    average = moments[0:4] / total_pixels
    inverse = lax.rsqrt(moments[4:8] / total_pixels - average * average + epsilon)
    for k in range(4):
        @pl.loop(0, blocks)
        def _(a):
            normed = (zn[k, a] - average[k : k + 1]) * inverse[k : k + 1]
            value, slant = silu_parts(gain_ref[k : k + 1] * normed + shift_ref[k : k + 1])
            zn[k, a] = normed
            slope[k, a] = slant
            joined[pl.ds(pl.multiple_of(a * rb, rb), rb), k * width : (k + 1) * width] = value.astype(BF16)

    zf[...] = jnp.dot(joined[...], wpj_ref[...], preferred_element_type=F32)
    first, second = zero, zero
    for a in range(blocks):
        value = zf[a * rb : (a + 1) * rb]
        first, second = first + row_sum(value), second + row_sum(value * value)

    def put_upstream():
        upstream[...] = jnp.dot(order_ref[...], cot_ref[...], preferred_element_type=F32)

    moments = all_sum(1, jnp.concatenate([first, second] + [zero] * 6, axis=0), (None, put_upstream))
    final_avg = moments[0:1] / total_pixels
    final_inverse = lax.rsqrt(moments[1:2] / total_pixels - final_avg * final_avg + epsilon)
    shift_last, gain_last = zero, zero
    for a in range(blocks):
        piece = slice(a * rb, (a + 1) * rb)
        normed = (zf[piece] - final_avg) * final_inverse
        result, slant = silu_parts(gain_ref[5:6] * normed + shift_ref[5:6])
        active[piece] = result.astype(BF16)
        grad = upstream[piece] * slant
        zf[piece] = normed
        dzf[piece] = grad
        shift_last, gain_last = shift_last + row_sum(grad), gain_last + row_sum(grad * normed)

    def put_output():
        out_ref[...] = jnp.dot(back_ref[...], active[...], preferred_element_type=F32).astype(BF16)

    sums = all_sum(2, jnp.concatenate([shift_last, gain_last] + [zero] * 6, axis=0), (None, put_output))
    send_members((2, 4, 3, 5), (1,))
    shift_last, gain_last = sums[0:1], sums[1:2]
    gain = gain_ref[5:6]
    for a in range(blocks):
        piece = slice(a * rb, (a + 1) * rb)
        dzf[piece] = final_inverse * (
            dzf[piece] * gain
            - gain * shift_last / total_pixels
            - zf[piece] * (gain * gain_last / total_pixels)
        )
    grad_final = dzf[...].astype(BF16)

    shifts, gains = [], []
    for k in range(4):
        grad = contract_lanes(grad_final, wpj_ref[k * width : (k + 1) * width])
        shift_sum, gain_sum = zero, zero
        for a in range(blocks):
            part = grad[a * rb : (a + 1) * rb] * slope[k, a]
            slope[k, a] = part
            shift_sum, gain_sum = shift_sum + row_sum(part), gain_sum + row_sum(part * zn[k, a])
        shifts.append(shift_sum)
        gains.append(gain_sum)

    def put_images():
        grad_pixel = contract_lanes(grad_final, wpj_ref[4 * width : 5 * width])
        upper = grad_pixel.astype(BF16)
        lower = (grad_pixel - upper.astype(F32)).astype(BF16)
        dap_ref[...] = (contract_rows(one_hot, upper) + contract_rows(one_hot, lower))[:images]

    def put_projection():
        for k in range(5):
            piece = slice(k * width, (k + 1) * width)
            pj_ref[piece] = contract_rows(joined[:, piece], grad_final).astype(BF16)

    sums = all_sum(3, jnp.concatenate(shifts + gains, axis=0), (put_images, put_projection))
    for k in range(4):
        gain = gain_ref[k : k + 1]
        from_shift = gain * sums[k : k + 1] / total_pixels
        from_gain = gain * sums[4 + k : 5 + k] / total_pixels

        @pl.loop(0, blocks)
        def _(a):
            dz_ref[k, a] = (
                inverse[k : k + 1] * (slope[k, a] * gain - from_shift - zn[k, a] * from_gain)
            ).astype(BF16)

    stat_ref[...] = jnp.concatenate([sums, shift_last, gain_last, pool_inverse] + [zero] * 5, axis=0)

    pool_rows.leave(share_of)
    for exchange in (pool_cols, pool_z, *started):
        exchange.leave()
    for m in (3, 2, 1):
        for sends, _, copy in side_copies(m) + rim_copies(m):
            pl.when(sends)(copy.wait_send)
    for copy in member_copies((0,), (0, 1)):
        copy.wait()
    for copy in member_copies(range(1, 8), (0, 1)):
        copy.wait_send()
    for l in range(2):
        for step, (dy, dx, dk) in enumerate(members):
            if step:
                y, x, k = lax.rem(r + dy, 2), lax.rem(c // 2 + dx, 2), lax.rem(c + dk, 2)
                there = xsub_ref.at[l, y * cols + 2 * x + k]
                pltpu.make_async_remote_copy(
                    src_ref=there,
                    dst_ref=there,
                    send_sem=xsend.at[l, step],
                    recv_sem=xrecv.at[l, y * cols + 2 * x + k],
                    device_id=(2 * (r // 2) + y, 2 * x + k),
                    device_id_type=MESH,
                ).wait_recv()


def forward_call(rows, cols, image_count, x, order, back, ids, wat, wpt, wpl, wpj, gain, shift, cot, counts):
    pixels, channels = x.shape
    width = wpt.shape[1]
    blocks, rb = 4, pixels // 4
    images = counts.shape[0]
    share = channels // rows
    total_pixels = float(pixels * rows * cols)
    vmem = pl.BlockSpec(memory_space=pltpu.VMEM)
    hbm = pl.BlockSpec(memory_space=pl.ANY)

    def each(shape, kind):
        return [pltpu.VMEM(shape(m) + (width,), kind) for m in (1, 2, 3)]

    dma = pltpu.SemaphoreType.DMA
    return pl.pallas_call(
        functools.partial(forward_kernel, rows, cols, float(image_count), total_pixels),
        out_shape=(
            jax.ShapeDtypeStruct((pixels, width), BF16),
            jax.ShapeDtypeStruct((4, blocks, rb, width), BF16),
            jax.ShapeDtypeStruct((5 * width, width), BF16),
            jax.ShapeDtypeStruct((16, width), F32),
            jax.ShapeDtypeStruct((images, share), BF16),
            jax.ShapeDtypeStruct((images, width), F32),
            jax.ShapeDtypeStruct((images, width), F32),
            jax.ShapeDtypeStruct((images, width), F32),
            jax.ShapeDtypeStruct((2, 8, pixels, share // 2), BF16),
        ),
        in_specs=[vmem, vmem, vmem, vmem, hbm, vmem, hbm, vmem, vmem, vmem, vmem, vmem],
        out_specs=(vmem,) * 8 + (hbm,),
        scratch_shapes=[
            pltpu.VMEM((pixels, channels), BF16),
            pltpu.VMEM((blocks + 2 * REACH, ids.shape[0], 128), F32),
            pltpu.VMEM((SLOTS, channels, width), BF16),
            pltpu.VMEM((share, width), BF16),
            each(lambda m: (3, blocks + 2 * m, rb), F32),
            each(lambda m: (blocks, 2 * HALO[m] + rb), F32),
            each(lambda m: (2, 3, m, rb), BF16), each(lambda m: (2, 3, m, rb), BF16),
            each(lambda m: (2, blocks, HALO[m]), BF16), each(lambda m: (2, blocks, HALO[m]), BF16),
            pltpu.VMEM((4, blocks, rb, width), F32),
            pltpu.VMEM((4, blocks, rb, width), F32),
            pltpu.VMEM((pixels, 5 * width), BF16),
            pltpu.VMEM((pixels, width), F32),
            pltpu.VMEM((pixels, width), F32),
            pltpu.VMEM((pixels, width), BF16),
            pltpu.VMEM((pixels, width), F32),
            pltpu.VMEM((images, channels), F32),
            pltpu.VMEM((4, cols, 8, width), F32),
            pltpu.VMEM((4, rows, 8, width), F32),
            pltpu.VMEM((rows, images, share), F32),
            pltpu.VMEM((cols, images, share), F32),
            pltpu.VMEM((rows, images, width), F32),
            dma((SLOTS,)), dma,
            dma((3, 2)), dma((3, 2)), dma((3, 2)), dma((3, 2)),
            dma((4, cols)), dma((4, cols)),
            dma((4, rows)), dma((4, rows)),
            dma((rows,)), dma((rows,)),
            dma((cols,)), dma((cols,)),
            dma((rows,)), dma((rows,)),
            dma((2, 8)), dma((2, 8)),
        ],
        compiler_params=pltpu.CompilerParams(
            collective_id=0, has_side_effects=True, vmem_limit_bytes=60 * 2**20
        ),
        cost_estimate=pl.CostEstimate(flops=2 * pixels * channels * width * 28, bytes_accessed=40_000_000, transcendentals=0),
    )(x, order, back, ids, wat, wpt, wpl, wpj, gain, shift, cot, counts)


def backward_kernel(
    rows, cols, image_count, height,
    dz_ref, xsub_ref, ids_ref, wat_ref, wpt_ref, wpl_ref, gain_ref, counts_ref,
    pooled_ref, pooln_ref, pools_ref, dap_ref, stat_ref, back_ref, pj_ref,
    gx_ref, dw_ref, dpoint_ref, gpool_ref, gstat_ref, gproj_ref,
    ext0, ext1, ext2, ext3, shifted, colmask, idrep, gmat, gown, xt, acc, wbuf, wpt,
    send1, recv1, keep, relay, dw, pcbuf, prbuf, quarters, quarter_sums, row_parts, final_parts,
    xsem, wsem, wptsem, zsend, zrecv, agsend, agrecv, s1send, s1recv, s2send, s2recv, s3send, s3recv,
    pcsend, pcrecv, prsend, prrecv, qsend, qrecv, rqsend, rqrecv, fqsend, fqrecv, outsem,
):
    r, c = lax.axis_index("rows"), lax.axis_index("cols")
    z, y = r // 2, lax.rem(r, 2)
    x, k = c // 2, lax.rem(c, 2)
    levels = rows // 2
    z_lo, z_hi = lax.rem(z, 2), z // 2
    blocks, rb, width = dz_ref.shape[1:]
    pair = 2 * rb
    across = cols * blocks
    pixels = blocks * rb
    own = REACH * 36
    half = xt.shape[0] // 2
    images = dap_ref.shape[0]
    ext = {0: ext0, 1: ext1, 2: ext2, 3: ext3}
    tall = {0: 0, **HALO}

    def x_copy(l, dev, a):
        dev_y, dev_c = dev // cols, lax.rem(dev, cols)
        start = pl.multiple_of((dev_c * blocks + a) * pair + dev_y * rb, 16)
        return pltpu.make_async_copy(
            xsub_ref.at[l, dev, a], gmat.at[pl.ds(start, rb), pl.ds(l * half, half)], xsem.at[l, dev, a]
        )

    for l in range(2):
        for a in range(blocks):
            @pl.loop(0, 2 * cols)
            def _(dev):
                x_copy(l, dev, a).start()

    groups = [[(0, 4), (1, 4), (2, 4)]]
    for m in (1, 2, 3):
        groups += [[(m - 1, 0), (m - 1, 1), (m - 1, 2)], [(m - 1, 6), (m - 1, 7), (m - 1, 8)], [(m - 1, 3), (m - 1, 5)]]

    def weight_copies(n):
        return [
            pltpu.make_async_copy(
                wat_ref.at[branch, tap], wbuf.at[n % 2, :, pl.ds(place * width, width)], wsem.at[n % 2, place]
            )
            for place, (branch, tap) in enumerate(groups[n])
        ]

    point_copy = pltpu.make_async_copy(wpt_ref, wpt, wptsem)
    point_copy.start()
    for n in range(2):
        for copy in weight_copies(n):
            copy.start()

    greet(rows, cols, r, c)

    def has_rim(dev_y):
        return (dev_y == 1) & (z >= 1) | (dev_y == 0) & (z <= levels - 2)

    def rim_copy(m, sending):
        high = tall[m]
        start = pl.multiple_of(y * (rb - high), 16)
        target = pl.multiple_of((1 - y) * (high + pair), 16)
        return pltpu.make_async_remote_copy(
            src_ref=dz_ref.at[m, :, pl.ds(start, high)],
            dst_ref=ext[m].at[pl.ds(c * blocks, blocks), pl.ds(target, high)],
            send_sem=zsend.at[m],
            recv_sem=zrecv.at[m],
            device_id=(lax.rem(r + 4 * y - 2 + rows, rows), c),
            device_id_type=MESH,
        )

    sends_rim = (y == 1) & (z <= levels - 2) | (y == 0) & (z >= 1)

    def item(m, kind, dev_y, dev_c, first=0, count=None):
        high = tall[m]
        count = blocks if count is None else count
        start = high + rb * dev_y if kind == 0 else (1 - dev_y) * (high + pair)
        height = rb if kind == 0 else high
        return ext[m].at[pl.ds(dev_c * blocks + first, count), pl.ds(pl.multiple_of(start, 16), height)]

    def gather_copy(m, kind, dev_y, dev_c, slot, target, first=0, count=None):
        piece = item(m, kind, dev_y, dev_c, first, count)
        return pltpu.make_async_remote_copy(
            src_ref=piece,
            dst_ref=piece,
            send_sem=agsend.at[m, kind, slot],
            recv_sem=agrecv.at[m, kind, 2 * cols if first else dev_y * cols + dev_c],
            device_id=target,
            device_id_type=MESH,
        )

    most = blocks // 2
    side = 2 * (1 - x) + k
    sibling, beside, below = (r, 2 * x + 1 - k), (r, side), (2 * z + 1 - y, c)

    def if_there(kind, dev_y, action):
        if kind == 0:
            action()
        else:
            pl.when(has_rim(dev_y))(action)

    def kinds(m):
        return (0,) if m == 0 else (0, 1)

    def own_copies(m, kind):
        return [gather_copy(m, kind, y, c, slot, to) for slot, to in enumerate((beside, below, sibling))]

    def side_copies(m, kind):
        return [gather_copy(m, kind, y, side, 3, below, 0, most), gather_copy(m, kind, y, side, 5, sibling)]

    def below_copies(m, kind):
        return [
            gather_copy(m, kind, 1 - y, c, 4, beside, most, blocks - most),
            gather_copy(m, kind, 1 - y, c, 6, sibling),
        ]

    def diagonal_copies(m, kind):
        return [gather_copy(m, kind, 1 - y, side, 7, sibling)]

    def start_own(m, kind):
        if kind == 0:
            high = tall[m]
            for a in range(blocks):
                ext[m][c * blocks + a, pl.ds(pl.multiple_of(high + rb * y, 16), rb)] = dz_ref[m, a]

        def action():
            if kind == 1:
                rim_copy(m, False).wait_recv()
            for copy in own_copies(m, kind):
                copy.start()

        if_there(kind, y, action)

    def pass_on(m):
        for kind in kinds(m):
            def from_side():
                gather_copy(m, kind, y, side, 0, beside).wait_recv()
                for copy in side_copies(m, kind):
                    copy.start()

            def from_below():
                gather_copy(m, kind, 1 - y, c, 0, below).wait_recv()
                for copy in below_copies(m, kind):
                    copy.start()

            if_there(kind, y, from_side)
            if_there(kind, 1 - y, from_below)

    def pass_last(m):
        for kind in kinds(m):
            def action():
                gather_copy(m, kind, 1 - y, side, 0, below, 0, most).wait_recv()
                gather_copy(m, kind, 1 - y, side, 0, beside, most, blocks - most).wait_recv()
                for copy in diagonal_copies(m, kind):
                    copy.start()

            if_there(kind, 1 - y, action)

    def finish_gather(m):
        for kind in kinds(m):
            for dev_y in (y, 1 - y):
                for dev_c in (c, side):
                    piece = gather_copy(m, kind, dev_y, dev_c + 1 - 2 * k, 0, sibling)
                    if_there(kind, dev_y, piece.wait_recv)

    def finish_sends(m):
        for kind in kinds(m):
            def action():
                for copy in own_copies(m, kind) + side_copies(m, kind):
                    copy.wait_send()

            def below_action():
                for copy in below_copies(m, kind) + diagonal_copies(m, kind):
                    copy.wait_send()

            if_there(kind, y, action)
            if_there(kind, 1 - y, below_action)

    for m in (1, 2, 3):
        pl.when(sends_rim)(rim_copy(m, True).start)
    start_own(1, 0)

    pool_cols = Exchange(cols, c, lambda other: (r, other), pcbuf, pcsend, pcrecv)
    pcbuf[c] = dap_ref[...]
    pool_cols.start()

    tall_piece, wide_piece = quarters.shape[2], quarters.shape[3]

    def quarter(other):
        rows_of = pl.ds(pl.multiple_of(lax.rem(other, 2) * tall_piece, 16), tall_piece)
        return pj_ref.at[:, rows_of, pl.ds(pl.multiple_of(other // 2 * wide_piece, 128), wide_piece)]

    proj_cols = Exchange(cols, c, lambda other: (r, other), quarters, qsend, qrecv)
    proj_rows = Exchange(rows, r, lambda other: (other, c), row_parts, rqsend, rqrecv)
    proj_last = Exchange(cols, c, lambda other: (r, other), final_parts, fqsend, fqrecv)
    own_rows = pl.ds(pl.multiple_of(k * tall_piece, 16), tall_piece)
    quarters[c] = pj_ref[:, own_rows, pl.ds(pl.multiple_of(x * wide_piece, 128), wide_piece)]
    proj_cols.start(quarter)

    def whole_sum(slots, count):
        value = slots[0].astype(F32)
        for other in range(1, count):
            value = value + slots[other].astype(F32)
        return value

    def proj_down():
        proj_cols.arrive()
        quarter_sums[...] = whole_sum(quarters, cols).astype(BF16)
        row_parts[r] = quarter_sums[r]
        proj_rows.start(lambda other: quarter_sums.at[other])

    def proj_spread():
        proj_rows.arrive()
        final_parts[c] = whole_sum(row_parts, rows).astype(BF16)
        proj_last.start()

    for block in range(across):
        idrep[block] = jnp.broadcast_to(ids_ref[:, block : block + 1], idrep.shape[1:])
    for m in (1, 2, 3):
        high = tall[m]

        @pl.when(z == 0)
        def _():
            @pl.loop(0, across)
            def _(block):
                ext[m][block, 0:high] = jnp.zeros((high, width), BF16)

        @pl.when(z == levels - 1)
        def _():
            @pl.loop(0, across)
            def _(block):
                ext[m][block, high + pair : 2 * high + pair] = jnp.zeros((high, width), BF16)

    for shift in range(-REACH, REACH + 1):
        for block in range(across):
            if 0 <= block - shift < across:
                same = idrep[block, own : own + 48] == idrep[block - shift, own : own + 48]
                colmask[REACH + shift, block] = wide(same.astype(F32), width).astype(BF16)
            else:
                colmask[REACH + shift, block] = jnp.zeros((48, width), BF16)

    start_own(1, 1)
    start_own(2, 0)
    start_own(2, 1)
    for l in range(2):
        for a in range(blocks):
            @pl.loop(0, 2 * cols)
            def _(dev):
                x_copy(l, dev, a).wait()

        spot = pl.multiple_of(lax.rem(l + z_lo, 2) * half, half)
        for chunk in range(gmat.shape[0] // 128):
            piece = slice(chunk * 128, (chunk + 1) * 128)
            xt[pl.ds(spot, half), piece] = gmat[piece, l * half : (l + 1) * half].astype(F32).T.astype(BF16)

    pass_on(1)
    start_own(3, 0)
    start_own(3, 1)

    point_copy.wait()

    @pl.loop(0, wpt.shape[0] // 256)
    def _(n):
        piece = pl.ds(pl.multiple_of(n * 256, 256), 256)
        left = jnp.concatenate([dz_ref[0, a] for a in range(blocks)], axis=0)
        acc[:, piece] = contract_lanes(left, wpt[piece, :])

    pool_copy = pltpu.make_async_copy(wpl_ref, wpt, wptsem)
    pool_copy.start()

    def build_shifted(m):
        high = tall[m]

        @pl.loop(0, across)
        def _(block):
            whole = ext[m][block].astype(F32)
            for i in range(3):
                down = (i - 1) * 36 * m
                value = whole[high - down : high - down + pair]
                if i != 1:
                    same = idrep[block, own : own + pair] == idrep[block, own - down : own - down + pair]
                    value = jnp.where(wide(same.astype(F32), width) > 0.0, value, 0.0)
                shifted[i, block] = value.astype(BF16)

    def masked(values, mask):
        count = values.shape[0] // 48
        return jnp.concatenate([values[48 * n : 48 * (n + 1)] * mask for n in range(count)], axis=0)

    def scatter_first(n, part):
        keep[n] = part[:half]
        send1[n] = part[half:].astype(BF16)
        stage1(n).start()

    def stage1(n):
        return pltpu.make_async_remote_copy(
            src_ref=send1.at[n], dst_ref=recv1.at[n], send_sem=s1send.at[n], recv_sem=s1recv.at[n],
            device_id=(r + 2 - 4 * z_lo, c), device_id_type=MESH,
        )

    def stage2(n):
        return pltpu.make_async_remote_copy(
            src_ref=relay.at[n], dst_ref=relay.at[n], send_sem=s2send.at[n], recv_sem=s2recv.at[n],
            device_id=(lax.rem(r + rows // 2, rows), c), device_id_type=MESH,
        )

    def stage3(n, from_x, slot, target):
        piece = dw.at[n, pl.ds(pl.multiple_of(from_x * half, half), half)]
        return pltpu.make_async_remote_copy(
            src_ref=piece, dst_ref=piece, send_sem=s3send.at[slot, n], recv_sem=s3recv.at[from_x, n],
            device_id=target, device_id_type=MESH,
        )

    last = z_hi == k

    def drain2(start, count):
        @pl.loop(start, start + count)
        def _(n):
            stage1(n).wait_recv()
            total = keep[n] + recv1[n].astype(F32)

            @pl.when(last)
            def _():
                keep[n] = total

            @pl.when(jnp.logical_not(last))
            def _():
                relay[n] = total.astype(BF16)
                stage2(n).start()

    def drain3(start, count):
        @pl.when(last)
        def _():
            @pl.loop(start, start + count)
            def _(n):
                stage2(n).wait_recv()
                dw[n, pl.ds(pl.multiple_of(x * half, half), half)] = (keep[n] + relay[n].astype(F32)).astype(BF16)
                stage3(n, x, 0, beside).start()
                stage3(n, x, 1, sibling).start()

    def drain4(start, count):
        @pl.when(last)
        def _():
            @pl.loop(start, start + count)
            def _(n):
                copy = stage3(n, 1 - x, 2, sibling)
                copy.wait_recv()
                copy.start()

        @pl.when(jnp.logical_not(last))
        def _():
            @pl.loop(start, start + count)
            def _(n):
                stage3(n, 0, 0, sibling).wait_recv()
                stage3(n, 1, 0, sibling).wait_recv()

    def weight_grad(m, between):
        @pl.loop(0, 9)
        def _(tap):
            for when, action in between.items():
                pl.when(tap == when)(action)
            i, j = tap // 3, lax.rem(tap, 3)
            shift = (j - 1) * m

            @pl.loop(0, across)
            def _(block):
                source = lax.rem(block - shift + across, across)
                gmat[pl.ds(pl.multiple_of(block * pair, 16), pair)] = masked(
                    shifted[i, source], colmask[REACH + shift, block]
                )

            scatter_first((m - 1) * 9 + tap, jnp.dot(xt[...], gmat[...], preferred_element_type=F32))

    def add_products(n, depth):
        for copy in weight_copies(n):
            copy.wait()

        @pl.loop(0, wbuf.shape[1] // 256)
        def _(chunk):
            piece = pl.ds(pl.multiple_of(chunk * 256, 256), 256)
            acc[:, piece] += contract_lanes(gown[:, :depth], wbuf[n % 2, piece, :depth])

        if n + 2 < len(groups):
            for copy in weight_copies(n + 2):
                copy.start()

    def feature_grad(m, lines):
        for line in lines:
            n = 1 + (m - 1) * 3 + line
            first, step = groups[n][0][1], groups[n][1][1] - groups[n][0][1]

            @pl.loop(0, len(groups[n]))
            def _(place):
                tap = first + step * place
                shift = (lax.rem(tap, 3) - 1) * m
                for a in range(blocks):
                    block = c * blocks + a
                    source = lax.rem(block - shift + across, across)
                    gown[a * rb : (a + 1) * rb, pl.ds(pl.multiple_of(place * width, width), width)] = masked(
                        shifted[tap // 3, source, pl.ds(pl.multiple_of(y * rb, 16), rb)],
                        colmask[REACH + shift, block],
                    )

            add_products(n, len(groups[n]) * width)

    for m in (1, 2, 3):
        for a in range(blocks):
            gown[a * rb : (a + 1) * rb, (m - 1) * width : m * width] = dz_ref[m, a]
    add_products(0, 3 * width)
    pass_last(1)
    finish_gather(1)
    build_shifted(1)

    def second_on():
        pass_on(2)
        start_own(0, 0)

    weight_grad(1, {4: second_on, 7: proj_down})
    pass_last(2)
    feature_grad(1, (0,))
    pass_on(3)
    drain2(0, 9)
    feature_grad(1, (1, 2))
    finish_gather(2)
    build_shifted(2)

    def third_last():
        pass_on(0)
        pass_last(3)

    weight_grad(2, {2: proj_spread, 5: third_last})
    pass_last(0)
    drain3(0, 9)
    feature_grad(2, (0,))
    drain2(9, 9)
    feature_grad(2, (1, 2))
    finish_gather(3)
    build_shifted(3)
    weight_grad(3, {})
    finish_gather(0)

    @pl.loop(0, across)
    def _(block):
        gmat[pl.ds(pl.multiple_of(block * pair, 16), pair)] = ext0[block]

    scatter_first(27, jnp.dot(xt[...], gmat[...], preferred_element_type=F32))
    drain4(0, 9)
    drain3(9, 9)

    pool_cols.arrive()
    pool_rows = Exchange(rows, r, lambda other: (other, c), prbuf, prsend, prrecv)
    prbuf[r] = pool_cols.total()
    pool_rows.start()
    feature_grad(3, (0, 1))
    drain2(18, 10)
    feature_grad(3, (2,))
    drain4(9, 9)
    pool_rows.arrive()
    normed = pooln_ref[...]
    grad = pool_rows.total() * pools_ref[...]
    shift_sum = jnp.sum(grad, axis=0, keepdims=True)
    gain_sum = jnp.sum(grad * normed, axis=0, keepdims=True)
    gain = gain_ref[4:5]
    grad_z = (
        stat_ref[10:11]
        * (grad * gain - gain * shift_sum / image_count - normed * (gain * gain_sum / image_count))
    ).astype(BF16)
    gpool_ref[...] = contract_rows(pooled_ref[...], grad_z)
    gstat_ref[...] = jnp.concatenate([shift_sum, gain_sum] + [jnp.zeros((1, width), F32)] * 6, axis=0)
    own_ids = jnp.concatenate([idrep[c * blocks + a, own : own + pair] for a in range(blocks)], axis=0)
    upper_row = jnp.broadcast_to((y == 0).astype(F32), (pixels, 128))
    own_ids = jnp.where(
        upper_row > 0.0,
        jnp.concatenate([own_ids[a * pair : a * pair + rb] for a in range(blocks)], axis=0),
        jnp.concatenate([own_ids[a * pair + rb : (a + 1) * pair] for a in range(blocks)], axis=0),
    )
    lanes = lax.broadcasted_iota(jnp.int32, (pixels, 128), 1).astype(F32)
    one_hot = (own_ids == lanes).astype(F32).astype(BF16)
    counts = wide(counts_ref[...], 256)
    pool_copy.wait()

    @pl.loop(0, wpt.shape[0] // 256)
    def _(n):
        piece = pl.ds(pl.multiple_of(n * 256, 256), 256)
        back = contract_lanes(grad_z, wpt[piece, :]) / counts
        back = jnp.concatenate([back, jnp.zeros((128 - images, 256), F32)], axis=0).astype(BF16)
        value = (acc[:, piece] + jnp.dot(one_hot, back, preferred_element_type=F32)).astype(BF16)
        gx_ref[:, piece] = jnp.dot(back_ref[...], value, preferred_element_type=F32).astype(BF16)

    drain3(18, 10)
    drain4(18, 10)
    results = (
        pltpu.make_async_copy(dw.at[pl.ds(0, 27)], dw_ref, outsem.at[0]),
        pltpu.make_async_copy(dw.at[27], dpoint_ref, outsem.at[1]),
    )
    for result in results:
        result.start()

    pool_cols.leave()
    pool_rows.leave()
    proj_last.arrive()
    for other in range(cols):
        piece_rows = slice(other % 2 * tall_piece, (other % 2 + 1) * tall_piece)
        gproj_ref[piece_rows, other // 2 * wide_piece : (other // 2 + 1) * wide_piece] = final_parts[other].astype(F32)
    proj_cols.leave(quarter)
    proj_rows.leave(lambda other: quarter_sums.at[other])
    proj_last.leave()
    for m in (1, 2, 3):
        pl.when(sends_rim)(rim_copy(m, True).wait_send)
    for m in (1, 2, 3, 0):
        finish_sends(m)

    @pl.loop(0, 28)
    def _(n):
        stage1(n).wait_send()

        @pl.when(last)
        def _():
            stage3(n, x, 0, beside).wait_send()
            stage3(n, x, 1, sibling).wait_send()
            stage3(n, 1 - x, 2, sibling).wait_send()

        @pl.when(jnp.logical_not(last))
        def _():
            stage2(n).wait_send()

    for result in results:
        result.wait()


def backward_call(
    rows, cols, image_count, dz, xsub, ids, wat, wpt, wpl, gain, counts, pooled, pooln, pools, dap, stat, back, proj
):
    _, blocks, rb, width = dz.shape
    channels = wpt.shape[0]
    share = channels // rows
    pair, across, pixels = 2 * rb, cols * blocks, blocks * rb
    images = dap.shape[0]
    group = pair * across
    vmem = pl.BlockSpec(memory_space=pltpu.VMEM)
    hbm = pl.BlockSpec(memory_space=pl.ANY)
    dma = pltpu.SemaphoreType.DMA
    taps = 28

    def ext(high):
        return pltpu.VMEM((across, 2 * high + pair, width), BF16)

    return pl.pallas_call(
        functools.partial(backward_kernel, rows, cols, float(image_count), rb),
        out_shape=(
            jax.ShapeDtypeStruct((pixels, channels), BF16),
            jax.ShapeDtypeStruct((taps - 1, share, width), BF16),
            jax.ShapeDtypeStruct((share, width), BF16),
            jax.ShapeDtypeStruct((share, width), F32),
            jax.ShapeDtypeStruct((8, width), F32),
            jax.ShapeDtypeStruct(proj.shape[1:], F32),
        ),
        in_specs=[vmem, hbm, vmem, hbm, hbm, hbm] + [vmem] * 9,
        out_specs=(vmem, hbm, hbm, vmem, vmem, vmem),
        scratch_shapes=[
            ext(0), ext(HALO[1]), ext(HALO[2]), ext(HALO[3]),
            pltpu.VMEM((3, across, pair, width), BF16),
            pltpu.VMEM((2 * REACH + 1, across, 48, width), BF16),
            pltpu.VMEM((across, ids.shape[0], 128), F32),
            pltpu.VMEM((group, width), BF16),
            pltpu.VMEM((pixels, 3 * width), BF16),
            pltpu.VMEM((share, group), BF16),
            pltpu.VMEM((pixels, channels), F32),
            pltpu.VMEM((2, channels, 3 * width), BF16),
            pltpu.VMEM((channels, width), BF16),
            pltpu.VMEM((taps, share // 2, width), BF16),
            pltpu.VMEM((taps, share // 2, width), BF16),
            pltpu.VMEM((taps, share // 2, width), F32),
            pltpu.VMEM((taps, share // 2, width), BF16),
            pltpu.VMEM((taps, share, width), BF16),
            pltpu.VMEM((cols, images, width), F32),
            pltpu.VMEM((rows, images, width), F32),
            pltpu.VMEM((cols, rows, proj.shape[1] // 2, width // 2), BF16),
            pltpu.VMEM((rows, proj.shape[1] // 2, width // 2), BF16),
            pltpu.VMEM((rows, proj.shape[1] // 2, width // 2), BF16),
            pltpu.VMEM((cols, proj.shape[1] // 2, width // 2), BF16),
            dma((2, 2 * cols, blocks)), dma((2, 3)), dma,
            dma((4,)), dma((4,)),
            dma((4, 2, 8)), dma((4, 2, 2 * cols + 1)),
            dma((taps,)), dma((taps,)),
            dma((taps,)), dma((taps,)),
            dma((3, taps)), dma((2, taps)),
            dma((cols,)), dma((cols,)),
            dma((rows,)), dma((rows,)),
            dma((cols,)), dma((cols,)),
            dma((rows,)), dma((rows,)),
            dma((cols,)), dma((cols,)),
            dma((2,)),
        ],
        compiler_params=pltpu.CompilerParams(
            collective_id=1, has_side_effects=True, vmem_limit_bytes=64 * 2**20
        ),
        cost_estimate=pl.CostEstimate(flops=4 * pixels * channels * width * 28, bytes_accessed=50_000_000, transcendentals=0),
    )(dz, xsub, ids, wat, wpt, wpl, gain, counts, pooled, pooln, pools, dap, stat, back, proj)


def extended(cells, sides, width):
    for axis, dim in sides:
        count = lax.axis_size(axis)
        ends = count - 1
        head = lax.slice_in_dim(cells, 0, width, axis=dim)
        tail = lax.slice_in_dim(cells, cells.shape[dim] - width, cells.shape[dim], axis=dim)
        cells = jnp.concatenate(
            [
                lax.ppermute(tail, axis, [(i, (i + 1) % count) for i in range(ends)]),
                cells,
                lax.ppermute(head, axis, [((i + 1) % count, i) for i in range(ends)]),
            ],
            axis=dim,
        )
    return cells


def image_match(window, own_ids, row_start, col_start):
    rows_here, cols_here = own_ids.shape
    section = window[row_start : row_start + rows_here, col_start : col_start + cols_here]
    return (section == own_ids).astype(jnp.float32).reshape(rows_here * cols_here, 1)


def silu_slope(preact_in):
    sigma = jax.nn.sigmoid(preact_in)
    return sigma * (1.0 + preact_in * (1.0 - sigma))


def transposed(left, right):
    return lax.dot_general(
        left, right, (((1,), (1,)), ((), ())), preferred_element_type=jnp.float32
    )


def shards(
    features, image_ids, w_point, w_atrous, w_pool, w_proj, norm_gain, norm_shift, cotangent
):
    rows_here, cols_here, channels = features.shape
    branch_width = w_point.shape[1]
    pixels = rows_here * cols_here
    grid_rows, grid_cols = image_ids.shape
    total_pixels = float(grid_rows * grid_cols)
    image_count = grid_rows // 16 * (grid_cols // 32)
    dilations = (RATE_LOW, RATE_MID, RATE_TOP)
    margin = RATE_TOP
    row_index = lax.axis_index("rows")
    col_index = lax.axis_index("cols")
    id_padded = jnp.pad(image_ids, margin, constant_values=-1)
    window = lax.dynamic_slice(
        id_padded,
        (row_index * rows_here, col_index * cols_here),
        (rows_here + 2 * margin, cols_here + 2 * margin),
    )
    own_ids = window[margin : margin + rows_here, margin : margin + cols_here]
    own_flat = own_ids.reshape(pixels)
    flattened = features.reshape(pixels, channels)
    padded = extended(features, (("rows", 0), ("cols", 1)), margin)
    one_hot = (own_flat[:, None] == jnp.arange(image_count, dtype=jnp.int32)[None, :]).astype(
        jnp.bfloat16
    )
    local_sums = jnp.einsum("pn,pc->nc", one_hot, flattened, preferred_element_type=jnp.float32)
    counts = jax.ops.segment_sum(
        jnp.ones((grid_rows * grid_cols,), jnp.float32), image_ids.reshape(-1), image_count
    )
    image_totals = lax.psum(local_sums, ("rows", "cols"))
    branch_outs = [jnp.dot(flattened, w_point, preferred_element_type=jnp.float32)]
    for branch, dilation in enumerate(dilations):
        running = jnp.zeros((pixels, branch_width), jnp.float32)
        for stencil in range(9):
            row_shift = (stencil // 3 - 1) * dilation
            col_shift = (stencil % 3 - 1) * dilation
            source = padded[
                margin + row_shift : margin + row_shift + rows_here,
                margin + col_shift : margin + col_shift + cols_here,
            ].reshape(pixels, channels)
            same_image = image_match(window, own_ids, margin + row_shift, margin + col_shift)
            running = running + same_image * jnp.dot(
                source, w_atrous[branch, stencil], preferred_element_type=jnp.float32
            )
        branch_outs.append(running)
    spatial = jnp.stack(branch_outs, axis=1)
    first_sum = jnp.sum(spatial, axis=0)
    second_sum = jnp.sum(spatial * spatial, axis=0)
    first_sum, second_sum = lax.psum((first_sum, second_sum), ("rows", "cols"))
    average = first_sum / total_pixels
    inverse_std = lax.rsqrt(second_sum / total_pixels - average * average + epsilon)
    normed = (spatial - average) * inverse_std
    preact = norm_gain[:4] * normed + norm_shift[:4]
    active = jax.nn.silu(preact).astype(jnp.bfloat16)
    pooled = (image_totals / counts[:, None]).astype(jnp.bfloat16)
    pool_z = jnp.dot(pooled, w_pool, preferred_element_type=jnp.float32)
    pool_avg = jnp.mean(pool_z, axis=0)
    pool_square = jnp.mean(pool_z * pool_z, axis=0)
    pool_inverse = lax.rsqrt(pool_square - pool_avg * pool_avg + epsilon)
    pool_normed = (pool_z - pool_avg) * pool_inverse
    pool_pre = norm_gain[4] * pool_normed + norm_shift[4]
    pool_active = jax.nn.silu(pool_pre).astype(jnp.bfloat16)
    joined = jnp.concatenate(
        [active.reshape(pixels, 4 * branch_width), jnp.take(pool_active, own_flat, axis=0)], axis=1
    )
    final_z = jnp.dot(joined, w_proj, preferred_element_type=jnp.float32)
    final_first, final_second = lax.psum(
        (jnp.sum(final_z, axis=0), jnp.sum(final_z * final_z, axis=0)), ("rows", "cols")
    )
    final_avg = final_first / total_pixels
    final_inverse = lax.rsqrt(final_second / total_pixels - final_avg * final_avg + epsilon)
    final_normed = (final_z - final_avg) * final_inverse
    final_pre = norm_gain[5] * final_normed + norm_shift[5]
    output = jax.nn.silu(final_pre).astype(jnp.bfloat16).reshape(rows_here, cols_here, branch_width)
    upstream = cotangent.reshape(pixels, branch_width).astype(jnp.float32)
    grad_final = upstream * silu_slope(final_pre)
    shift_last, gain_last = lax.psum(
        (jnp.sum(grad_final, axis=0), jnp.sum(grad_final * final_normed, axis=0)), ("rows", "cols")
    )
    grad_final_z = (
        final_inverse
        * (
            grad_final * norm_gain[5]
            - norm_gain[5] * shift_last / total_pixels
            - final_normed * (norm_gain[5] * gain_last / total_pixels)
        )
    ).astype(jnp.bfloat16)
    proj_term = jnp.einsum("pk,pc->kc", joined, grad_final_z, preferred_element_type=jnp.float32)
    grad_joined = transposed(grad_final_z, w_proj)
    grad_pre = grad_joined[:, : 4 * branch_width].reshape(pixels, 4, branch_width) * silu_slope(
        preact
    )
    grad_pixel = grad_joined[:, 4 * branch_width :]
    shift_sums = jnp.sum(grad_pre, axis=0)
    gain_sums = jnp.sum(grad_pre * normed, axis=0)
    image_grads = jax.ops.segment_sum(grad_pixel, own_flat, image_count)
    shift_sums, gain_sums, image_grads = lax.psum(
        (shift_sums, gain_sums, image_grads), ("rows", "cols")
    )
    grad_branch = (
        inverse_std
        * (
            grad_pre * norm_gain[:4]
            - norm_gain[:4] * shift_sums / total_pixels
            - normed * (norm_gain[:4] * gain_sums / total_pixels)
        )
    ).astype(jnp.bfloat16)
    grad_pool_pre = image_grads * silu_slope(pool_pre)
    pool_shift = jnp.sum(grad_pool_pre, axis=0)
    pool_gain = jnp.sum(grad_pool_pre * pool_normed, axis=0)
    grad_pool_z = (
        pool_inverse
        * (
            grad_pool_pre * norm_gain[4]
            - norm_gain[4] * pool_shift / image_count
            - pool_normed * (norm_gain[4] * pool_gain / image_count)
        )
    ).astype(jnp.bfloat16)
    row_share = channels // lax.axis_size("rows")
    pool_columns = lax.dynamic_slice_in_dim(pooled, row_index * row_share, row_share, 1)
    grad_pool = jnp.einsum(
        "nk,nc->kc", pool_columns, grad_pool_z, preferred_element_type=jnp.float32
    )
    grad_pooled = transposed(grad_pool_z, w_pool) / counts[:, None]
    grad_input = jnp.take(grad_pooled, own_flat, axis=0) + transposed(grad_branch[:, 0], w_point)
    point_term = jnp.einsum(
        "pk,pc->kc", flattened, grad_branch[:, 0], preferred_element_type=jnp.float32
    )
    stacked = grad_branch[:, 1:].reshape(rows_here, cols_here, 3 * branch_width)
    grad_padded = extended(stacked, (("rows", 0), ("cols", 1)), margin)
    rim_list = [
        grad_padded[:, :, branch * branch_width : (branch + 1) * branch_width]
        for branch in range(3)
    ]
    rim_bases = [margin, margin, margin]
    atrous_terms = []
    for branch, dilation in enumerate(dilations):
        tap_terms = []
        rim_base = rim_bases[branch]
        for stencil in range(9):
            row_shift = (stencil // 3 - 1) * dilation
            col_shift = (stencil % 3 - 1) * dilation
            source = padded[
                margin + row_shift : margin + row_shift + rows_here,
                margin + col_shift : margin + col_shift + cols_here,
            ].reshape(pixels, channels)
            same_image = image_match(window, own_ids, margin + row_shift, margin + col_shift)
            masked = same_image.astype(jnp.bfloat16) * grad_branch[:, branch + 1]
            tap_terms.append(
                jnp.einsum("pk,pc->kc", source, masked, preferred_element_type=jnp.float32)
            )
            incoming = rim_list[branch][
                rim_base - row_shift : rim_base - row_shift + rows_here,
                rim_base - col_shift : rim_base - col_shift + cols_here,
            ].reshape(pixels, branch_width)
            back_image = image_match(window, own_ids, margin - row_shift, margin - col_shift)
            grad_input = grad_input + back_image * transposed(incoming, w_atrous[branch, stencil])
        atrous_terms.append(jnp.stack(tap_terms))
    atrous_term = jnp.stack(atrous_terms)
    shared = (
        lax.psum_scatter(
            point_term.astype(jnp.bfloat16), "rows", scatter_dimension=0, tiled=True
        ).astype(jnp.float32),
        lax.psum_scatter(
            atrous_term.astype(jnp.bfloat16), "rows", scatter_dimension=2, tiled=True
        ).astype(jnp.float32),
        lax.psum_scatter(
            proj_term.astype(jnp.bfloat16), "rows", scatter_dimension=0, tiled=True
        ).astype(jnp.float32),
    )
    shared = (
        lax.psum(shared[0].astype(jnp.bfloat16), "cols").astype(jnp.float32),
        lax.psum(shared[1].astype(jnp.bfloat16), "cols").astype(jnp.float32),
        lax.psum(shared[2].astype(jnp.bfloat16), "cols").astype(jnp.float32),
    )
    grad_gain = jnp.concatenate([gain_sums, pool_gain[None], gain_last[None]], axis=0)
    grad_shift = jnp.concatenate([shift_sums, pool_shift[None], shift_last[None]], axis=0)
    grad_features = grad_input.astype(jnp.bfloat16).reshape(rows_here, cols_here, channels)
    return (
        output,
        grad_features,
        shared[0],
        shared[1],
        grad_pool,
        shared[2],
        grad_gain,
        grad_shift,
    )


def block_order(height, breadth):
    pixel = np.arange(height * breadth).reshape(height, breadth // STEP, STEP).transpose(1, 0, 2).reshape(-1)
    return np.eye(height * breadth, dtype=np.float32)[pixel]


def id_columns(ids):
    height, breadth = ids.shape
    table = ids.reshape(height, breadth // STEP, STEP).transpose(0, 2, 1).reshape(height * STEP, breadth // STEP)
    return jnp.pad(table.astype(F32), ((0, 0), (0, 128 - breadth // STEP)))


def quick_shards(
    features, image_ids, w_point, w_atrous, w_pool, w_proj, norm_gain, norm_shift, cotangent
):
    rows_here, cols_here, channels = features.shape
    branch_width = w_point.shape[1]
    pixels = rows_here * cols_here
    grid_rows, grid_cols = image_ids.shape
    image_count = grid_rows // 16 * (grid_cols // 32)
    images = -(-image_count // 16) * 16
    margin = RATE_TOP
    rows, cols = lax.axis_size("rows"), lax.axis_size("cols")
    row_index = lax.axis_index("rows")
    col_index = lax.axis_index("cols")
    id_padded = jnp.pad(image_ids, margin, constant_values=-1)
    window = lax.dynamic_slice(
        id_padded,
        (row_index * rows_here, col_index * cols_here),
        (rows_here + 2 * margin, cols_here + 2 * margin),
    )
    own_ids = window[margin : margin + rows_here, margin : margin + cols_here]
    own_flat = own_ids.reshape(pixels)
    counts = jnp.sum(
        (image_ids.reshape(-1, 1) == jnp.arange(images, dtype=jnp.int32)[None, :]).astype(F32), axis=0
    )
    counts = jnp.maximum(counts, 1.0)
    count_table = jnp.broadcast_to(counts[:, None], (images, 128))
    order = block_order(rows_here, cols_here)
    order, back = jnp.asarray(order, BF16), jnp.asarray(order.T, BF16)
    output, dz, proj_term, stats, pooled, pool_normed, pool_slope, dap, xsub = forward_call(
        rows, cols, image_count, features.reshape(pixels, channels), order, back, id_columns(window), w_atrous, w_point, w_pool, w_proj,
        norm_gain, norm_shift, cotangent.reshape(pixels, branch_width), count_table,
    )
    output = output.reshape(rows_here, cols_here, branch_width)
    pair_window = lax.dynamic_slice(
        id_padded,
        (row_index // 2 * (2 * rows_here), jnp.int32(margin)),
        (2 * rows_here + 2 * margin, grid_cols),
    )
    grad_input, atrous, point, grad_pool, pool_sums, grad_proj = backward_call(
        rows, cols, image_count, dz, xsub.reshape(2, 8, 4, pixels // 4, -1), id_columns(pair_window), w_atrous, w_point, w_pool,
        norm_gain, count_table, pooled, pool_normed, pool_slope, dap, stats, back, proj_term.reshape(rows, -1, branch_width),
    )
    grad_atrous = atrous.astype(F32).reshape(3, 9, channels // rows, branch_width)

    grad_gain = jnp.concatenate([stats[4:8], pool_sums[1:2], stats[9:10]], axis=0)
    grad_shift = jnp.concatenate([stats[0:4], pool_sums[0:1], stats[8:9]], axis=0)
    grad_features = grad_input.reshape(rows_here, cols_here, channels)
    return (
        output, grad_features, point.astype(F32), grad_atrous, grad_pool,
        grad_proj, grad_gain, grad_shift,
    )


def solution(mesh):
    placed = (P("rows", "cols", None), P(), P(), P(), P(), P(), P(), P(), P("rows", "cols", None))
    quick = mesh.shape["rows"] == 8 and mesh.shape["cols"] == 4
    return jax.shard_map(
        quick_shards if quick else shards,
        mesh=mesh,
        in_specs=placed,
        out_specs=(
            P("rows", "cols", None),
            P("rows", "cols", None),
            P("rows", None),
            P(None, None, "rows", None),
            P("rows", None),
            P("rows", None),
            P(),
            P(),
        ),
        check_vma=False,
    )
```
